32 devices in a mesh: groups: 2 (over y), gx: 4 (over z), gy: 2 (over x), gz: 2 (over core).
Axes of the slice: x: 2, y: 2, z: 4, core: 2. Of those that a mesh axis runs over, the one named last changes fastest.
Arguments:
- fields: float32 [5, 64, 128, 256], P(None, 'gz', ('groups', 'gx'), 'gy'), parts along dimension 2, may hold values from -6 to 6
- parent_wind: float32 [3, 128], P(None, ('groups', 'gz')), parts along dimension 1, may hold values from -1 to 1
- diffusivity: float32 [5], replicated, may hold values from 0.05 to 0.3
- wall_type: int32 [128, 256], P(('groups', 'gx'), 'gy'), parts along dimension 0, may hold values from 0 to 3
- building_count: int32 [128], P(('groups', 'gx')), parts along dimension 0, may hold values from 0 to 32, as said below
- slot_of: int32 [128], P('groups'), parts along dimension 0, may hold values from -1 to 31, as said below
- parent_of: int32 [128], P('groups'), parts along dimension 0, may hold values from 0 to 7, as said below
Outputs:
- new_fields: float32 [5, 64, 128, 256], P(None, 'gz', ('groups', 'gx'), 'gy'), parts along dimension 2
- wall_stress: float32 [64, 64, 256], P('gz', ('groups', 'gx'), 'gy'), parts along dimension 1
- parent_mean: float32 [16, 5, 8, 32], P(('groups', 'gx'), None, 'gz', 'gy'), parts along dimension 0
The draws below stay inside these ranges and needn't reach their ends.
There are 2 independent parts, one for each index of `groups`. The reference program is written for one: setup_inputs(seed, part) draws one part's arguments, and reference() takes and returns one part's arrays. A program takes and returns all parts, laid end to end along the dimension named above; an argument that names none is the same for every part. Nothing has to cross between parts.
Inputs may be any that keep to these rules, and one draw needn't show every extreme that they name: `slot_of`: exactly 32 tiles have a slot; every value 0 to 31 names exactly one tile, so each block of 8 slots (one device's) is full. Of the tiles of one block of 16 tiles (one device's), at most 4 have slots of the same block of 8, and some block reaches 4. `building_count`: positive exactly where slot_of is not -1. Parent column p begins at tile p * 8 - o[p], with o[0] = 0 and each other o[p] one of 0 to 7; parent_of[x] is the last column that begins at or before x. So it is non-decreasing, every parent column gets at least one tile, and a tile's parent column belongs to its own block of 2 parent columns or is the first of the next block.
All inputs are finite; a program needn't handle non-finite values.
Results may differ from the reference program's by a relative error of at most 0.00011.
Values sent between devices are 32-bit elements; how exact they have to be, the bound alone decides.
No kernel may reach another device: no remote copies, remote signals or barrier semaphores. Data moves between devices by JAX's collectives and lax.ppermute only.
A program may use at most 64 MiB of HBM per device.

```python
import math
import jax
import jax.numpy as jnp
from jax import lax

FIELDS = 5
CX = 16
RATIO = 8
BMAX = 32
SLOTS = 8
SLOTS_ALL = 32
NX = 64
NY = 256
NZ = 64


def built_tiles(key):
    device_count = NX // CX
    key_base, key_heavy, key_noise = jax.random.split(key, 3)
    device_base = jax.random.randint(key_base, (device_count,), 0, 4) * 64
    heavy_device = jax.random.randint(key_heavy, (), 0, device_count)
    device_base = jnp.where(jnp.arange(device_count) == heavy_device, 100000, device_base)
    scores = (jnp.repeat(device_base, CX) + jax.random.randint(key_noise, (NX,), 0, 64)) * NX + jnp.arange(NX)
    chosen = lax.top_k(scores, SLOTS * device_count)[1]
    is_built = jnp.zeros((NX,), jnp.int32).at[chosen].set(1)
    return (is_built, heavy_device)


def draw_slot_of(key, part):
    is_built, heavy_device = built_tiles(key)
    device_count = NX // CX
    tile_rank = jnp.cumsum(is_built) - 1
    slots = tile_rank % device_count * SLOTS + tile_rank // device_count
    return jnp.where(is_built == 1, slots, -1).astype(jnp.int32)


def draw_building_count(key, part):
    is_built, heavy_device = built_tiles(key)
    key = jax.random.fold_in(key, 12)
    counts = jax.random.randint(key, (NX,), 1, BMAX + 1)
    counts = jnp.where(jnp.arange(NX) == heavy_device * CX, BMAX, counts)
    return jnp.where(is_built == 1, counts, 0).astype(jnp.int32)


def draw_parent_of(key, part):
    key = jax.random.fold_in(key, 13)
    parent_count = NX // RATIO
    offsets = jax.random.randint(key, (parent_count,), 0, RATIO)
    offsets = jnp.where(jnp.arange(parent_count) == 0, 0, offsets)
    starts = jnp.arange(parent_count, dtype=jnp.int32) * RATIO - offsets
    begun = (starts[None, :] <= jnp.arange(NX, dtype=jnp.int32)[:, None]).astype(jnp.int32)
    return (jnp.sum(begun, axis=1) - 1).astype(jnp.int32)


def set_ends(entries, key, least, top_value):
    longest = entries.shape.index(max(entries.shape))
    spots = []
    for shift in (0, 1):
        where = [jax.random.randint(jax.random.fold_in(key, axis), (), 0, length) for axis, length in enumerate(entries.shape)]
        where[longest] = (where[longest] + shift) % entries.shape[longest]
        spots.append(tuple(where))
    return entries.at[spots[0]].set(least).at[spots[1]].set(top_value)


def level_of(key, dims, shards, low, high):
    factor_of = 1.0
    for dim, blocks in shards:
        steps = jax.random.uniform(jax.random.fold_in(jax.random.fold_in(key, 6), dim), (blocks,), jnp.float32, low / len(shards), high / len(shards))
        factor_of = factor_of * jnp.repeat(jnp.exp(steps), dims[dim] // blocks).reshape((-1,) + (1,) * (len(dims) - 1 - dim))
    return factor_of


def scatter_about(stream_key, extent, spread, bound, pieces=(), held_as=jnp.bfloat16):
    array = spread * jax.random.normal(stream_key, extent, jnp.float32)
    if pieces:
        array = array * level_of(stream_key, extent, pieces, -0.22, 0.18)
    return jnp.clip(array, -bound, bound).astype(held_as)


def setup_inputs(seed: int = 0, part: int = 0) -> dict:
    splits = jax.random.split(jax.random.key(seed), 8)
    own_keys = jax.random.split(jax.random.fold_in(splits[7], part), 8)
    fields = scatter_about(own_keys[0], (FIELDS, NZ, NX, NY), 1.0, 6.0, ((1, 2), (2, 4), (3, 2)), jnp.float32)
    parent_wind = jnp.clip(jax.random.uniform(own_keys[1], (3, NZ), jnp.float32, -1.0, 1.0) * level_of(own_keys[1], (3, NZ), ((1, 2),), -0.4, 0.0), -1.0, 1.0)
    diffusivity = jnp.clip(jnp.exp(jax.random.uniform(splits[2], (FIELDS,), jnp.float32, math.log(0.05), math.log(0.3))), 0.05, 0.3)
    wall_type = set_ends(jax.random.randint(own_keys[3], (NX, NY), 0, 4), jax.random.fold_in(own_keys[3], 1), 0, 3).astype(jnp.int32)
    building_count = draw_building_count(jax.random.fold_in(jax.random.fold_in(splits[7], part), 71), part)
    slot_of = draw_slot_of(jax.random.fold_in(jax.random.fold_in(splits[7], part), 71), part)
    parent_of = draw_parent_of(jax.random.fold_in(jax.random.fold_in(splits[7], part), 71), part)
    return dict(fields=fields, parent_wind=parent_wind, diffusivity=diffusivity, wall_type=wall_type, building_count=building_count, slot_of=slot_of, parent_of=parent_of)


TABLE = (0.4, 0.8, 1.3, 2.0)
STEP = 0.25

def lookup(wall_type):
    result = jnp.zeros(wall_type.shape, jnp.float32)
    for wall_code, wall_value in enumerate(TABLE):
        result = result + jnp.where(wall_type == wall_code, wall_value, 0.0)
    return result

def tendency(fields, padded, parent_wind, diffusivity):
    diff_x = padded[:, 1:-1, 2:, 1:-1] - padded[:, 1:-1, :-2, 1:-1]
    diff_y = padded[:, 1:-1, 1:-1, 2:] - padded[:, 1:-1, 1:-1, :-2]
    diff_z = padded[:, 2:, 1:-1, 1:-1] - padded[:, :-2, 1:-1, 1:-1]
    beside = padded[:, 1:-1, 2:, 1:-1] + padded[:, 1:-1, :-2, 1:-1]
    beside = beside + padded[:, 1:-1, 1:-1, 2:] + padded[:, 1:-1, 1:-1, :-2]
    beside = beside + padded[:, 2:, 1:-1, 1:-1] + padded[:, :-2, 1:-1, 1:-1]
    advect = 0.5 * (parent_wind[0][None, :, None, None] * diff_x + parent_wind[1][None, :, None, None] * diff_y + parent_wind[2][None, :, None, None] * diff_z)
    return -advect + diffusivity[:, None, None, None] * (beside - 6.0 * fields)

def reference(fields, parent_wind, diffusivity, wall_type, building_count, slot_of, parent_of):
    strength = jnp.where(slot_of >= 0, building_count.astype(jnp.float32) / BMAX, 0.0)
    wall_coef = lookup(wall_type) * strength[:, None]
    factor = jnp.zeros(fields.shape[1:], jnp.float32)
    for step_number in range(2):
        padded = jnp.pad(fields, ((0, 0), (1, 1), (1, 1), (1, 1)))
        change = tendency(fields, padded, parent_wind, diffusivity)
        factor = wall_coef[None] * jnp.sqrt(fields[0] * fields[0] + fields[1] * fields[1] + fields[2] * fields[2] + 1.0)
        wall_part = -(factor[None] * fields[:3])
        fields = fields + STEP * jnp.concatenate([change[:3] + wall_part, change[3:]], axis=0)
    slot_pick = (slot_of[:, None] == jnp.arange(SLOTS_ALL, dtype=jnp.int32)[None, :]).astype(jnp.float32)
    wall_stress = jnp.einsum('zxy,xs->zsy', factor, slot_pick, precision=lax.Precision.HIGHEST)
    coarse = fields.reshape(FIELDS, NZ // RATIO, RATIO, NX, NY // RATIO, RATIO).sum(axis=(2, 5))
    owner_pick = (parent_of[:, None] == jnp.arange(NX // RATIO, dtype=jnp.int32)[None, :]).astype(jnp.float32)
    parent_sums = jnp.einsum('fzxy,xp->pfzy', coarse, owner_pick, precision=lax.Precision.HIGHEST)
    tile_tally = lax.optimization_barrier(jnp.sum(owner_pick, axis=0))
    parent_mean = parent_sums / (tile_tally[:, None, None, None] * (RATIO * RATIO))
    return (fields, wall_stress, parent_mean)
```

```python
import functools

import jax
import jax.numpy as jnp
from jax import lax
from jax.experimental import pallas as pl
from jax.experimental.pallas import tpu as pltpu
from jax.sharding import PartitionSpec as P

FIELDS = 5
RATIO = 8
BMAX = 32
SLOTS = 8

TABLE = (0.4, 0.8, 1.3, 2.0)
STEP = 0.25

FRONT = 8
LANES = 128
F32 = jnp.float32

VM = pl.BlockSpec(memory_space=pltpu.VMEM)
SM = pl.BlockSpec(memory_space=pltpu.SMEM)


def in_vmem(array):
    return pltpu.with_memory_space_constraint(array, pltpu.VMEM)


class Dims:
    def __init__(self, levels, tiles, columns, all_tiles, n_gx, n_gy):
        self.levels, self.tiles, self.columns = levels, tiles, columns
        self.all_tiles, self.n_gx, self.n_gy = all_tiles, n_gx, n_gy
        self.block = FRONT + tiles
        self.pad_rows = FIELDS * (levels + 2) * self.block + 8
        self.capacity = (tiles + n_gx - 1) // n_gx
        self.per_group = LANES // (2 * levels)
        self.groups = -(-FIELDS // self.per_group)
        self.parents = tiles // RATIO
        self.y_sends = 1 if n_gy == 2 else 2


def base_row(d, f, z):
    return (f * (d.levels + 2) + z + 1) * d.block


def lane_of(d, f, z):
    return 2 * ((f % d.per_group) * d.levels + z)


def y_choices(d):
    if d.n_gy == 2:
        first = lax.axis_index("gy") == 0
        return [(jnp.where(first, d.columns - 1, 0), jnp.where(first, 1, 0))]
    return [(d.columns - 1, 1), (0, 0)]


def x_choices(d):
    even = lax.rem(lax.axis_index("gx"), 2) == 0
    return [jnp.where(even, d.tiles - 1, 0), jnp.where(even, 0, d.tiles - 1)]


def gather_y(d, accs, f, z, cells, lane):
    g = f // d.per_group
    for i, (column, side) in enumerate(y_choices(d)):
        place = lane_of(d, f, z) + side
        moved = pltpu.roll(cells, lax.rem(place - column + 2 * LANES, LANES), 1)
        accs[i][g] = jnp.where(lane == place, moved, accs[i][g])
    return accs


def pack_kernel(d, fields, pad, xa, xb, zface, *yq):
    lane = lax.broadcasted_iota(jnp.int32, (d.tiles, LANES), 1)
    zeros = jnp.zeros((d.tiles, LANES), F32)
    rows = d.levels * d.tiles

    def level(z, accs):
        accs = [list(a) for a in accs]
        for f in range(FIELDS):
            cells = fields[pl.ds(pl.multiple_of(f * rows + z * d.tiles, 8), d.tiles), :]
            pad[pl.ds(pl.multiple_of(base_row(d, f, z) + FRONT, 8), d.tiles), :] = cells
            accs = gather_y(d, accs, f, z, cells, lane)
        return tuple(tuple(a) for a in accs)

    accs = lax.fori_loop(
        0, d.levels, level, tuple(tuple(zeros for _ in range(d.groups)) for _ in range(d.y_sends)), unroll=2
    )
    for i in range(d.y_sends):
        for g in range(d.groups):
            yq[i][:, g * LANES : (g + 1) * LANES] = accs[i][g]
    for out, tile in zip((xa, xb), x_choices(d)):
        for f in range(FIELDS):
            out[f * d.levels : (f + 1) * d.levels, :] = pad[
                pl.ds(base_row(d, f, 0) + FRONT + tile, d.levels, stride=d.block), :
            ]
    z_out = jnp.where(lax.axis_index("gz") == 0, d.levels - 1, 0)
    for f in range(FIELDS):
        zface[f * d.tiles : (f + 1) * d.tiles, :] = fields[
            pl.ds(pl.multiple_of(f * rows + z_out * d.tiles, 8), d.tiles), :
        ]


def set_halos(d, pad, xa, xb, zface):
    me = lax.axis_index("gx")
    even = lax.rem(me, 2) == 0
    zero_x = jnp.zeros((d.levels, LANES), F32)
    for f in range(FIELDS):
        a = xa[f * d.levels : (f + 1) * d.levels, :]
        b = xb[f * d.levels : (f + 1) * d.levels, :]
        left = jnp.where(me == 0, zero_x, jnp.where(even, b, a))
        right = jnp.where(me == d.n_gx - 1, zero_x, jnp.where(even, a, b))
        pad[pl.ds(base_row(d, f, 0) + FRONT - 1, d.levels, stride=d.block), :] = left
        pad[pl.ds(base_row(d, f, 0) + d.block, d.levels, stride=d.block), :] = right
    low = lax.axis_index("gz") == 0
    zero_z = jnp.zeros((d.tiles, LANES), F32)
    for f in range(FIELDS):
        face = zface[f * d.tiles : (f + 1) * d.tiles, :]
        pad[pl.ds(base_row(d, f, -1) + FRONT, d.tiles), :] = jnp.where(low, zero_z, face)
        pad[pl.ds(base_row(d, f, d.levels) + FRONT, d.tiles), :] = jnp.where(low, face, zero_z)


def stencil(d, pad, yq, wind, diff, f, z, lane):
    base = base_row(d, f, z)
    v = pad[pl.ds(pl.multiple_of(base + FRONT, 8), d.tiles), :]
    xm = pad[pl.ds(base + FRONT - 1, d.tiles), :]
    xp = pad[pl.ds(base + FRONT + 1, d.tiles), :]
    zm = pad[pl.ds(pl.multiple_of(base + FRONT - d.block, 8), d.tiles), :]
    zp = pad[pl.ds(pl.multiple_of(base + FRONT + d.block, 8), d.tiles), :]
    g = f // d.per_group
    halo = yq[0][:, g * LANES : (g + 1) * LANES]
    if d.y_sends == 2:
        halo = halo + yq[1][:, g * LANES : (g + 1) * LANES]
    halo = pltpu.roll(halo, LANES - 1 - lane_of(d, f, z), 1)
    yp = jnp.where(lane == d.columns - 1, halo, pltpu.roll(v, LANES - 1, 1))
    ym = jnp.where(lane == 0, halo, pltpu.roll(v, 1, 1))
    spread = STEP * diff[f]
    wx = (0.5 * STEP) * wind[0, z]
    wy = (0.5 * STEP) * wind[1, z]
    wz = (0.5 * STEP) * wind[2, z]
    new = (1.0 - 6.0 * spread) * v
    new = new + ((spread - wx) * xp + (spread + wx) * xm)
    new = new + ((spread - wy) * yp + (spread + wy) * ym)
    new = new + ((spread - wz) * zp + (spread + wz) * zm)
    return v, new


def speed(u, v, w):
    return jnp.sqrt(u * u + v * v + w * w + 1.0)


def wall_coefficients(d, wall_type, count, slot_of):
    first_tile = lax.axis_index("gx") * d.tiles
    row = lax.broadcasted_iota(jnp.int32, (d.tiles, LANES), 0)
    strength = jnp.zeros((d.tiles, LANES), F32)
    for x in range(d.tiles):
        held = jnp.where(slot_of[first_tile + x] >= 0, count[x], 0).astype(F32) * (1.0 / BMAX)
        strength = jnp.where(row == x, held, strength)
    kind = wall_type[...]
    value = jnp.zeros((d.tiles, LANES), F32)
    for code, entry in enumerate(TABLE):
        value = jnp.where(kind == code, entry, value)
    return value * strength


def step_one_kernel(d, pad_in, xa, xb, zface, *refs):
    yq = refs[: d.y_sends]
    wall_type, wind, diff, count, slot_of = refs[d.y_sends : d.y_sends + 5]
    outs = refs[d.y_sends + 5 :]
    pad, new_pad, factor, xa_out, xb_out, z_out = outs[:6]
    yq_out = outs[6 : 6 + d.y_sends]
    stress = outs[6 + d.y_sends : 6 + d.y_sends + d.n_gx]
    table, tally = outs[6 + d.y_sends + d.n_gx :]
    set_halos(d, pad, xa, xb, zface)
    lane = lax.broadcasted_iota(jnp.int32, (d.tiles, LANES), 1)
    zeros = jnp.zeros((d.tiles, LANES), F32)
    coef = wall_coefficients(d, wall_type, count, slot_of)

    def level(z, accs):
        accs = [list(a) for a in accs]
        both = [stencil(d, pad, yq, wind, diff, f, z, lane) for f in range(FIELDS)]
        drag = STEP * (coef * speed(*(both[f][0] for f in range(3))))
        news = [both[f][1] - drag * both[f][0] if f < 3 else both[f][1] for f in range(FIELDS)]
        for f in range(FIELDS):
            new_pad[pl.ds(pl.multiple_of(base_row(d, f, z) + FRONT, 8), d.tiles), :] = news[f]
            accs = gather_y(d, accs, f, z, news[f], lane)
        factor[pl.ds(pl.multiple_of(z * d.tiles, 8), d.tiles), :] = coef * speed(*news[:3])
        return tuple(tuple(a) for a in accs)

    accs = lax.fori_loop(
        0, d.levels, level, tuple(tuple(zeros for _ in range(d.groups)) for _ in range(d.y_sends)), unroll=2
    )
    for i in range(d.y_sends):
        for g in range(d.groups):
            yq_out[i][:, g * LANES : (g + 1) * LANES] = accs[i][g]
    for out, tile in zip((xa_out, xb_out), x_choices(d)):
        for f in range(FIELDS):
            out[f * d.levels : (f + 1) * d.levels, :] = new_pad[
                pl.ds(base_row(d, f, 0) + FRONT + tile, d.levels, stride=d.block), :
            ]
    z_level = jnp.where(lax.axis_index("gz") == 0, d.levels - 1, 0)
    for f in range(FIELDS):
        z_out[f * d.tiles : (f + 1) * d.tiles, :] = new_pad[
            pl.ds(pl.multiple_of(base_row(d, f, z_level) + FRONT, 8), d.tiles), :
        ]
    me = lax.axis_index("gx")
    for k in range(d.n_gx):
        tally[k] = 0
    for i in range(d.n_gx * d.capacity):
        table[i] = 0
    for x in range(d.tiles):
        slot = slot_of[me * d.tiles + x]

        @pl.when(slot >= 0)
        def _():
            away = lax.rem(lax.shift_right_logical(slot, 3) - me + d.n_gx, d.n_gx)
            rank = tally[away]
            table[away * d.capacity + rank] = x
            tally[away] = rank + 1

    for k in range(d.n_gx):
        for c in range(d.capacity):
            tile = table[k * d.capacity + c]
            stress[k][c * d.levels : (c + 1) * d.levels, :] = factor[pl.ds(tile, d.levels, stride=d.tiles), :]


def step_two_kernel(d, pad_in, factor, xa, xb, zface, *refs):
    yq = refs[: d.y_sends]
    wind, diff, parent_of = refs[d.y_sends : d.y_sends + 3]
    pad, new_fields, own_sums, sent_sums, coarse = refs[d.y_sends + 3 :]
    set_halos(d, pad, xa, xb, zface)
    lane = lax.broadcasted_iota(jnp.int32, (d.tiles, LANES), 1)
    row = lax.broadcasted_iota(jnp.int32, (d.tiles, LANES), 0)
    zeros = jnp.zeros((d.tiles, LANES), F32)
    me = lax.axis_index("gx")
    held = jnp.full((d.tiles, LANES), -1, jnp.int32)
    for x in range(d.tiles):
        held = jnp.where(row == x, parent_of[me * d.tiles + x] - me * d.parents, held)
    masks = [jnp.where(held == p, 1.0, 0.0) for p in range(d.parents + 1)]
    coarse_levels = d.levels // RATIO
    coarse[...] = jnp.zeros_like(coarse)
    rows = d.levels * d.tiles
    per_parent = own_sums.shape[0] // d.parents

    def coarse_level(k, carry):
        def level(i, sums):
            z = k * RATIO + i
            drag = STEP * factor[pl.ds(pl.multiple_of(z * d.tiles, 8), d.tiles), :]
            added = []
            for f in range(FIELDS):
                v, new = stencil(d, pad, yq, wind, diff, f, z, lane)
                if f < 3:
                    new = new - drag * v
                new_fields[pl.ds(pl.multiple_of(f * rows + z * d.tiles, 8), d.tiles), :] = new
                added.append(sums[f] + new)
            return tuple(added)

        sums = lax.fori_loop(0, RATIO, level, (zeros,) * FIELDS, unroll=2)
        for p in range(d.parents + 1):
            for f in range(FIELDS):
                line = jnp.sum(sums[f] * masks[p], axis=0, keepdims=True)
                coarse[pl.ds(p * per_parent + f * coarse_levels + k, 1), :] = line
        return carry

    lax.fori_loop(0, coarse_levels, coarse_level, 0)
    pick_row = lax.broadcasted_iota(jnp.int32, (LANES, LANES), 0)
    pick_lane = lax.broadcasted_iota(jnp.int32, (LANES, LANES), 1)
    pick = jnp.where(pick_row // RATIO == pick_lane, 1.0, 0.0)
    summed = jnp.dot(coarse[...], pick, precision=lax.Precision.HIGHEST, preferred_element_type=F32)
    own_sums[...] = summed[: d.parents * per_parent, :]
    sent_sums[...] = summed[d.parents * per_parent :, :]


def place_kernel(d, own_sums, got_sums, slot_of, parent_of, *refs):
    stress = refs[: d.n_gx]
    wall_stress, parent_mean, gathered, table = refs[d.n_gx :]
    me = lax.axis_index("gx")
    part = d.capacity * d.levels
    for k in range(d.n_gx):
        gathered[k * part : (k + 1) * part, :] = stress[k][...]

    def source(s, carry):
        away = lax.rem(me - s + d.n_gx, d.n_gx)

        def tile(x, rank):
            slot = slot_of[s * d.tiles + x]
            mine = (slot >= 0) & (lax.shift_right_logical(slot, 3) == me)
            place = jnp.where(mine, slot - me * SLOTS, SLOTS)
            table[place] = away * d.capacity + rank
            return rank + mine.astype(jnp.int32)

        lax.fori_loop(0, d.tiles, tile, 0, unroll=True)
        return carry

    lax.fori_loop(0, d.n_gx, source, 0)
    for s in range(SLOTS):
        start = pl.multiple_of(table[s] * d.levels, 8)
        wall_stress[pl.ds(s, d.levels, stride=SLOTS), :] = gathered[pl.ds(start, d.levels), :]
    before = jnp.maximum(me - 1, 0) * d.tiles
    per_parent = own_sums.shape[0] // d.parents
    coarse_levels = d.levels // RATIO
    cells = d.columns // RATIO
    for p in range(d.parents):
        count = jnp.int32(0)
        for x in range(d.tiles):
            count = count + (parent_of[me * d.tiles + x] == me * d.parents + p).astype(jnp.int32)
            if p == 0:
                earlier = parent_of[before + x] == me * d.parents + p
                count = count + ((me > 0) & earlier).astype(jnp.int32)
        total = own_sums[p * per_parent : (p + 1) * per_parent, :]
        if p == 0:
            total = jnp.where(me == 0, total, total + got_sums[...])
        mean = total / (jnp.full(total.shape, count, jnp.int32).astype(F32) * (RATIO * RATIO))
        for f in range(FIELDS):
            parent_mean[p, f] = mean[f * coarse_levels : (f + 1) * coarse_levels, :cells]


def swapped(block, axis):
    return lax.ppermute(block, axis, [(i, i ^ 1) for i in range(lax.axis_size(axis))])


def swapped_between(block, axis):
    n = lax.axis_size(axis)
    other = lambda i: (i + 1) % n if i % 2 else (i - 1) % n
    return lax.ppermute(block, axis, [(i, other(i)) for i in range(n)])


def rotated(block, axis, distance):
    n = lax.axis_size(axis)
    return lax.ppermute(block, axis, [(i, (i + distance) % n) for i in range(n)])


def faces_swapped(d, xa, xb, zface, yq):
    xa = swapped(xa, "gx")
    xb = swapped_between(xb, "gx")
    if d.y_sends == 1:
        yq = [swapped(yq[0], "gy")]
    else:
        n = d.n_gy
        yq = [
            lax.ppermute(yq[0], "gy", [(i, i + 1) for i in range(n - 1)]),
            lax.ppermute(yq[1], "gy", [(i + 1, i) for i in range(n - 1)]),
        ]
    zface = swapped(zface, "gz")
    return [in_vmem(a) for a in (xa, xb, zface, *yq)]


def body(fields, parent_wind, diffusivity, wall_type, building_count, slot_of, parent_of):
    _, levels, tiles, columns = fields.shape
    d = Dims(levels, tiles, columns, slot_of.shape[0], lax.axis_size("gx"), lax.axis_size("gy"))
    assert columns == LANES and lax.axis_size("gz") == 2 and d.n_gx % 2 == 0
    params = pltpu.CompilerParams(vmem_limit_bytes=24 << 20)
    rows = FIELDS * levels * tiles
    pad_t = pltpu.VMEM((d.pad_rows, LANES), F32)
    x_t = pltpu.VMEM((FIELDS * levels, LANES), F32)
    z_t = pltpu.VMEM((FIELDS * tiles, LANES), F32)
    y_ts = [pltpu.VMEM((tiles, d.groups * LANES), F32)] * d.y_sends
    stress_t = pltpu.VMEM((d.capacity * levels, LANES), F32)

    pad, xa, xb, zface, *yq = pl.pallas_call(
        functools.partial(pack_kernel, d),
        out_shape=[pad_t, x_t, x_t, z_t, *y_ts],
        in_specs=[VM],
        out_specs=[VM] * (4 + d.y_sends),
        compiler_params=params,
        name="pack",
    )(fields.reshape(rows, LANES))
    faces = faces_swapped(d, xa, xb, zface, yq)

    n_out = 6 + d.y_sends + d.n_gx
    _, new_pad, factor, xa, xb, zface, *rest = pl.pallas_call(
        functools.partial(step_one_kernel, d),
        out_shape=[pad_t, pad_t, pltpu.VMEM(((levels + 1) * tiles, LANES), F32), x_t, x_t, z_t, *y_ts]
        + [stress_t] * d.n_gx,
        in_specs=[VM] * (5 + d.y_sends) + [SM] * 4,
        out_specs=[VM] * n_out,
        scratch_shapes=[pltpu.SMEM((d.n_gx * d.capacity,), jnp.int32), pltpu.SMEM((d.n_gx,), jnp.int32)],
        input_output_aliases={0: 0},
        compiler_params=params,
        name="step_one",
    )(in_vmem(pad), *faces, wall_type, parent_wind, diffusivity, building_count, slot_of)
    yq, stress = rest[: d.y_sends], rest[d.y_sends :]
    faces = faces_swapped(d, xa, xb, zface, yq)
    stress = [stress[0]] + [rotated(stress[k], "gx", k) for k in range(1, d.n_gx)]

    per_parent = -(-FIELDS * (levels // RATIO) // 8) * 8
    _, new_fields, own_sums, sent_sums = pl.pallas_call(
        functools.partial(step_two_kernel, d),
        out_shape=[
            pad_t,
            jax.ShapeDtypeStruct((rows, LANES), F32),
            pltpu.VMEM((d.parents * per_parent, LANES), F32),
            pltpu.VMEM((per_parent, LANES), F32),
        ],
        in_specs=[VM] * (5 + d.y_sends) + [SM] * 3,
        out_specs=[VM] * 4,
        scratch_shapes=[pltpu.VMEM(((d.parents + 1) * per_parent, LANES), F32)],
        input_output_aliases={0: 0},
        compiler_params=params,
        name="step_two",
    )(in_vmem(new_pad), in_vmem(factor), *faces, parent_wind, diffusivity, parent_of)
    got_sums = rotated(sent_sums, "gx", 1)

    wall_stress, parent_mean = pl.pallas_call(
        functools.partial(place_kernel, d),
        out_shape=[
            jax.ShapeDtypeStruct((levels * SLOTS, LANES), F32),
            jax.ShapeDtypeStruct((d.parents, FIELDS, levels // RATIO, columns // RATIO), F32),
        ],
        in_specs=[VM, VM, SM, SM] + [VM] * d.n_gx,
        out_specs=[VM, VM],
        scratch_shapes=[
            pltpu.VMEM((d.n_gx * d.capacity * levels, LANES), F32),
            pltpu.SMEM((SLOTS + 1,), jnp.int32),
        ],
        compiler_params=params,
        name="place",
    )(in_vmem(own_sums), in_vmem(got_sums), slot_of, parent_of, *[in_vmem(s) for s in stress])
    return (
        new_fields.reshape(fields.shape),
        wall_stress.reshape(levels, SLOTS, columns),
        parent_mean,
    )


def solution(mesh):
    in_specs = (
        P(None, "gz", ("groups", "gx"), "gy"),
        P(None, ("groups", "gz")),
        P(),
        P(("groups", "gx"), "gy"),
        P(("groups", "gx")),
        P("groups"),
        P("groups"),
    )
    out_specs = (
        P(None, "gz", ("groups", "gx"), "gy"),
        P("gz", ("groups", "gx"), "gy"),
        P(("groups", "gx"), None, "gz", "gy"),
    )
    return jax.shard_map(body, mesh=mesh, in_specs=in_specs, out_specs=out_specs, check_vma=False)
```

```python
import functools

import jax
import jax.numpy as jnp
from jax import lax
from jax.experimental import pallas as pl
from jax.experimental.pallas import tpu as pltpu
from jax.sharding import PartitionSpec as P

FIELDS = 5
RATIO = 8
BMAX = 32
SLOTS = 8

TABLE = (0.4, 0.8, 1.3, 2.0)
STEP = 0.25

FRONT = 8
LANES = 128
F32 = jnp.float32

VM = pl.BlockSpec(memory_space=pltpu.VMEM)
SM = pl.BlockSpec(memory_space=pltpu.SMEM)


def in_hbm(array):
    return pltpu.with_memory_space_constraint(array, pltpu.HBM)


def in_vmem(array):
    return pltpu.with_memory_space_constraint(array, pltpu.VMEM)


class Dims:
    def __init__(self, levels, tiles, columns, all_tiles, n_gx, n_gy):
        self.levels, self.tiles, self.columns = levels, tiles, columns
        self.all_tiles, self.n_gx, self.n_gy = all_tiles, n_gx, n_gy
        self.block = FRONT + tiles
        self.pad_rows = FIELDS * (levels + 2) * self.block + 8
        self.capacity = (tiles + n_gx - 1) // n_gx
        self.per_group = LANES // (2 * levels)
        self.groups = -(-FIELDS // self.per_group)
        self.parents = tiles // RATIO
        self.y_sends = 1 if n_gy == 2 else 2


def base_row(d, f, z):
    return (f * (d.levels + 2) + z + 1) * d.block


def lane_of(d, f, z):
    return 2 * ((f % d.per_group) * d.levels + z)


def x_choices(d):
    even = lax.rem(lax.axis_index("gx"), 2) == 0
    return [jnp.where(even, d.tiles - 1, 0), jnp.where(even, 0, d.tiles - 1)]


def add_edges(d, packed, pad, f, lane):
    pair = lax.rem(lax.shift_right_logical(lane + 1, 1), LANES // 2)
    g = f // d.per_group
    for z in range(d.levels):
        cells = pad[pl.ds(base_row(d, f, z) + FRONT, d.tiles), :]
        place = lane_of(d, f, z)
        moved = pltpu.roll(cells, place, 1) if place else cells
        packed[g] = jnp.where(pair == place // 2, moved, packed[g])
    return packed


def write_y(d, outs, packed, lane):
    odd = lax.rem(lane, 2) == 1
    first = lax.axis_index("gy") == 0
    for g in range(d.groups):
        tail = pltpu.roll(jnp.where(odd, packed[g], 0.0), 2, 1)
        head = jnp.where(odd, 0.0, packed[g])
        messages = [jnp.where(first, tail, head)] if d.y_sends == 1 else [tail, head]
        for out, message in zip(outs, messages):
            out[:, g * LANES : (g + 1) * LANES] = message


def pack_kernel(d, fields, *refs):
    n_small = len(refs[: (len(refs) - 5 - d.y_sends) // 2])
    small, refs = refs[:n_small], refs[n_small:]
    small_out, (pad, xa, xb, zface), yq = refs[:n_small], refs[n_small : n_small + 4], refs[n_small + 4 : -1]
    sems = refs[-1]
    lane = lax.broadcasted_iota(jnp.int32, (d.tiles, LANES), 1)
    copies = []
    for f in range(FIELDS):
        blocks = pad.at[pl.ds(base_row(d, f, 0), d.levels * d.block), :].reshape(d.levels, d.block, LANES)
        copies.append(pltpu.make_async_copy(fields.at[f], blocks.at[:, pl.ds(FRONT, d.tiles), :], sems.at[f]))
    moves = [
        pltpu.make_async_copy(source, target, sems.at[FIELDS + i])
        for i, (source, target) in enumerate(zip(small, small_out))
    ]
    for copy in copies + moves:
        copy.start()
    z_out = jnp.where(lax.axis_index("gz") == 0, d.levels - 1, 0)
    packed = [jnp.zeros((d.tiles, LANES), F32)] * d.groups
    for f in range(FIELDS):
        copies[f].wait()
        packed = add_edges(d, packed, pad, f, lane)
        for out, tile in zip((xa, xb), x_choices(d)):
            out[f * d.levels : (f + 1) * d.levels, :] = pad[
                pl.ds(base_row(d, f, 0) + FRONT + tile, d.levels, stride=d.block), :
            ]
        zface[f * d.tiles : (f + 1) * d.tiles, :] = pad[
            pl.ds(pl.multiple_of(base_row(d, f, z_out) + FRONT, 8), d.tiles), :
        ]
    write_y(d, yq, packed, lane)
    for copy in moves:
        copy.wait()


def set_halos(d, pad, xa, xb, zface):
    me = lax.axis_index("gx")
    even = lax.rem(me, 2) == 0
    zero_x = jnp.zeros((d.levels, LANES), F32)
    for f in range(FIELDS):
        a = xa[f * d.levels : (f + 1) * d.levels, :]
        b = xb[f * d.levels : (f + 1) * d.levels, :]
        left = jnp.where(me == 0, zero_x, jnp.where(even, b, a))
        right = jnp.where(me == d.n_gx - 1, zero_x, jnp.where(even, a, b))
        pad[pl.ds(base_row(d, f, 0) + FRONT - 1, d.levels, stride=d.block), :] = left
        pad[pl.ds(base_row(d, f, 0) + d.block, d.levels, stride=d.block), :] = right
    low = lax.axis_index("gz") == 0
    zero_z = jnp.zeros((d.tiles, LANES), F32)
    for f in range(FIELDS):
        face = zface[f * d.tiles : (f + 1) * d.tiles, :]
        pad[pl.ds(base_row(d, f, -1) + FRONT, d.tiles), :] = jnp.where(low, zero_z, face)
        pad[pl.ds(base_row(d, f, d.levels) + FRONT, d.tiles), :] = jnp.where(low, face, zero_z)


def stencil(d, pad, yq, wind, diff, f, z, lane):
    base = base_row(d, f, z)
    v = pad[pl.ds(pl.multiple_of(base + FRONT, 8), d.tiles), :]
    xm = pad[pl.ds(base + FRONT - 1, d.tiles), :]
    xp = pad[pl.ds(base + FRONT + 1, d.tiles), :]
    zm = pad[pl.ds(pl.multiple_of(base + FRONT - d.block, 8), d.tiles), :]
    zp = pad[pl.ds(pl.multiple_of(base + FRONT + d.block, 8), d.tiles), :]
    g = f // d.per_group
    halo = yq[0][:, g * LANES : (g + 1) * LANES]
    if d.y_sends == 2:
        halo = halo + yq[1][:, g * LANES : (g + 1) * LANES]
    halo = pltpu.roll(halo, LANES - 1 - lane_of(d, f, z), 1)
    yp = jnp.where(lane == d.columns - 1, halo, pltpu.roll(v, LANES - 1, 1))
    ym = jnp.where(lane == 0, halo, pltpu.roll(v, 1, 1))
    spread = STEP * diff[f]
    wx = (0.5 * STEP) * wind[0, z]
    wy = (0.5 * STEP) * wind[1, z]
    wz = (0.5 * STEP) * wind[2, z]
    new = (1.0 - 6.0 * spread) * v
    new = new + ((spread - wx) * xp + (spread + wx) * xm)
    new = new + ((spread - wy) * yp + (spread + wy) * ym)
    new = new + ((spread - wz) * zp + (spread + wz) * zm)
    return v, new


def speed(u, v, w):
    return jnp.sqrt(u * u + v * v + w * w + 1.0)


def wall_coefficients(d, wall_type, count, slot_of):
    first_tile = lax.axis_index("gx") * d.tiles
    row = lax.broadcasted_iota(jnp.int32, (d.tiles, LANES), 0)
    strength = jnp.zeros((d.tiles, LANES), F32)
    for x in range(d.tiles):
        held = jnp.where(slot_of[first_tile + x] >= 0, count[x], 0).astype(F32) * (1.0 / BMAX)
        strength = jnp.where(row == x, held, strength)
    kind = wall_type[...]
    value = jnp.zeros((d.tiles, LANES), F32)
    for code, entry in enumerate(TABLE):
        value = jnp.where(kind == code, entry, value)
    return value * strength


def step_one_kernel(d, pad_in, xa, xb, zface, *refs):
    yq = refs[: d.y_sends]
    wall_type, wind, diff, count, slot_of = refs[d.y_sends : d.y_sends + 5]
    outs = refs[d.y_sends + 5 :]
    pad, new_pad, factor, xa_out, xb_out, z_out = outs[:6]
    yq_out = outs[6 : 6 + d.y_sends]
    stress = outs[6 + d.y_sends : 6 + d.y_sends + d.n_gx]
    table, tally = outs[6 + d.y_sends + d.n_gx :]
    set_halos(d, pad, xa, xb, zface)
    lane = lax.broadcasted_iota(jnp.int32, (d.tiles, LANES), 1)
    zeros = jnp.zeros((d.tiles, LANES), F32)
    coef = wall_coefficients(d, wall_type, count, slot_of)

    def level(z, carry):
        both = [stencil(d, pad, yq, wind, diff, f, z, lane) for f in range(FIELDS)]
        drag = STEP * (coef * speed(*(both[f][0] for f in range(3))))
        news = [both[f][1] - drag * both[f][0] if f < 3 else both[f][1] for f in range(FIELDS)]
        for f in range(FIELDS):
            new_pad[pl.ds(pl.multiple_of(base_row(d, f, z) + FRONT, 8), d.tiles), :] = news[f]
        factor[pl.ds(pl.multiple_of(z * d.tiles, 8), d.tiles), :] = coef * speed(*news[:3])
        return carry

    lax.fori_loop(0, d.levels, level, 0, unroll=8)
    packed = [zeros] * d.groups
    for f in range(FIELDS):
        packed = add_edges(d, packed, new_pad, f, lane)
    write_y(d, yq_out, packed, lane)
    for out, tile in zip((xa_out, xb_out), x_choices(d)):
        for f in range(FIELDS):
            out[f * d.levels : (f + 1) * d.levels, :] = new_pad[
                pl.ds(base_row(d, f, 0) + FRONT + tile, d.levels, stride=d.block), :
            ]
    z_level = jnp.where(lax.axis_index("gz") == 0, d.levels - 1, 0)
    for f in range(FIELDS):
        z_out[f * d.tiles : (f + 1) * d.tiles, :] = new_pad[
            pl.ds(pl.multiple_of(base_row(d, f, z_level) + FRONT, 8), d.tiles), :
        ]
    me = lax.axis_index("gx")
    for k in range(d.n_gx):
        tally[k] = 0
    for i in range(d.n_gx * d.capacity):
        table[i] = 0
    for x in range(d.tiles):
        slot = slot_of[me * d.tiles + x]

        @pl.when(slot >= 0)
        def _():
            away = lax.rem(lax.shift_right_logical(slot, 3) - me + d.n_gx, d.n_gx)
            rank = tally[away]
            table[away * d.capacity + rank] = x
            tally[away] = rank + 1

    for k in range(d.n_gx):
        for c in range(d.capacity):
            tile = table[k * d.capacity + c]
            stress[k][c * d.levels : (c + 1) * d.levels, :] = factor[pl.ds(tile, d.levels, stride=d.tiles), :]


def step_two_kernel(d, pad_in, factor, xa, xb, zface, *refs):
    yq = refs[: d.y_sends]
    wind, diff, parent_of = refs[d.y_sends : d.y_sends + 3]
    pad, new_fields, own_sums, sent_sums, coarse = refs[d.y_sends + 3 :]
    set_halos(d, pad, xa, xb, zface)
    lane = lax.broadcasted_iota(jnp.int32, (d.tiles, LANES), 1)
    row = lax.broadcasted_iota(jnp.int32, (d.tiles, LANES), 0)
    zeros = jnp.zeros((d.tiles, LANES), F32)
    me = lax.axis_index("gx")
    held = jnp.full((d.tiles, LANES), -1, jnp.int32)
    for x in range(d.tiles):
        held = jnp.where(row == x, parent_of[me * d.tiles + x] - me * d.parents, held)
    masks = [jnp.where(held == p, 1.0, 0.0) for p in range(d.parents + 1)]
    coarse_levels = d.levels // RATIO
    coarse[...] = jnp.zeros_like(coarse)
    rows = d.levels * d.tiles
    per_parent = own_sums.shape[0] // d.parents

    def coarse_level(k, carry):
        def level(i, sums):
            z = k * RATIO + i
            drag = STEP * factor[pl.ds(pl.multiple_of(z * d.tiles, 8), d.tiles), :]
            added = []
            for f in range(FIELDS):
                v, new = stencil(d, pad, yq, wind, diff, f, z, lane)
                if f < 3:
                    new = new - drag * v
                new_fields[pl.ds(pl.multiple_of(f * rows + z * d.tiles, 8), d.tiles), :] = new
                added.append(sums[f] + new)
            return tuple(added)

        sums = lax.fori_loop(0, RATIO, level, (zeros,) * FIELDS, unroll=8)
        for p in range(d.parents + 1):
            for f in range(FIELDS):
                line = jnp.sum(sums[f] * masks[p], axis=0, keepdims=True)
                coarse[pl.ds(p * per_parent + f * coarse_levels + k, 1), :] = line
        return carry

    lax.fori_loop(0, coarse_levels, coarse_level, 0)
    pick_row = lax.broadcasted_iota(jnp.int32, (LANES, LANES), 0)
    pick_lane = lax.broadcasted_iota(jnp.int32, (LANES, LANES), 1)
    pick = jnp.where(pick_row // RATIO == pick_lane, 1.0, 0.0)
    summed = jnp.dot(coarse[...], pick, precision=lax.Precision.HIGHEST, preferred_element_type=F32)
    own_sums[...] = summed[: d.parents * per_parent, :]
    sent_sums[...] = summed[d.parents * per_parent :, :]


def place_kernel(d, own_sums, got_sums, slot_of, parent_of, *refs):
    stress = refs[: d.n_gx]
    wall_stress, parent_mean, gathered, table = refs[d.n_gx :]
    me = lax.axis_index("gx")
    part = d.capacity * d.levels
    for k in range(d.n_gx):
        gathered[k * part : (k + 1) * part, :] = stress[k][...]

    def source(s, carry):
        away = lax.rem(me - s + d.n_gx, d.n_gx)

        def tile(x, rank):
            slot = slot_of[s * d.tiles + x]
            mine = (slot >= 0) & (lax.shift_right_logical(slot, 3) == me)
            place = jnp.where(mine, slot - me * SLOTS, SLOTS)
            table[place] = away * d.capacity + rank
            return rank + mine.astype(jnp.int32)

        lax.fori_loop(0, d.tiles, tile, 0, unroll=True)
        return carry

    lax.fori_loop(0, d.n_gx, source, 0)
    for s in range(SLOTS):
        start = pl.multiple_of(table[s] * d.levels, 8)
        wall_stress[pl.ds(s, d.levels, stride=SLOTS), :] = gathered[pl.ds(start, d.levels), :]
    before = jnp.maximum(me - 1, 0) * d.tiles
    per_parent = own_sums.shape[0] // d.parents
    coarse_levels = d.levels // RATIO
    cells = d.columns // RATIO
    for p in range(d.parents):
        count = jnp.int32(0)
        for x in range(d.tiles):
            count = count + (parent_of[me * d.tiles + x] == me * d.parents + p).astype(jnp.int32)
            if p == 0:
                earlier = parent_of[before + x] == me * d.parents + p
                count = count + ((me > 0) & earlier).astype(jnp.int32)
        total = own_sums[p * per_parent : (p + 1) * per_parent, :]
        if p == 0:
            total = jnp.where(me == 0, total, total + got_sums[...])
        mean = total / (jnp.full(total.shape, count, jnp.int32).astype(F32) * (RATIO * RATIO))
        for f in range(FIELDS):
            parent_mean[p, f] = mean[f * coarse_levels : (f + 1) * coarse_levels, :cells]


def swapped(block, axis):
    return lax.ppermute(block, axis, [(i, i ^ 1) for i in range(lax.axis_size(axis))])


def swapped_between(block, axis):
    n = lax.axis_size(axis)
    other = lambda i: (i + 1) % n if i % 2 else (i - 1) % n
    return lax.ppermute(block, axis, [(i, other(i)) for i in range(n)])


def rotated(block, axis, distance):
    n = lax.axis_size(axis)
    return lax.ppermute(block, axis, [(i, (i + distance) % n) for i in range(n)])


def faces_swapped(d, xa, xb, zface, yq):
    xa = swapped(xa, "gx")
    xb = swapped_between(xb, "gx")
    if d.y_sends == 1:
        yq = [swapped(yq[0], "gy")]
    else:
        n = d.n_gy
        yq = [
            lax.ppermute(yq[0], "gy", [(i, i + 1) for i in range(n - 1)]),
            lax.ppermute(yq[1], "gy", [(i + 1, i) for i in range(n - 1)]),
        ]
    zface = swapped(zface, "gz")
    return [in_vmem(a) for a in (xa, xb, zface, *yq)]


def body(fields, parent_wind, diffusivity, wall_type, building_count, slot_of, parent_of):
    _, levels, tiles, columns = fields.shape
    d = Dims(levels, tiles, columns, slot_of.shape[0], lax.axis_size("gx"), lax.axis_size("gy"))
    assert columns == LANES and lax.axis_size("gz") == 2 and d.n_gx % 2 == 0
    params = pltpu.CompilerParams(vmem_limit_bytes=24 << 20)
    small = [in_hbm(a) for a in (wall_type, parent_wind, diffusivity, building_count, slot_of, parent_of)]
    rows = FIELDS * levels * tiles
    pad_t = pltpu.VMEM((d.pad_rows, LANES), F32)
    x_t = pltpu.VMEM((FIELDS * levels, LANES), F32)
    z_t = pltpu.VMEM((FIELDS * tiles, LANES), F32)
    y_ts = [pltpu.VMEM((tiles, d.groups * LANES), F32)] * d.y_sends
    stress_t = pltpu.VMEM((d.capacity * levels, LANES), F32)

    n_small = len(small)
    *small, pad, xa, xb, zface = (packed := pl.pallas_call(
        functools.partial(pack_kernel, d),
        out_shape=[pltpu.SMEM(a.shape, a.dtype) if a.shape != wall_type.shape else pltpu.VMEM(a.shape, a.dtype) for a in small]
        + [pad_t, x_t, x_t, z_t, *y_ts],
        in_specs=[pl.BlockSpec(memory_space=pltpu.HBM)] * (1 + n_small),
        out_specs=[VM] + [SM] * (n_small - 1) + [VM] * (4 + d.y_sends),
        scratch_shapes=[pltpu.SemaphoreType.DMA((FIELDS + n_small,))],
        compiler_params=params,
        name="pack",
    )(in_hbm(fields), *small))[: n_small + 4]
    yq = packed[n_small + 4 :]
    faces = faces_swapped(d, xa, xb, zface, yq)

    n_out = 6 + d.y_sends + d.n_gx
    _, new_pad, factor, xa, xb, zface, *rest = pl.pallas_call(
        functools.partial(step_one_kernel, d),
        out_shape=[pad_t, pad_t, pltpu.VMEM(((levels + 1) * tiles, LANES), F32), x_t, x_t, z_t, *y_ts]
        + [stress_t] * d.n_gx,
        in_specs=[VM] * (5 + d.y_sends) + [SM] * 4,
        out_specs=[VM] * n_out,
        scratch_shapes=[pltpu.SMEM((d.n_gx * d.capacity,), jnp.int32), pltpu.SMEM((d.n_gx,), jnp.int32)],
        input_output_aliases={0: 0},
        compiler_params=params,
        name="step_one",
    )(in_vmem(pad), *faces, *small[:5])
    yq, stress = rest[: d.y_sends], rest[d.y_sends :]
    faces = faces_swapped(d, xa, xb, zface, yq)
    stress = [stress[0]] + [rotated(stress[k], "gx", k) for k in range(1, d.n_gx)]

    per_parent = -(-FIELDS * (levels // RATIO) // 8) * 8
    _, new_fields, own_sums, sent_sums = pl.pallas_call(
        functools.partial(step_two_kernel, d),
        out_shape=[
            pad_t,
            jax.ShapeDtypeStruct((rows, LANES), F32),
            pltpu.VMEM((d.parents * per_parent, LANES), F32),
            pltpu.VMEM((per_parent, LANES), F32),
        ],
        in_specs=[VM] * (5 + d.y_sends) + [SM] * 3,
        out_specs=[VM] * 4,
        scratch_shapes=[pltpu.VMEM(((d.parents + 1) * per_parent, LANES), F32)],
        input_output_aliases={0: 0},
        compiler_params=params,
        name="step_two",
    )(in_vmem(new_pad), in_vmem(factor), *faces, small[1], small[2], small[5])
    got_sums = rotated(sent_sums, "gx", 1)

    wall_stress, parent_mean = pl.pallas_call(
        functools.partial(place_kernel, d),
        out_shape=[
            jax.ShapeDtypeStruct((levels * SLOTS, LANES), F32),
            jax.ShapeDtypeStruct((d.parents, FIELDS, levels // RATIO, columns // RATIO), F32),
        ],
        in_specs=[VM, VM, SM, SM] + [VM] * d.n_gx,
        out_specs=[VM, VM],
        scratch_shapes=[
            pltpu.VMEM((d.n_gx * d.capacity * levels, LANES), F32),
            pltpu.SMEM((SLOTS + 1,), jnp.int32),
        ],
        compiler_params=params,
        name="place",
    )(in_vmem(own_sums), in_vmem(got_sums), small[4], small[5], *[in_vmem(s) for s in stress])
    return (
        new_fields.reshape(fields.shape),
        wall_stress.reshape(levels, SLOTS, columns),
        parent_mean,
    )


def solution(mesh):
    in_specs = (
        P(None, "gz", ("groups", "gx"), "gy"),
        P(None, ("groups", "gz")),
        P(),
        P(("groups", "gx"), "gy"),
        P(("groups", "gx")),
        P("groups"),
        P("groups"),
    )
    out_specs = (
        P(None, "gz", ("groups", "gx"), "gy"),
        P("gz", ("groups", "gx"), "gy"),
        P(("groups", "gx"), None, "gz", "gy"),
    )
    return jax.shard_map(body, mesh=mesh, in_specs=in_specs, out_specs=out_specs, check_vma=False)
```

```python
import functools

import jax
import jax.numpy as jnp
from jax import lax
from jax.experimental import pallas as pl
from jax.experimental.pallas import tpu as pltpu
from jax.sharding import PartitionSpec as P

FIELDS = 5
RATIO = 8
BMAX = 32
SLOTS = 8

TABLE = (0.4, 0.8, 1.3, 2.0)
STEP = 0.25

FRONT = 8
LANES = 128
F32 = jnp.float32

VM = pl.BlockSpec(memory_space=pltpu.VMEM)
SM = pl.BlockSpec(memory_space=pltpu.SMEM)


def in_hbm(array):
    return pltpu.with_memory_space_constraint(array, pltpu.HBM)


def in_vmem(array):
    return pltpu.with_memory_space_constraint(array, pltpu.VMEM)


class Dims:
    def __init__(self, levels, tiles, columns, all_tiles, n_gx, n_gy):
        self.levels, self.tiles, self.columns = levels, tiles, columns
        self.all_tiles, self.n_gx, self.n_gy = all_tiles, n_gx, n_gy
        self.block = FRONT + tiles
        self.pad_rows = FIELDS * (levels + 2) * self.block + 8
        self.capacity = (tiles + n_gx - 1) // n_gx
        self.per_group = LANES // (2 * levels)
        self.groups = -(-FIELDS // self.per_group)
        self.parents = tiles // RATIO
        self.y_sends = 1 if n_gy == 2 else 2


def base_row(d, f, z):
    return (f * (d.levels + 2) + z + 1) * d.block


def lane_of(d, f, z):
    return 2 * ((f % d.per_group) * d.levels + z)


def x_choices(d):
    even = lax.rem(lax.axis_index("gx"), 2) == 0
    return [jnp.where(even, d.tiles - 1, 0), jnp.where(even, 0, d.tiles - 1)]


def add_edges(d, packed, pad, f, lane):
    pair = lax.rem(lax.shift_right_logical(lane + 1, 1), LANES // 2)
    g = f // d.per_group
    for z in range(d.levels):
        cells = pad[pl.ds(base_row(d, f, z) + FRONT, d.tiles), :]
        place = lane_of(d, f, z)
        moved = pltpu.roll(cells, place, 1) if place else cells
        packed[g] = jnp.where(pair == place // 2, moved, packed[g])
    return packed


def write_y(d, outs, packed, lane):
    odd = lax.rem(lane, 2) == 1
    first = lax.axis_index("gy") == 0
    for g in range(d.groups):
        tail = pltpu.roll(jnp.where(odd, packed[g], 0.0), 2, 1)
        head = jnp.where(odd, 0.0, packed[g])
        messages = [jnp.where(first, tail, head)] if d.y_sends == 1 else [tail, head]
        for out, message in zip(outs, messages):
            out[:, g * LANES : (g + 1) * LANES] = message


def pack_kernel(d, fields, *refs):
    n_small = len(refs[: (len(refs) - 5 - d.y_sends) // 2])
    small, refs = refs[:n_small], refs[n_small:]
    small_out, (pad, xa, xb, zface), yq = refs[:n_small], refs[n_small : n_small + 4], refs[n_small + 4 : -1]
    sems = refs[-1]
    lane = lax.broadcasted_iota(jnp.int32, (d.tiles, LANES), 1)
    copies = []
    for f in range(FIELDS):
        blocks = pad.at[pl.ds(base_row(d, f, 0), d.levels * d.block), :].reshape(d.levels, d.block, LANES)
        copies.append(pltpu.make_async_copy(fields.at[f], blocks.at[:, pl.ds(FRONT, d.tiles), :], sems.at[f]))
    moves = [
        pltpu.make_async_copy(source, target, sems.at[FIELDS + i])
        for i, (source, target) in enumerate(zip(small, small_out))
    ]
    for copy in copies + moves:
        copy.start()
    z_out = jnp.where(lax.axis_index("gz") == 0, d.levels - 1, 0)
    packed = [jnp.zeros((d.tiles, LANES), F32)] * d.groups
    for f in range(FIELDS):
        copies[f].wait()
        packed = add_edges(d, packed, pad, f, lane)
        for out, tile in zip((xa, xb), x_choices(d)):
            out[f * d.levels : (f + 1) * d.levels, :] = pad[
                pl.ds(base_row(d, f, 0) + FRONT + tile, d.levels, stride=d.block), :
            ]
        zface[f * d.tiles : (f + 1) * d.tiles, :] = pad[
            pl.ds(pl.multiple_of(base_row(d, f, z_out) + FRONT, 8), d.tiles), :
        ]
    write_y(d, yq, packed, lane)
    for copy in moves:
        copy.wait()


def x_halos(d, xa, xb, rows):
    me = lax.axis_index("gx")
    even = lax.rem(me, 2) == 0
    a, b = xa[rows, :], xb[rows, :]
    left = jnp.where(me == 0, 0.0, jnp.where(even, b, a))
    right = jnp.where(me == d.n_gx - 1, 0.0, jnp.where(even, a, b))
    return left, right


def set_x_halos(d, pad, f, left, right):
    pad[pl.ds(base_row(d, f, 0) + FRONT - 1, d.levels, stride=d.block), :] = left
    pad[pl.ds(base_row(d, f, 0) + d.block, d.levels, stride=d.block), :] = right


def set_z_halos(d, pad, zface):
    low = lax.axis_index("gz") == 0
    for f in range(FIELDS):
        face = zface[f * d.tiles : (f + 1) * d.tiles, :]
        pad[pl.ds(base_row(d, f, -1) + FRONT, d.tiles), :] = jnp.where(low, 0.0, face)
        pad[pl.ds(base_row(d, f, d.levels) + FRONT, d.tiles), :] = jnp.where(low, face, 0.0)


def stencil(d, pad, yq, wind, diff, f, z, lane):
    base = base_row(d, f, z)
    v = pad[pl.ds(pl.multiple_of(base + FRONT, 8), d.tiles), :]
    xm = pad[pl.ds(base + FRONT - 1, d.tiles), :]
    xp = pad[pl.ds(base + FRONT + 1, d.tiles), :]
    zm = pad[pl.ds(pl.multiple_of(base + FRONT - d.block, 8), d.tiles), :]
    zp = pad[pl.ds(pl.multiple_of(base + FRONT + d.block, 8), d.tiles), :]
    g = f // d.per_group
    halo = yq[0][:, g * LANES : (g + 1) * LANES]
    if d.y_sends == 2:
        halo = halo + yq[1][:, g * LANES : (g + 1) * LANES]
    halo = pltpu.roll(halo, LANES - 1 - lane_of(d, f, z), 1)
    yp = jnp.where(lane == d.columns - 1, halo, pltpu.roll(v, LANES - 1, 1))
    ym = jnp.where(lane == 0, halo, pltpu.roll(v, 1, 1))
    spread = STEP * diff[f]
    wx = (0.5 * STEP) * wind[0, z]
    wy = (0.5 * STEP) * wind[1, z]
    wz = (0.5 * STEP) * wind[2, z]
    new = (1.0 - 6.0 * spread) * v
    new = new + ((spread - wx) * xp + (spread + wx) * xm)
    new = new + ((spread - wy) * yp + (spread + wy) * ym)
    new = new + ((spread - wz) * zp + (spread + wz) * zm)
    return v, new


def speed(u, v, w):
    return jnp.sqrt(u * u + v * v + w * w + 1.0)


def prepare_kernel(d, wall_type, wind, diff, count, slot_of, parent_of, *outs):
    wall_coef, from_left, from_right, masks, send_table, place_table, counts, tally = outs
    me = lax.axis_index("gx")
    first_tile = me * d.tiles
    row = lax.broadcasted_iota(jnp.int32, (d.tiles, LANES), 0)
    strength = jnp.zeros((d.tiles, LANES), F32)
    owner = jnp.full((d.tiles, LANES), -1, jnp.int32)
    for x in range(d.tiles):
        held = jnp.where(slot_of[first_tile + x] >= 0, count[x], 0).astype(F32) * (1.0 / BMAX)
        strength = jnp.where(row == x, held, strength)
        owner = jnp.where(row == x, parent_of[first_tile + x] - me * d.parents, owner)
    kind = wall_type[...]
    value = jnp.zeros((d.tiles, LANES), F32)
    for code, entry in enumerate(TABLE):
        value = jnp.where(kind == code, entry, value)
    wall_coef[...] = value * strength
    for p in range(d.parents + 1):
        masks[p * d.tiles : (p + 1) * d.tiles, :] = jnp.where(owner == p, 1.0, 0.0)
    for z in range(d.levels):
        wx = (0.5 * STEP) * wind[0, z]
        for f in range(FIELDS):
            spread = STEP * diff[f]
            from_left[f * d.levels + z : f * d.levels + z + 1, :] = jnp.full((1, LANES), spread + wx, F32)
            from_right[f * d.levels + z : f * d.levels + z + 1, :] = jnp.full((1, LANES), spread - wx, F32)
    for k in range(d.n_gx):
        tally[k] = 0
    for i in range(d.n_gx * d.capacity):
        send_table[i] = 0
    for x in range(d.tiles):
        slot = slot_of[first_tile + x]

        @pl.when(slot >= 0)
        def _():
            away = lax.bitwise_xor(lax.shift_right_logical(slot, 3), me)
            rank = tally[away]
            send_table[away * d.capacity + rank] = x
            tally[away] = rank + 1

    def source(s, carry):
        away = lax.bitwise_xor(s, me)

        def tile(x, rank):
            slot = slot_of[s * d.tiles + x]
            mine = (slot >= 0) & (lax.shift_right_logical(slot, 3) == me)
            place = jnp.where(mine, slot - me * SLOTS, SLOTS)
            place_table[place] = away * d.capacity + rank
            return rank + mine.astype(jnp.int32)

        lax.fori_loop(0, d.tiles, tile, 0, unroll=True)
        return carry

    lax.fori_loop(0, d.n_gx, source, 0)
    before = jnp.maximum(first_tile - d.tiles, 0)
    for p in range(d.parents):
        total = jnp.int32(0)
        for x in range(d.tiles):
            total = total + (parent_of[first_tile + x] == me * d.parents + p).astype(jnp.int32)
            if p == 0:
                earlier = parent_of[before + x] == me * d.parents
                total = total + ((me > 0) & earlier).astype(jnp.int32)
        counts[p] = total


def step_one_kernel(d, pad_in, xa, xb, zface, *refs):
    yq = refs[: d.y_sends]
    wall_coef, wind, diff, send_table = refs[d.y_sends : d.y_sends + 4]
    outs = refs[d.y_sends + 4 :]
    pad, new_pad, factor, z_out = outs[:4]
    yq_out = outs[4 : 4 + d.y_sends]
    stress = outs[4 + d.y_sends :]
    for f in range(FIELDS):
        set_x_halos(d, pad, f, *x_halos(d, xa, xb, slice(f * d.levels, (f + 1) * d.levels)))
    set_z_halos(d, pad, zface)
    lane = lax.broadcasted_iota(jnp.int32, (d.tiles, LANES), 1)
    zeros = jnp.zeros((d.tiles, LANES), F32)
    coef = wall_coef[...]

    def level(z, carry):
        both = [stencil(d, pad, yq, wind, diff, f, z, lane) for f in range(FIELDS)]
        drag = STEP * (coef * speed(*(both[f][0] for f in range(3))))
        news = [both[f][1] - drag * both[f][0] if f < 3 else both[f][1] for f in range(FIELDS)]
        for f in range(FIELDS):
            new_pad[pl.ds(pl.multiple_of(base_row(d, f, z) + FRONT, 8), d.tiles), :] = news[f]
        factor[pl.ds(pl.multiple_of(z * d.tiles, 8), d.tiles), :] = coef * speed(*news[:3])
        return carry

    lax.fori_loop(0, d.levels, level, 0, unroll=8)
    packed = [zeros] * d.groups
    for f in range(FIELDS):
        packed = add_edges(d, packed, new_pad, f, lane)
    write_y(d, yq_out, packed, lane)
    z_level = jnp.where(lax.axis_index("gz") == 0, d.levels - 1, 0)
    for f in range(FIELDS):
        z_out[f * d.tiles : (f + 1) * d.tiles, :] = new_pad[
            pl.ds(pl.multiple_of(base_row(d, f, z_level) + FRONT, 8), d.tiles), :
        ]
    for k in range(d.n_gx):
        for c in range(d.capacity):
            tile = send_table[k * d.capacity + c]
            stress[k][c * d.levels : (c + 1) * d.levels, :] = factor[pl.ds(tile, d.levels, stride=d.tiles), :]


def step_two_kernel(d, pad_in, factor, zface, *refs):
    yq = refs[: d.y_sends]
    masks_in, wind, diff = refs[d.y_sends : d.y_sends + 3]
    pad, new_fields, coarse, xa_out, xb_out = refs[-5:]
    zero_x = jnp.zeros((d.levels, LANES), F32)
    for f in range(FIELDS):
        set_x_halos(d, pad, f, zero_x, zero_x)
    set_z_halos(d, pad, zface)
    lane = lax.broadcasted_iota(jnp.int32, (d.tiles, LANES), 1)
    zeros = jnp.zeros((d.tiles, LANES), F32)
    masks = [masks_in[p * d.tiles : (p + 1) * d.tiles, :] for p in range(d.parents + 1)]
    coarse_levels = d.levels // RATIO
    coarse[...] = jnp.zeros_like(coarse)
    rows = d.levels * d.tiles
    per_parent = coarse.shape[0] // (d.parents + 1)

    def coarse_level(k, carry):
        def level(i, sums):
            z = k * RATIO + i
            drag = STEP * factor[pl.ds(pl.multiple_of(z * d.tiles, 8), d.tiles), :]
            added = []
            for f in range(FIELDS):
                v, new = stencil(d, pad, yq, wind, diff, f, z, lane)
                if f < 3:
                    new = new - drag * v
                new_fields[pl.ds(pl.multiple_of(f * rows + z * d.tiles, 8), d.tiles), :] = new
                added.append(sums[f] + new)
            return tuple(added)

        sums = lax.fori_loop(0, RATIO, level, (zeros,) * FIELDS, unroll=8)
        for p in range(d.parents + 1):
            for f in range(FIELDS):
                line = jnp.sum(sums[f] * masks[p], axis=0, keepdims=True)
                coarse[pl.ds(p * per_parent + f * coarse_levels + k, 1), :] = line
        return carry

    lax.fori_loop(0, coarse_levels, coarse_level, 0)
    edge = FIELDS * d.levels
    for out, tile in zip((xa_out, xb_out), x_choices(d)):
        for f in range(FIELDS):
            out[f * d.levels : (f + 1) * d.levels, :] = pad[
                pl.ds(base_row(d, f, 0) + FRONT + tile, d.levels, stride=d.block), :
            ]
        out[edge : edge + per_parent, :] = coarse[d.parents * per_parent :, :]


def finish_kernel(d, from_left, from_right, state_in, xa, xb, own_a, own_b, coarse, parent_of, place_table, counts, *refs):
    stress = refs[: d.n_gx]
    state, new_fields, wall_stress, parent_mean, terms, gathered, placed, sems = refs[d.n_gx :]
    me = lax.axis_index("gx")
    even = lax.rem(me, 2) == 0
    rows = d.levels * d.tiles
    coarse_levels = d.levels // RATIO
    per_parent = coarse.shape[0] // (d.parents + 1)
    copies = []
    for f in range(FIELDS):
        cut = slice(f * d.levels, (f + 1) * d.levels)
        left, right = x_halos(d, xa, xb, cut)
        left, right = from_left[cut, :] * left, from_right[cut, :] * right
        ahead = from_right[cut, :] * jnp.where(even, own_b[cut, :], own_a[cut, :])
        for tile, added in ((0, left), (d.tiles - 1, right)):
            place = pl.ds(f * rows + tile, d.levels, stride=d.tiles)
            state[place, :] = state[place, :] + added
        copies.append(
            pltpu.make_async_copy(
                state.at[pl.ds(f * rows, rows), :], new_fields.at[pl.ds(f * rows, rows), :], sems.at[f]
            )
        )
        copies[-1].start()
        for i, term in enumerate((left, right, ahead)):
            terms[i * per_parent + f * coarse_levels : i * per_parent + (f + 1) * coarse_levels, :] = jnp.sum(
                term.reshape(coarse_levels, RATIO, LANES), axis=1
            )
    part = d.capacity * d.levels
    for k in range(d.n_gx):
        gathered[k * part : (k + 1) * part, :] = stress[k][...]
    for s in range(SLOTS):
        start = pl.multiple_of(place_table[s] * d.levels, 8)
        placed[pl.ds(s, d.levels, stride=SLOTS), :] = gathered[pl.ds(start, d.levels), :]
    copies.append(pltpu.make_async_copy(placed.at[pl.ds(0, d.levels * SLOTS), :], wall_stress, sems.at[FIELDS]))
    copies[-1].start()
    filled = FIELDS * coarse_levels
    if filled < per_parent:
        for i in range(3):
            terms[i * per_parent + filled : (i + 1) * per_parent, :] = jnp.zeros((per_parent - filled, LANES), F32)
    edge = FIELDS * d.levels
    got = jnp.where(even, xb[edge : edge + per_parent, :], xa[edge : edge + per_parent, :])
    first_tile = me * d.tiles
    first_parent = parent_of[first_tile] - me * d.parents
    last_parent = parent_of[first_tile + d.tiles - 1] - me * d.parents
    before = jnp.maximum(first_tile - 1, 0)
    ahead_counts = (me > 0) & (parent_of[before] == me * d.parents)
    pick_row = lax.broadcasted_iota(jnp.int32, (LANES, LANES), 0)
    pick_lane = lax.broadcasted_iota(jnp.int32, (LANES, LANES), 1)
    pick = jnp.where(pick_row // RATIO == pick_lane, 1.0, 0.0)
    for p in range(d.parents):
        total = coarse[p * per_parent : (p + 1) * per_parent, :]
        total = total + jnp.where(first_parent == p, terms[:per_parent, :], 0.0)
        total = total + jnp.where(last_parent == p, terms[per_parent : 2 * per_parent, :], 0.0)
        if p == 0:
            total = total + jnp.where(me == 0, 0.0, got)
            total = total + jnp.where(ahead_counts, terms[2 * per_parent :, :], 0.0)
        total = jnp.dot(total, pick, precision=lax.Precision.HIGHEST, preferred_element_type=F32)
        mean = total / (jnp.full(total.shape, counts[p], jnp.int32).astype(F32) * (RATIO * RATIO))
        for f in range(FIELDS):
            parent_mean[p, f] = mean[f * coarse_levels : (f + 1) * coarse_levels, : d.columns // RATIO]
    for copy in copies:
        copy.wait()


def swapped(block, axis):
    return lax.ppermute(block, axis, [(i, i ^ 1) for i in range(lax.axis_size(axis))])


def swapped_between(block, axis, inner):
    n = lax.axis_size(axis)
    route = []
    for i in range(n):
        for k in range(2):
            other = (i, 1 - k) if i in (0, n - 1) else (i + 1 if i % 2 else i - 1, k)
            route.append((2 * i + k, 2 * other[0] + other[1]))
    return lax.ppermute(block, (axis, inner), route)


def crossed(block, axis, distance):
    return lax.ppermute(block, axis, [(i, i ^ distance) for i in range(lax.axis_size(axis))])


def x_swapped(xa, xb):
    return [in_vmem(swapped(xa, "gx")), in_vmem(swapped_between(xb, "gx", "gz"))]


def zy_swapped(d, zface, yq):
    if d.y_sends == 1:
        yq = [swapped(yq[0], "gy")]
    else:
        n = d.n_gy
        yq = [
            lax.ppermute(yq[0], "gy", [(i, i + 1) for i in range(n - 1)]),
            lax.ppermute(yq[1], "gy", [(i + 1, i) for i in range(n - 1)]),
        ]
    return [in_vmem(a) for a in (swapped(zface, "gz"), *yq)]


def body(fields, parent_wind, diffusivity, wall_type, building_count, slot_of, parent_of):
    _, levels, tiles, columns = fields.shape
    d = Dims(levels, tiles, columns, slot_of.shape[0], lax.axis_size("gx"), lax.axis_size("gy"))
    assert columns == LANES and lax.axis_size("gz") == 2 and d.n_gx & (d.n_gx - 1) == 0
    params = pltpu.CompilerParams(vmem_limit_bytes=24 << 20)
    small = [in_hbm(a) for a in (wall_type, parent_wind, diffusivity, building_count, slot_of, parent_of)]
    rows = FIELDS * levels * tiles
    pad_t = pltpu.VMEM((d.pad_rows, LANES), F32)
    x_t = pltpu.VMEM((FIELDS * levels, LANES), F32)
    z_t = pltpu.VMEM((FIELDS * tiles, LANES), F32)
    y_ts = [pltpu.VMEM((tiles, d.groups * LANES), F32)] * d.y_sends
    stress_t = pltpu.VMEM((d.capacity * levels, LANES), F32)

    n_small = len(small)
    *small, pad, xa, xb, zface = (packed := pl.pallas_call(
        functools.partial(pack_kernel, d),
        out_shape=[pltpu.SMEM(a.shape, a.dtype) if a.shape != wall_type.shape else pltpu.VMEM(a.shape, a.dtype) for a in small]
        + [pad_t, x_t, x_t, z_t, *y_ts],
        in_specs=[pl.BlockSpec(memory_space=pltpu.HBM)] * (1 + n_small),
        out_specs=[VM] + [SM] * (n_small - 1) + [VM] * (4 + d.y_sends),
        scratch_shapes=[pltpu.SemaphoreType.DMA((FIELDS + n_small,))],
        compiler_params=params,
        name="pack",
    )(in_hbm(fields), *small))[: n_small + 4]
    yq = packed[n_small + 4 :]
    faces = x_swapped(xa, xb) + zy_swapped(d, zface, yq)
    hbm = pl.BlockSpec(memory_space=pltpu.HBM)

    def ints(n):
        return pltpu.SMEM((n,), jnp.int32)

    wall_coef, from_left, from_right, masks, send_table, place_table, counts = pl.pallas_call(
        functools.partial(prepare_kernel, d),
        out_shape=[pltpu.VMEM((tiles, LANES), F32), x_t, x_t, pltpu.VMEM(((d.parents + 1) * tiles, LANES), F32)]
        + [ints(d.n_gx * d.capacity), ints(SLOTS + 1), ints(d.parents)],
        in_specs=[VM] + [SM] * 5,
        out_specs=[VM] * 4 + [SM] * 3,
        scratch_shapes=[ints(d.n_gx)],
        compiler_params=params,
        name="prepare",
    )(in_vmem(small[0]), *small[1:])

    _, new_pad, factor, zface, *rest = pl.pallas_call(
        functools.partial(step_one_kernel, d),
        out_shape=[pad_t, pad_t, pltpu.VMEM(((levels + 1) * tiles, LANES), F32), z_t, *y_ts] + [stress_t] * d.n_gx,
        in_specs=[VM] * (5 + d.y_sends) + [SM] * 3,
        out_specs=[VM] * (4 + d.y_sends + d.n_gx),
        input_output_aliases={0: 0},
        compiler_params=params,
        name="step_one",
    )(in_vmem(pad), *faces, in_vmem(wall_coef), small[1], small[2], send_table)
    yq, stress = rest[: d.y_sends], rest[d.y_sends :]
    faces = zy_swapped(d, zface, yq)
    stress = [stress[0]] + [in_vmem(crossed(stress[k], "gx", k)) for k in range(1, d.n_gx)]

    early = stress[1:]
    per_parent = -(-FIELDS * (levels // RATIO) // 8) * 8
    state_t = pltpu.VMEM((rows + tiles, LANES), F32)
    message_t = pltpu.VMEM((FIELDS * levels + per_parent, LANES), F32)
    _, state, coarse, own_a, own_b = pl.pallas_call(
        functools.partial(step_two_kernel, d),
        out_shape=[pad_t, state_t, pltpu.VMEM(((d.parents + 1) * per_parent, LANES), F32), message_t, message_t],
        in_specs=[VM] * (4 + d.y_sends) + [SM] * 2 + [VM] * len(early),
        out_specs=[VM] * 5,
        input_output_aliases={0: 0},
        compiler_params=params,
        name="step_two",
    )(in_vmem(new_pad), in_vmem(factor), *faces, in_vmem(masks), small[1], small[2], *early)
    xs = x_swapped(own_a, own_b)

    _, new_fields, wall_stress, parent_mean = pl.pallas_call(
        functools.partial(finish_kernel, d),
        out_shape=[
            state_t,
            jax.ShapeDtypeStruct((rows, LANES), F32),
            jax.ShapeDtypeStruct((levels * SLOTS, LANES), F32),
            jax.ShapeDtypeStruct((d.parents, FIELDS, levels // RATIO, columns // RATIO), F32),
        ],
        in_specs=[VM] * 8 + [SM] * 3 + [VM] * d.n_gx,
        out_specs=[VM, hbm, hbm, VM],
        scratch_shapes=[
            pltpu.VMEM((3 * per_parent, LANES), F32),
            pltpu.VMEM((d.n_gx * d.capacity * levels, LANES), F32),
            pltpu.VMEM(((levels + 1) * SLOTS, LANES), F32),
            pltpu.SemaphoreType.DMA((FIELDS + 1,)),
        ],
        input_output_aliases={2: 0},
        compiler_params=params,
        name="finish",
    )(
        *[in_vmem(a) for a in (from_left, from_right, state, *xs, own_a, own_b, coarse)],
        small[5],
        place_table,
        counts,
        *[in_vmem(stress[0])],
        *stress[1:],
    )
    return (
        new_fields.reshape(fields.shape),
        wall_stress.reshape(levels, SLOTS, columns),
        parent_mean,
    )


def solution(mesh):
    in_specs = (
        P(None, "gz", ("groups", "gx"), "gy"),
        P(None, ("groups", "gz")),
        P(),
        P(("groups", "gx"), "gy"),
        P(("groups", "gx")),
        P("groups"),
        P("groups"),
    )
    out_specs = (
        P(None, "gz", ("groups", "gx"), "gy"),
        P("gz", ("groups", "gx"), "gy"),
        P(("groups", "gx"), None, "gz", "gy"),
    )
    return jax.shard_map(body, mesh=mesh, in_specs=in_specs, out_specs=out_specs, check_vma=False)
```

```python
import functools

import jax
import jax.numpy as jnp
from jax import lax
from jax.experimental import pallas as pl
from jax.experimental.pallas import tpu as pltpu
from jax.sharding import PartitionSpec as P

FIELDS = 5
RATIO = 8
BMAX = 32
SLOTS = 8

TABLE = (0.4, 0.8, 1.3, 2.0)
STEP = 0.25

FRONT = 8
LANES = 128
F32 = jnp.float32

VM = pl.BlockSpec(memory_space=pltpu.VMEM)
SM = pl.BlockSpec(memory_space=pltpu.SMEM)


def in_hbm(array):
    return pltpu.with_memory_space_constraint(array, pltpu.HBM)


def in_vmem(array):
    return pltpu.with_memory_space_constraint(array, pltpu.VMEM)


class Dims:
    def __init__(self, levels, tiles, columns, all_tiles, n_gx, n_gy):
        self.levels, self.tiles, self.columns = levels, tiles, columns
        self.all_tiles, self.n_gx, self.n_gy = all_tiles, n_gx, n_gy
        self.block = FRONT + tiles
        self.pad_rows = FIELDS * (levels + 2) * self.block + 8
        self.capacity = (tiles + n_gx - 1) // n_gx
        self.per_group = LANES // (2 * levels)
        self.groups = -(-FIELDS // self.per_group)
        self.parents = tiles // RATIO
        self.y_sends = 1 if n_gy == 2 else 2
        self.part = self.capacity * levels
        self.early = 2 if n_gx == 4 else 0
        self.late = FIELDS - self.early

    def riders(self, k):
        return self.levels * (FIELDS if k == 1 else self.early if k == 3 else 0)


def base_row(d, f, z):
    return (f * (d.levels + 2) + z + 1) * d.block


def lane_of(d, f, z):
    return 2 * ((f % d.per_group) * d.levels + z)


def x_choices(d):
    even = lax.rem(lax.axis_index("gx"), 2) == 0
    return [jnp.where(even, d.tiles - 1, 0), jnp.where(even, 0, d.tiles - 1)]


def add_edges(d, packed, pad, f, lane):
    pair = lax.rem(lax.shift_right_logical(lane + 1, 1), LANES // 2)
    g = f // d.per_group
    for z in range(d.levels):
        cells = pad[pl.ds(base_row(d, f, z) + FRONT, d.tiles), :]
        place = lane_of(d, f, z)
        moved = pltpu.roll(cells, place, 1) if place else cells
        packed[g] = jnp.where(pair == place // 2, moved, packed[g])
    return packed


def write_y(d, outs, packed, lane):
    odd = lax.rem(lane, 2) == 1
    first = lax.axis_index("gy") == 0
    for g in range(d.groups):
        tail = pltpu.roll(jnp.where(odd, packed[g], 0.0), 2, 1)
        head = jnp.where(odd, 0.0, packed[g])
        messages = [jnp.where(first, tail, head)] if d.y_sends == 1 else [tail, head]
        for out, message in zip(outs, messages):
            out[:, g * LANES : (g + 1) * LANES] = message


def pack_kernel(d, fields, *refs):
    n_small = len(refs[: (len(refs) - 5 - d.y_sends) // 2])
    small, refs = refs[:n_small], refs[n_small:]
    small_out, (pad, xa, xb, zface), yq = refs[:n_small], refs[n_small : n_small + 4], refs[n_small + 4 : -1]
    sems = refs[-1]
    lane = lax.broadcasted_iota(jnp.int32, (d.tiles, LANES), 1)
    copies = []
    for f in range(FIELDS):
        blocks = pad.at[pl.ds(base_row(d, f, 0), d.levels * d.block), :].reshape(d.levels, d.block, LANES)
        copies.append(pltpu.make_async_copy(fields.at[f], blocks.at[:, pl.ds(FRONT, d.tiles), :], sems.at[f]))
    moves = [
        pltpu.make_async_copy(source, target, sems.at[FIELDS + i])
        for i, (source, target) in enumerate(zip(small, small_out))
    ]
    for copy in copies + moves:
        copy.start()
    z_out = jnp.where(lax.axis_index("gz") == 0, d.levels - 1, 0)
    packed = [jnp.zeros((d.tiles, LANES), F32)] * d.groups
    for f in range(FIELDS):
        copies[f].wait()
        packed = add_edges(d, packed, pad, f, lane)
        for out, tile in zip((xa, xb), x_choices(d)):
            out[f * d.levels : (f + 1) * d.levels, :] = pad[
                pl.ds(base_row(d, f, 0) + FRONT + tile, d.levels, stride=d.block), :
            ]
        zface[f * d.tiles : (f + 1) * d.tiles, :] = pad[
            pl.ds(pl.multiple_of(base_row(d, f, z_out) + FRONT, 8), d.tiles), :
        ]
    write_y(d, yq, packed, lane)
    for copy in moves:
        copy.wait()


def x_halos(d, xa, xb, rows):
    a, b = xa[rows, :], xb[rows, :]
    return left_right(d, a, b)


def left_right(d, a, b):
    me = lax.axis_index("gx")
    even = lax.rem(me, 2) == 0
    left = jnp.where(me == 0, 0.0, jnp.where(even, b, a))
    right = jnp.where(me == d.n_gx - 1, 0.0, jnp.where(even, a, b))
    return left, right


def set_x_halos(d, pad, f, left, right):
    pad[pl.ds(base_row(d, f, 0) + FRONT - 1, d.levels, stride=d.block), :] = left
    pad[pl.ds(base_row(d, f, 0) + d.block, d.levels, stride=d.block), :] = right


def set_z_halos(d, pad, zface):
    low = lax.axis_index("gz") == 0
    for f in range(FIELDS):
        face = zface[f * d.tiles : (f + 1) * d.tiles, :]
        pad[pl.ds(base_row(d, f, -1) + FRONT, d.tiles), :] = jnp.where(low, 0.0, face)
        pad[pl.ds(base_row(d, f, d.levels) + FRONT, d.tiles), :] = jnp.where(low, face, 0.0)


def stencil(d, pad, yq, wind, diff, f, z, lane):
    base = base_row(d, f, z)
    v = pad[pl.ds(pl.multiple_of(base + FRONT, 8), d.tiles), :]
    xm = pad[pl.ds(base + FRONT - 1, d.tiles), :]
    xp = pad[pl.ds(base + FRONT + 1, d.tiles), :]
    zm = pad[pl.ds(pl.multiple_of(base + FRONT - d.block, 8), d.tiles), :]
    zp = pad[pl.ds(pl.multiple_of(base + FRONT + d.block, 8), d.tiles), :]
    g = f // d.per_group
    halo = yq[0][:, g * LANES : (g + 1) * LANES]
    if d.y_sends == 2:
        halo = halo + yq[1][:, g * LANES : (g + 1) * LANES]
    halo = pltpu.roll(halo, LANES - 1 - lane_of(d, f, z), 1)
    yp = jnp.where(lane == d.columns - 1, halo, pltpu.roll(v, LANES - 1, 1))
    ym = jnp.where(lane == 0, halo, pltpu.roll(v, 1, 1))
    spread = STEP * diff[f]
    wx = (0.5 * STEP) * wind[0, z]
    wy = (0.5 * STEP) * wind[1, z]
    wz = (0.5 * STEP) * wind[2, z]
    new = (1.0 - 6.0 * spread) * v
    new = new + ((spread - wx) * xp + (spread + wx) * xm)
    new = new + ((spread - wy) * yp + (spread + wy) * ym)
    new = new + ((spread - wz) * zp + (spread + wz) * zm)
    return v, new


def speed(u, v, w):
    return jnp.sqrt(u * u + v * v + w * w + 1.0)


def prepare_kernel(d, wall_type, wind, diff, count, slot_of, parent_of, *outs):
    wall_coef, from_left, from_right, masks, send_table, place_table, counts, tally = outs
    me = lax.axis_index("gx")
    first_tile = me * d.tiles
    row = lax.broadcasted_iota(jnp.int32, (d.tiles, LANES), 0)
    strength = jnp.zeros((d.tiles, LANES), F32)
    owner = jnp.full((d.tiles, LANES), -1, jnp.int32)
    for x in range(d.tiles):
        held = jnp.where(slot_of[first_tile + x] >= 0, count[x], 0).astype(F32) * (1.0 / BMAX)
        strength = jnp.where(row == x, held, strength)
        owner = jnp.where(row == x, parent_of[first_tile + x] - me * d.parents, owner)
    kind = wall_type[...]
    value = jnp.zeros((d.tiles, LANES), F32)
    for code, entry in enumerate(TABLE):
        value = jnp.where(kind == code, entry, value)
    wall_coef[...] = value * strength
    for p in range(d.parents + 1):
        masks[p * d.tiles : (p + 1) * d.tiles, :] = jnp.where(owner == p, 1.0, 0.0)
    for z in range(d.levels):
        wx = (0.5 * STEP) * wind[0, z]
        for f in range(FIELDS):
            spread = STEP * diff[f]
            from_left[f * d.levels + z : f * d.levels + z + 1, :] = jnp.full((1, LANES), spread + wx, F32)
            from_right[f * d.levels + z : f * d.levels + z + 1, :] = jnp.full((1, LANES), spread - wx, F32)
    for k in range(d.n_gx):
        tally[k] = 0
    for i in range(d.n_gx * d.capacity):
        send_table[i] = 0
    for x in range(d.tiles):
        slot = slot_of[first_tile + x]

        @pl.when(slot >= 0)
        def _():
            away = lax.bitwise_xor(lax.shift_right_logical(slot, 3), me)
            rank = tally[away]
            send_table[away * d.capacity + rank] = x
            tally[away] = rank + 1

    def source(s, carry):
        away = lax.bitwise_xor(s, me)

        def tile(x, rank):
            slot = slot_of[s * d.tiles + x]
            mine = (slot >= 0) & (lax.shift_right_logical(slot, 3) == me)
            place = jnp.where(mine, slot - me * SLOTS, SLOTS)
            place_table[place] = away * d.capacity + rank
            return rank + mine.astype(jnp.int32)

        lax.fori_loop(0, d.tiles, tile, 0, unroll=True)
        return carry

    lax.fori_loop(0, d.n_gx, source, 0)
    before = jnp.maximum(first_tile - d.tiles, 0)
    for p in range(d.parents):
        total = jnp.int32(0)
        for x in range(d.tiles):
            total = total + (parent_of[first_tile + x] == me * d.parents + p).astype(jnp.int32)
            if p == 0:
                earlier = parent_of[before + x] == me * d.parents
                total = total + ((me > 0) & earlier).astype(jnp.int32)
        counts[p] = total


def step_one_kernel(d, pad_in, xa, xb, zface, *refs):
    yq = refs[: d.y_sends]
    wall_coef, wind, diff, send_table = refs[d.y_sends : d.y_sends + 4]
    outs = refs[d.y_sends + 4 :]
    pad, new_pad, factor, z_out, head = outs[:5]
    yq_out = outs[5 : 5 + d.y_sends]
    stress = outs[5 + d.y_sends :]
    for f in range(FIELDS):
        set_x_halos(d, pad, f, *x_halos(d, xa, xb, slice(f * d.levels, (f + 1) * d.levels)))
    set_z_halos(d, pad, zface)
    lane = lax.broadcasted_iota(jnp.int32, (d.tiles, LANES), 1)
    zeros = jnp.zeros((d.tiles, LANES), F32)
    coef = wall_coef[...]

    def level(z, carry):
        both = [stencil(d, pad, yq, wind, diff, f, z, lane) for f in range(FIELDS)]
        drag = STEP * (coef * speed(*(both[f][0] for f in range(3))))
        news = [both[f][1] - drag * both[f][0] if f < 3 else both[f][1] for f in range(FIELDS)]
        for f in range(FIELDS):
            new_pad[pl.ds(pl.multiple_of(base_row(d, f, z) + FRONT, 8), d.tiles), :] = news[f]
        factor[pl.ds(pl.multiple_of(z * d.tiles, 8), d.tiles), :] = coef * speed(*news[:3])
        return carry

    lax.fori_loop(0, d.levels, level, 0, unroll=8)
    packed = [zeros] * d.groups
    for f in range(FIELDS):
        packed = add_edges(d, packed, new_pad, f, lane)
    write_y(d, yq_out, packed, lane)
    first, second = x_choices(d)
    targets = [(head, f * d.levels, f, 0) for f in range(FIELDS)]
    targets += [(stress[1], d.part + f * d.levels, f, first) for f in range(FIELDS)]
    targets += [(stress[3], d.part + i * d.levels, d.late + i, second) for i in range(d.early)]
    for out, start, f, tile in targets:
        out[start : start + d.levels, :] = new_pad[
            pl.ds(base_row(d, f, 0) + FRONT + tile, d.levels, stride=d.block), :
        ]
    z_level = jnp.where(lax.axis_index("gz") == 0, d.levels - 1, 0)
    for f in range(FIELDS):
        z_out[f * d.tiles : (f + 1) * d.tiles, :] = new_pad[
            pl.ds(pl.multiple_of(base_row(d, f, z_level) + FRONT, 8), d.tiles), :
        ]
    for k in range(d.n_gx):
        for c in range(d.capacity):
            tile = send_table[k * d.capacity + c]
            stress[k][c * d.levels : (c + 1) * d.levels, :] = factor[pl.ds(tile, d.levels, stride=d.tiles), :]


def step_two_kernel(d, pad_in, factor, zface, *refs):
    yq = refs[: d.y_sends]
    masks_in, wind, diff = refs[d.y_sends : d.y_sends + 3]
    pad, new_fields, own_sums, sent_sums, sent_b, coarse = refs[-6:]
    zero_x = jnp.zeros((d.levels, LANES), F32)
    for f in range(FIELDS):
        set_x_halos(d, pad, f, zero_x, zero_x)
    set_z_halos(d, pad, zface)
    lane = lax.broadcasted_iota(jnp.int32, (d.tiles, LANES), 1)
    zeros = jnp.zeros((d.tiles, LANES), F32)
    masks = [masks_in[p * d.tiles : (p + 1) * d.tiles, :] for p in range(d.parents + 1)]
    coarse_levels = d.levels // RATIO
    coarse[...] = jnp.zeros_like(coarse)
    rows = d.levels * d.tiles
    per_parent = coarse.shape[0] // (d.parents + 1)

    def coarse_level(k, carry):
        def level(i, sums):
            z = k * RATIO + i
            drag = STEP * factor[pl.ds(pl.multiple_of(z * d.tiles, 8), d.tiles), :]
            added = []
            for f in range(FIELDS):
                v, new = stencil(d, pad, yq, wind, diff, f, z, lane)
                if f < 3:
                    new = new - drag * v
                new_fields[pl.ds(pl.multiple_of(f * rows + z * d.tiles, 8), d.tiles), :] = new
                added.append(sums[f] + new)
            return tuple(added)

        sums = lax.fori_loop(0, RATIO, level, (zeros,) * FIELDS, unroll=8)
        for p in range(d.parents + 1):
            for f in range(FIELDS):
                line = jnp.sum(sums[f] * masks[p], axis=0, keepdims=True)
                coarse[pl.ds(p * per_parent + f * coarse_levels + k, 1), :] = line
        return carry

    lax.fori_loop(0, coarse_levels, coarse_level, 0)
    own_sums[...] = coarse[: d.parents * per_parent, :]
    sent_sums[...] = coarse[d.parents * per_parent :, :]
    second = x_choices(d)[1]
    for f in range(d.late):
        sent_b[f * d.levels : (f + 1) * d.levels, :] = pad[
            pl.ds(base_row(d, f, 0) + FRONT + second, d.levels, stride=d.block), :
        ]
    sent_b[d.late * d.levels :, :] = coarse[d.parents * per_parent :, :]


def finish_kernel(d, from_left, from_right, state_in, head, coarse, *refs):
    got_a, got_b, parent_of, place_table, counts = refs[:5]
    stress, refs = refs[5 : 5 + d.n_gx], refs[5:]
    state, new_fields, wall_stress, parent_mean, terms, gathered, placed, sems = refs[d.n_gx :]
    me = lax.axis_index("gx")
    even = lax.rem(me, 2) == 0
    rows = d.levels * d.tiles
    coarse_levels = d.levels // RATIO
    per_parent = coarse.shape[0] // d.parents
    copies = []
    for f in range(FIELDS):
        cut = slice(f * d.levels, (f + 1) * d.levels)
        a = stress[1][d.part + f * d.levels : d.part + (f + 1) * d.levels, :]
        if f < d.late:
            b = got_b[cut, :]
        else:
            b = stress[3][d.part + (f - d.late) * d.levels : d.part + (f - d.late + 1) * d.levels, :]
        left, right = left_right(d, a, b)
        left, right = from_left[cut, :] * left, from_right[cut, :] * right
        ahead = from_right[cut, :] * head[cut, :]
        for tile, added in ((0, left), (d.tiles - 1, right)):
            place = pl.ds(f * rows + tile, d.levels, stride=d.tiles)
            state[place, :] = state[place, :] + added
        copies.append(
            pltpu.make_async_copy(
                state.at[pl.ds(f * rows, rows), :], new_fields.at[pl.ds(f * rows, rows), :], sems.at[f]
            )
        )
        copies[-1].start()
        for i, term in enumerate((left, right, ahead)):
            terms[i * per_parent + f * coarse_levels : i * per_parent + (f + 1) * coarse_levels, :] = jnp.sum(
                term.reshape(coarse_levels, RATIO, LANES), axis=1
            )
    part = d.part
    for k in range(d.n_gx):
        gathered[k * part : (k + 1) * part, :] = stress[k][:part, :]
    for s in range(SLOTS):
        start = pl.multiple_of(place_table[s] * d.levels, 8)
        placed[pl.ds(s, d.levels, stride=SLOTS), :] = gathered[pl.ds(start, d.levels), :]
    copies.append(pltpu.make_async_copy(placed.at[pl.ds(0, d.levels * SLOTS), :], wall_stress, sems.at[FIELDS]))
    copies[-1].start()
    filled = FIELDS * coarse_levels
    if filled < per_parent:
        for i in range(3):
            terms[i * per_parent + filled : (i + 1) * per_parent, :] = jnp.zeros((per_parent - filled, LANES), F32)
    got = jnp.where(even, got_b[d.late * d.levels :, :], got_a[...])
    first_tile = me * d.tiles
    first_parent = parent_of[first_tile] - me * d.parents
    last_parent = parent_of[first_tile + d.tiles - 1] - me * d.parents
    before = jnp.maximum(first_tile - 1, 0)
    ahead_counts = (me > 0) & (parent_of[before] == me * d.parents)
    pick_row = lax.broadcasted_iota(jnp.int32, (LANES, LANES), 0)
    pick_lane = lax.broadcasted_iota(jnp.int32, (LANES, LANES), 1)
    pick = jnp.where(pick_row // RATIO == pick_lane, 1.0, 0.0)
    for p in range(d.parents):
        total = coarse[p * per_parent : (p + 1) * per_parent, :]
        total = total + jnp.where(first_parent == p, terms[:per_parent, :], 0.0)
        total = total + jnp.where(last_parent == p, terms[per_parent : 2 * per_parent, :], 0.0)
        if p == 0:
            total = total + jnp.where(me == 0, 0.0, got)
            total = total + jnp.where(ahead_counts, terms[2 * per_parent :, :], 0.0)
        total = jnp.dot(total, pick, precision=lax.Precision.HIGHEST, preferred_element_type=F32)
        mean = total / (jnp.full(total.shape, counts[p], jnp.int32).astype(F32) * (RATIO * RATIO))
        for f in range(FIELDS):
            parent_mean[p, f] = mean[f * coarse_levels : (f + 1) * coarse_levels, : d.columns // RATIO]
    for copy in copies:
        copy.wait()


def swapped(block, axis):
    return lax.ppermute(block, axis, [(i, i ^ 1) for i in range(lax.axis_size(axis))])


def swapped_between(block, axis, inner):
    n = lax.axis_size(axis)
    route = []
    for i in range(n):
        for k in range(2):
            other = (i, 1 - k) if i in (0, n - 1) else (i + 1 if i % 2 else i - 1, k)
            route.append((2 * i + k, 2 * other[0] + other[1]))
    return lax.ppermute(block, (axis, inner), route)


def crossed(block, axis, distance):
    return lax.ppermute(block, axis, [(i, i ^ distance) for i in range(lax.axis_size(axis))])


def x_swapped(xa, xb):
    return [in_vmem(swapped(xa, "gx")), in_vmem(swapped_between(xb, "gx", "gz"))]


def zy_swapped(d, zface, yq):
    if d.y_sends == 1:
        yq = [swapped(yq[0], "gy")]
    else:
        n = d.n_gy
        yq = [
            lax.ppermute(yq[0], "gy", [(i, i + 1) for i in range(n - 1)]),
            lax.ppermute(yq[1], "gy", [(i + 1, i) for i in range(n - 1)]),
        ]
    return [in_vmem(a) for a in (swapped(zface, "gz"), *yq)]


def body(fields, parent_wind, diffusivity, wall_type, building_count, slot_of, parent_of):
    _, levels, tiles, columns = fields.shape
    d = Dims(levels, tiles, columns, slot_of.shape[0], lax.axis_size("gx"), lax.axis_size("gy"))
    assert columns == LANES and lax.axis_size("gz") == 2 and d.n_gx & (d.n_gx - 1) == 0
    params = pltpu.CompilerParams(vmem_limit_bytes=24 << 20)
    small = [in_hbm(a) for a in (wall_type, parent_wind, diffusivity, building_count, slot_of, parent_of)]
    rows = FIELDS * levels * tiles
    pad_t = pltpu.VMEM((d.pad_rows, LANES), F32)
    x_t = pltpu.VMEM((FIELDS * levels, LANES), F32)
    z_t = pltpu.VMEM((FIELDS * tiles, LANES), F32)
    y_ts = [pltpu.VMEM((tiles, d.groups * LANES), F32)] * d.y_sends

    n_small = len(small)
    *small, pad, xa, xb, zface = (packed := pl.pallas_call(
        functools.partial(pack_kernel, d),
        out_shape=[pltpu.SMEM(a.shape, a.dtype) if a.shape != wall_type.shape else pltpu.VMEM(a.shape, a.dtype) for a in small]
        + [pad_t, x_t, x_t, z_t, *y_ts],
        in_specs=[pl.BlockSpec(memory_space=pltpu.HBM)] * (1 + n_small),
        out_specs=[VM] + [SM] * (n_small - 1) + [VM] * (4 + d.y_sends),
        scratch_shapes=[pltpu.SemaphoreType.DMA((FIELDS + n_small,))],
        compiler_params=params,
        name="pack",
    )(in_hbm(fields), *small))[: n_small + 4]
    yq = packed[n_small + 4 :]
    faces = x_swapped(xa, xb) + zy_swapped(d, zface, yq)
    hbm = pl.BlockSpec(memory_space=pltpu.HBM)

    def ints(n):
        return pltpu.SMEM((n,), jnp.int32)

    wall_coef, from_left, from_right, masks, send_table, place_table, counts = pl.pallas_call(
        functools.partial(prepare_kernel, d),
        out_shape=[pltpu.VMEM((tiles, LANES), F32), x_t, x_t, pltpu.VMEM(((d.parents + 1) * tiles, LANES), F32)]
        + [ints(d.n_gx * d.capacity), ints(SLOTS + 1), ints(d.parents)],
        in_specs=[VM] + [SM] * 5,
        out_specs=[VM] * 4 + [SM] * 3,
        scratch_shapes=[ints(d.n_gx)],
        compiler_params=params,
        name="prepare",
    )(in_vmem(small[0]), *small[1:])

    _, new_pad, factor, zface, head, *rest = pl.pallas_call(
        functools.partial(step_one_kernel, d),
        out_shape=[pad_t, pad_t, pltpu.VMEM(((levels + 1) * tiles, LANES), F32), z_t, x_t, *y_ts]
        + [pltpu.VMEM((d.part + d.riders(k), LANES), F32) for k in range(d.n_gx)],
        in_specs=[VM] * (5 + d.y_sends) + [SM] * 3,
        out_specs=[VM] * (5 + d.y_sends + d.n_gx),
        input_output_aliases={0: 0},
        compiler_params=params,
        name="step_one",
    )(in_vmem(pad), *faces, in_vmem(wall_coef), small[1], small[2], send_table)
    yq, stress = rest[: d.y_sends], rest[d.y_sends :]
    faces = zy_swapped(d, zface, yq)
    stress = [stress[0]] + [in_vmem(crossed(stress[k], "gx", k)) for k in range(1, d.n_gx)]

    per_parent = -(-FIELDS * (levels // RATIO) // 8) * 8
    state_t = pltpu.VMEM((rows + tiles, LANES), F32)
    _, state, own_sums, sent_sums, sent_b = pl.pallas_call(
        functools.partial(step_two_kernel, d),
        out_shape=[
            pad_t,
            state_t,
            pltpu.VMEM((d.parents * per_parent, LANES), F32),
            pltpu.VMEM((per_parent, LANES), F32),
            pltpu.VMEM((d.late * levels + per_parent, LANES), F32),
        ],
        in_specs=[VM] * (4 + d.y_sends) + [SM] * 2,
        out_specs=[VM] * 5,
        scratch_shapes=[pltpu.VMEM(((d.parents + 1) * per_parent, LANES), F32)],
        input_output_aliases={0: 0},
        compiler_params=params,
        name="step_two",
    )(in_vmem(new_pad), in_vmem(factor), *faces, in_vmem(masks), small[1], small[2])
    got = x_swapped(sent_sums, sent_b)

    _, new_fields, wall_stress, parent_mean = pl.pallas_call(
        functools.partial(finish_kernel, d),
        out_shape=[
            state_t,
            jax.ShapeDtypeStruct((rows, LANES), F32),
            jax.ShapeDtypeStruct((levels * SLOTS, LANES), F32),
            jax.ShapeDtypeStruct((d.parents, FIELDS, levels // RATIO, columns // RATIO), F32),
        ],
        in_specs=[VM] * 7 + [SM] * 3 + [VM] * d.n_gx,
        out_specs=[VM, hbm, hbm, VM],
        scratch_shapes=[
            pltpu.VMEM((3 * per_parent, LANES), F32),
            pltpu.VMEM((d.n_gx * d.capacity * levels, LANES), F32),
            pltpu.VMEM(((levels + 1) * SLOTS, LANES), F32),
            pltpu.SemaphoreType.DMA((FIELDS + 1,)),
        ],
        input_output_aliases={2: 0},
        compiler_params=params,
        name="finish",
    )(
        *[in_vmem(a) for a in (from_left, from_right, state, head, own_sums)],
        *got,
        small[5],
        place_table,
        counts,
        *[in_vmem(stress[0])],
        *stress[1:],
    )
    return (
        new_fields.reshape(fields.shape),
        wall_stress.reshape(levels, SLOTS, columns),
        parent_mean,
    )


def solution(mesh):
    in_specs = (
        P(None, "gz", ("groups", "gx"), "gy"),
        P(None, ("groups", "gz")),
        P(),
        P(("groups", "gx"), "gy"),
        P(("groups", "gx")),
        P("groups"),
        P("groups"),
    )
    out_specs = (
        P(None, "gz", ("groups", "gx"), "gy"),
        P("gz", ("groups", "gx"), "gy"),
        P(("groups", "gx"), None, "gz", "gy"),
    )
    return jax.shard_map(body, mesh=mesh, in_specs=in_specs, out_specs=out_specs, check_vma=False)
```

```python
import functools

import jax
import jax.numpy as jnp
from jax import lax
from jax.experimental import pallas as pl
from jax.experimental.pallas import tpu as pltpu
from jax.sharding import PartitionSpec as P

FIELDS = 5
RATIO = 8
BMAX = 32
SLOTS = 8

TABLE = (0.4, 0.8, 1.3, 2.0)
STEP = 0.25

FRONT = 8
LANES = 128
F32 = jnp.float32

VM = pl.BlockSpec(memory_space=pltpu.VMEM)
SM = pl.BlockSpec(memory_space=pltpu.SMEM)


def in_hbm(array):
    return pltpu.with_memory_space_constraint(array, pltpu.HBM)


def in_vmem(array):
    return pltpu.with_memory_space_constraint(array, pltpu.VMEM)


class Dims:
    def __init__(self, levels, tiles, columns, all_tiles, n_gx, n_gy):
        self.levels, self.tiles, self.columns = levels, tiles, columns
        self.all_tiles, self.n_gx, self.n_gy = all_tiles, n_gx, n_gy
        self.block = FRONT + tiles
        self.pad_rows = FIELDS * (levels + 2) * self.block + 8
        self.capacity = (tiles + n_gx - 1) // n_gx
        self.per_group = LANES // (2 * levels)
        self.groups = -(-FIELDS // self.per_group)
        self.parents = tiles // RATIO
        self.y_sends = 1 if n_gy == 2 else 2
        self.part = self.capacity * levels
        self.early = 2 if n_gx == 4 else 0
        self.late = FIELDS - self.early

    def riders(self, k):
        return self.levels * (FIELDS if k == 1 else self.early if k == 3 else 0)


def base_row(d, f, z):
    return (f * (d.levels + 2) + z + 1) * d.block


def lane_of(d, f, z):
    return 2 * ((f % d.per_group) * d.levels + z)


def x_choices(d):
    even = lax.rem(lax.axis_index("gx"), 2) == 0
    return [jnp.where(even, d.tiles - 1, 0), jnp.where(even, 0, d.tiles - 1)]


def add_edges(d, packed, pad, f, lane):
    pair = lax.rem(lax.shift_right_logical(lane + 1, 1), LANES // 2)
    g = f // d.per_group
    for z in range(d.levels):
        cells = pad[pl.ds(base_row(d, f, z) + FRONT, d.tiles), :]
        place = lane_of(d, f, z)
        moved = pltpu.roll(cells, place, 1) if place else cells
        packed[g] = jnp.where(pair == place // 2, moved, packed[g])
    return packed


def write_y(d, outs, packed, lane):
    odd = lax.rem(lane, 2) == 1
    first = lax.axis_index("gy") == 0
    for g in range(d.groups):
        tail = pltpu.roll(jnp.where(odd, packed[g], 0.0), 2, 1)
        head = jnp.where(odd, 0.0, packed[g])
        messages = [jnp.where(first, tail, head)] if d.y_sends == 1 else [tail, head]
        for out, message in zip(outs, messages):
            out[:, g * LANES : (g + 1) * LANES] = message


def pack_kernel(d, fields, *refs):
    n_small = len(refs[: (len(refs) - 5 - d.y_sends) // 2])
    small, refs = refs[:n_small], refs[n_small:]
    small_out, (pad, xa, xb, zface), yq = refs[:n_small], refs[n_small : n_small + 4], refs[n_small + 4 : -1]
    sems = refs[-1]
    lane = lax.broadcasted_iota(jnp.int32, (d.tiles, LANES), 1)
    copies = []
    for f in range(FIELDS):
        blocks = pad.at[pl.ds(base_row(d, f, 0), d.levels * d.block), :].reshape(d.levels, d.block, LANES)
        copies.append(pltpu.make_async_copy(fields.at[f], blocks.at[:, pl.ds(FRONT, d.tiles), :], sems.at[f]))
    moves = [
        pltpu.make_async_copy(source, target, sems.at[FIELDS + i])
        for i, (source, target) in enumerate(zip(small, small_out))
    ]
    for copy in copies + moves:
        copy.start()
    z_out = jnp.where(lax.axis_index("gz") == 0, d.levels - 1, 0)
    packed = [jnp.zeros((d.tiles, LANES), F32)] * d.groups
    for f in range(FIELDS):
        copies[f].wait()
        packed = add_edges(d, packed, pad, f, lane)
        for out, tile in zip((xa, xb), x_choices(d)):
            out[f * d.levels : (f + 1) * d.levels, :] = pad[
                pl.ds(base_row(d, f, 0) + FRONT + tile, d.levels, stride=d.block), :
            ]
        zface[f * d.tiles : (f + 1) * d.tiles, :] = pad[
            pl.ds(pl.multiple_of(base_row(d, f, z_out) + FRONT, 8), d.tiles), :
        ]
    write_y(d, yq, packed, lane)
    for copy in moves:
        copy.wait()


def x_halos(d, xa, xb, rows):
    a, b = xa[rows, :], xb[rows, :]
    return left_right(d, a, b)


def left_right(d, a, b):
    me = lax.axis_index("gx")
    even = lax.rem(me, 2) == 0
    left = jnp.where(me == 0, 0.0, jnp.where(even, b, a))
    right = jnp.where(me == d.n_gx - 1, 0.0, jnp.where(even, a, b))
    return left, right


def set_x_halos(d, pad, f, left, right):
    pad[pl.ds(base_row(d, f, 0) + FRONT - 1, d.levels, stride=d.block), :] = left
    pad[pl.ds(base_row(d, f, 0) + d.block, d.levels, stride=d.block), :] = right


def set_z_halos(d, pad, zface):
    low = lax.axis_index("gz") == 0
    for f in range(FIELDS):
        face = zface[f * d.tiles : (f + 1) * d.tiles, :]
        pad[pl.ds(base_row(d, f, -1) + FRONT, d.tiles), :] = jnp.where(low, 0.0, face)
        pad[pl.ds(base_row(d, f, d.levels) + FRONT, d.tiles), :] = jnp.where(low, face, 0.0)


def stencil(d, pad, yq, wind, diff, f, z, lane):
    base = base_row(d, f, z)
    v = pad[pl.ds(pl.multiple_of(base + FRONT, 8), d.tiles), :]
    xm = pad[pl.ds(base + FRONT - 1, d.tiles), :]
    xp = pad[pl.ds(base + FRONT + 1, d.tiles), :]
    zm = pad[pl.ds(pl.multiple_of(base + FRONT - d.block, 8), d.tiles), :]
    zp = pad[pl.ds(pl.multiple_of(base + FRONT + d.block, 8), d.tiles), :]
    g = f // d.per_group
    halo = yq[0][:, g * LANES : (g + 1) * LANES]
    if d.y_sends == 2:
        halo = halo + yq[1][:, g * LANES : (g + 1) * LANES]
    halo = pltpu.roll(halo, LANES - 1 - lane_of(d, f, z), 1)
    yp = jnp.where(lane == d.columns - 1, halo, pltpu.roll(v, LANES - 1, 1))
    ym = jnp.where(lane == 0, halo, pltpu.roll(v, 1, 1))
    spread = STEP * diff[f]
    wx = (0.5 * STEP) * wind[0, z]
    wy = (0.5 * STEP) * wind[1, z]
    wz = (0.5 * STEP) * wind[2, z]
    new = (1.0 - 6.0 * spread) * v
    new = new + ((spread - wx) * xp + (spread + wx) * xm)
    new = new + ((spread - wy) * yp + (spread + wy) * ym)
    new = new + ((spread - wz) * zp + (spread + wz) * zm)
    return v, new


def speed(u, v, w):
    return jnp.sqrt(u * u + v * v + w * w + 1.0)


def prepare_kernel(d, pad, wall_type, wind, diff, count, slot_of, parent_of, *outs):
    wall_coef, drag, from_left, from_right, masks, send_table, place_table, counts, tally = outs
    me = lax.axis_index("gx")
    first_tile = me * d.tiles
    row = lax.broadcasted_iota(jnp.int32, (d.tiles, LANES), 0)
    strength = jnp.zeros((d.tiles, LANES), F32)
    owner = jnp.full((d.tiles, LANES), -1, jnp.int32)
    for x in range(d.tiles):
        held = jnp.where(slot_of[first_tile + x] >= 0, count[x], 0).astype(F32) * (1.0 / BMAX)
        strength = jnp.where(row == x, held, strength)
        owner = jnp.where(row == x, parent_of[first_tile + x] - me * d.parents, owner)
    kind = wall_type[...]
    value = jnp.zeros((d.tiles, LANES), F32)
    for code, entry in enumerate(TABLE):
        value = jnp.where(kind == code, entry, value)
    coef = value * strength
    wall_coef[...] = coef

    def level(z, carry):
        at = [pl.ds(pl.multiple_of(base_row(d, f, z) + FRONT, 8), d.tiles) for f in range(3)]
        drag[pl.ds(pl.multiple_of(z * d.tiles, 8), d.tiles), :] = STEP * (coef * speed(*(pad[a, :] for a in at)))
        return carry

    lax.fori_loop(0, d.levels, level, 0, unroll=8)
    for p in range(d.parents + 1):
        masks[p * d.tiles : (p + 1) * d.tiles, :] = jnp.where(owner == p, 1.0, 0.0)
    for z in range(d.levels):
        wx = (0.5 * STEP) * wind[0, z]
        for f in range(FIELDS):
            spread = STEP * diff[f]
            from_left[f * d.levels + z : f * d.levels + z + 1, :] = jnp.full((1, LANES), spread + wx, F32)
            from_right[f * d.levels + z : f * d.levels + z + 1, :] = jnp.full((1, LANES), spread - wx, F32)
    for k in range(d.n_gx):
        tally[k] = 0
    for i in range(d.n_gx * d.capacity):
        send_table[i] = 0
    for x in range(d.tiles):
        slot = slot_of[first_tile + x]

        @pl.when(slot >= 0)
        def _():
            away = lax.bitwise_xor(lax.shift_right_logical(slot, 3), me)
            rank = tally[away]
            send_table[away * d.capacity + rank] = x
            tally[away] = rank + 1

    def source(s, carry):
        away = lax.bitwise_xor(s, me)

        def tile(x, rank):
            slot = slot_of[s * d.tiles + x]
            mine = (slot >= 0) & (lax.shift_right_logical(slot, 3) == me)
            place = jnp.where(mine, slot - me * SLOTS, SLOTS)
            place_table[place] = away * d.capacity + rank
            return rank + mine.astype(jnp.int32)

        lax.fori_loop(0, d.tiles, tile, 0, unroll=True)
        return carry

    lax.fori_loop(0, d.n_gx, source, 0)
    before = jnp.maximum(first_tile - d.tiles, 0)
    for p in range(d.parents):
        total = jnp.int32(0)
        for x in range(d.tiles):
            total = total + (parent_of[first_tile + x] == me * d.parents + p).astype(jnp.int32)
            if p == 0:
                earlier = parent_of[before + x] == me * d.parents
                total = total + ((me > 0) & earlier).astype(jnp.int32)
        counts[p] = total


def step_one_kernel(d, pad_in, xa, xb, zface, *refs):
    yq = refs[: d.y_sends]
    wall_coef, first_drag, wind, diff, send_table = refs[d.y_sends : d.y_sends + 5]
    outs = refs[d.y_sends + 5 :]
    pad, new_pad, factor, z_out, head = outs[:5]
    yq_out = outs[5 : 5 + d.y_sends]
    stress = outs[5 + d.y_sends :]
    for f in range(FIELDS):
        set_x_halos(d, pad, f, *x_halos(d, xa, xb, slice(f * d.levels, (f + 1) * d.levels)))
    set_z_halos(d, pad, zface)
    lane = lax.broadcasted_iota(jnp.int32, (d.tiles, LANES), 1)
    zeros = jnp.zeros((d.tiles, LANES), F32)
    coef = wall_coef[...]

    def level(z, carry):
        both = [stencil(d, pad, yq, wind, diff, f, z, lane) for f in range(FIELDS)]
        drag = first_drag[pl.ds(pl.multiple_of(z * d.tiles, 8), d.tiles), :]
        news = [both[f][1] - drag * both[f][0] if f < 3 else both[f][1] for f in range(FIELDS)]
        for f in range(FIELDS):
            new_pad[pl.ds(pl.multiple_of(base_row(d, f, z) + FRONT, 8), d.tiles), :] = news[f]
        factor[pl.ds(pl.multiple_of(z * d.tiles, 8), d.tiles), :] = coef * speed(*news[:3])
        return carry

    lax.fori_loop(0, d.levels, level, 0, unroll=8)
    packed = [zeros] * d.groups
    for f in range(FIELDS):
        packed = add_edges(d, packed, new_pad, f, lane)
    write_y(d, yq_out, packed, lane)
    first, second = x_choices(d)
    targets = [(head, f * d.levels, f, 0) for f in range(FIELDS)]
    targets += [(stress[1], d.part + f * d.levels, f, first) for f in range(FIELDS)]
    targets += [(stress[3], d.part + i * d.levels, d.late + i, second) for i in range(d.early)]
    for out, start, f, tile in targets:
        out[start : start + d.levels, :] = new_pad[
            pl.ds(base_row(d, f, 0) + FRONT + tile, d.levels, stride=d.block), :
        ]
    z_level = jnp.where(lax.axis_index("gz") == 0, d.levels - 1, 0)
    for f in range(FIELDS):
        z_out[f * d.tiles : (f + 1) * d.tiles, :] = new_pad[
            pl.ds(pl.multiple_of(base_row(d, f, z_level) + FRONT, 8), d.tiles), :
        ]
    for k in range(d.n_gx):
        for c in range(d.capacity):
            tile = send_table[k * d.capacity + c]
            stress[k][c * d.levels : (c + 1) * d.levels, :] = factor[pl.ds(tile, d.levels, stride=d.tiles), :]


def step_two_kernel(d, pad_in, factor, zface, *refs):
    yq = refs[: d.y_sends]
    masks_in, wind, diff = refs[d.y_sends : d.y_sends + 3]
    pad, new_fields, own_sums, sent_sums, sent_b, coarse = refs[-6:]
    zero_x = jnp.zeros((d.levels, LANES), F32)
    for f in range(FIELDS):
        set_x_halos(d, pad, f, zero_x, zero_x)
    set_z_halos(d, pad, zface)
    lane = lax.broadcasted_iota(jnp.int32, (d.tiles, LANES), 1)
    zeros = jnp.zeros((d.tiles, LANES), F32)
    masks = [masks_in[p * d.tiles : (p + 1) * d.tiles, :] for p in range(d.parents + 1)]
    coarse_levels = d.levels // RATIO
    coarse[...] = jnp.zeros_like(coarse)
    rows = d.levels * d.tiles
    per_parent = coarse.shape[0] // (d.parents + 1)

    def coarse_level(k, carry):
        def level(i, sums):
            z = k * RATIO + i
            drag = STEP * factor[pl.ds(pl.multiple_of(z * d.tiles, 8), d.tiles), :]
            added = []
            for f in range(FIELDS):
                v, new = stencil(d, pad, yq, wind, diff, f, z, lane)
                if f < 3:
                    new = new - drag * v
                new_fields[pl.ds(pl.multiple_of(f * rows + z * d.tiles, 8), d.tiles), :] = new
                added.append(sums[f] + new)
            return tuple(added)

        sums = lax.fori_loop(0, RATIO, level, (zeros,) * FIELDS, unroll=8)
        for p in range(d.parents + 1):
            for f in range(FIELDS):
                line = jnp.sum(sums[f] * masks[p], axis=0, keepdims=True)
                coarse[pl.ds(p * per_parent + f * coarse_levels + k, 1), :] = line
        return carry

    lax.fori_loop(0, coarse_levels, coarse_level, 0)
    own_sums[...] = coarse[: d.parents * per_parent, :]
    sent_sums[...] = coarse[d.parents * per_parent :, :]
    second = x_choices(d)[1]
    for f in range(d.late):
        sent_b[f * d.levels : (f + 1) * d.levels, :] = pad[
            pl.ds(base_row(d, f, 0) + FRONT + second, d.levels, stride=d.block), :
        ]
    sent_b[d.late * d.levels :, :] = coarse[d.parents * per_parent :, :]


def flush_kernel(d, state, new_fields, sem):
    copy = pltpu.make_async_copy(state.at[pl.ds(0, new_fields.shape[0]), :], new_fields, sem.at[0])
    copy.start()
    copy.wait()


def finish_kernel(d, from_left, from_right, flushed, state_in, head, coarse, *refs):
    got_a, got_b, parent_of, place_table, counts = refs[:5]
    stress, refs = refs[5 : 5 + d.n_gx], refs[5:]
    new_fields, state, wall_stress, parent_mean, terms, gathered, placed, mean_out, sems = refs[d.n_gx :]
    me = lax.axis_index("gx")
    even = lax.rem(me, 2) == 0
    rows = d.levels * d.tiles
    coarse_levels = d.levels // RATIO
    per_parent = coarse.shape[0] // d.parents
    copies = []
    part = d.part
    for k in range(d.n_gx):
        gathered[k * part : (k + 1) * part, :] = stress[k][:part, :]
    for s in range(SLOTS):
        start = pl.multiple_of(place_table[s] * d.levels, 8)
        placed[pl.ds(s, d.levels, stride=SLOTS), :] = gathered[pl.ds(start, d.levels), :]
    copies.append(pltpu.make_async_copy(placed.at[pl.ds(0, d.levels * SLOTS), :], wall_stress, sems.at[2 * FIELDS]))
    copies[-1].start()
    for f in range(FIELDS):
        cut = slice(f * d.levels, (f + 1) * d.levels)
        a = stress[1][d.part + f * d.levels : d.part + (f + 1) * d.levels, :]
        if f < d.late:
            b = got_b[cut, :]
        else:
            b = stress[3][d.part + (f - d.late) * d.levels : d.part + (f - d.late + 1) * d.levels, :]
        left, right = left_right(d, a, b)
        left, right = from_left[cut, :] * left, from_right[cut, :] * right
        ahead = from_right[cut, :] * head[cut, :]
        for tile, added in ((0, left), (d.tiles - 1, right)):
            place = pl.ds(f * rows + tile, d.levels, stride=d.tiles)
            state[place, :] = state[place, :] + added
        for i, tile in enumerate((0, d.tiles - 1)):
            ends = [
                array.at[pl.ds(f * rows, rows), :].reshape(d.levels, d.tiles, LANES).at[:, pl.ds(tile, 1), :]
                for array in (state, new_fields)
            ]
            copies.append(pltpu.make_async_copy(*ends, sems.at[2 * f + i]))
            copies[-1].start()
        for i, term in enumerate((left, right, ahead)):
            terms[i * per_parent + f * coarse_levels : i * per_parent + (f + 1) * coarse_levels, :] = jnp.sum(
                term.reshape(coarse_levels, RATIO, LANES), axis=1
            )
    filled = FIELDS * coarse_levels
    if filled < per_parent:
        for i in range(3):
            terms[i * per_parent + filled : (i + 1) * per_parent, :] = jnp.zeros((per_parent - filled, LANES), F32)
    got = jnp.where(even, got_b[d.late * d.levels :, :], got_a[...])
    first_tile = me * d.tiles
    first_parent = parent_of[first_tile] - me * d.parents
    last_parent = parent_of[first_tile + d.tiles - 1] - me * d.parents
    before = jnp.maximum(first_tile - 1, 0)
    ahead_counts = (me > 0) & (parent_of[before] == me * d.parents)
    pick_row = lax.broadcasted_iota(jnp.int32, (LANES, LANES), 0)
    pick_lane = lax.broadcasted_iota(jnp.int32, (LANES, LANES), 1)
    pick = jnp.where(pick_row // RATIO == pick_lane, 1.0, 0.0)
    for p in range(d.parents):
        total = coarse[p * per_parent : (p + 1) * per_parent, :]
        total = total + jnp.where(first_parent == p, terms[:per_parent, :], 0.0)
        total = total + jnp.where(last_parent == p, terms[per_parent : 2 * per_parent, :], 0.0)
        if p == 0:
            total = total + jnp.where(me == 0, 0.0, got)
            total = total + jnp.where(ahead_counts, terms[2 * per_parent :, :], 0.0)
        total = jnp.dot(total, pick, precision=lax.Precision.HIGHEST, preferred_element_type=F32)
        mean = total / (jnp.full(total.shape, counts[p], jnp.int32).astype(F32) * (RATIO * RATIO))
        for f in range(FIELDS):
            mean_out[p, f] = mean[f * coarse_levels : (f + 1) * coarse_levels, : d.columns // RATIO]
    copies.append(pltpu.make_async_copy(mean_out, parent_mean, sems.at[2 * FIELDS + 1]))
    copies[-1].start()
    for copy in copies:
        copy.wait()


def swapped(block, axis):
    return lax.ppermute(block, axis, [(i, i ^ 1) for i in range(lax.axis_size(axis))])


def swapped_between(block, axis, inner):
    n = lax.axis_size(axis)
    route = []
    for i in range(n):
        for k in range(2):
            other = (i, 1 - k) if i in (0, n - 1) else (i + 1 if i % 2 else i - 1, k)
            route.append((2 * i + k, 2 * other[0] + other[1]))
    return lax.ppermute(block, (axis, inner), route)


def crossed(block, axis, distance):
    return lax.ppermute(block, axis, [(i, i ^ distance) for i in range(lax.axis_size(axis))])


def x_swapped(xa, xb):
    return [in_vmem(swapped(xa, "gx")), in_vmem(swapped_between(xb, "gx", "gz"))]


def zy_swapped(d, zface, yq):
    if d.y_sends == 1:
        yq = [swapped(yq[0], "gy")]
    else:
        n = d.n_gy
        yq = [
            lax.ppermute(yq[0], "gy", [(i, i + 1) for i in range(n - 1)]),
            lax.ppermute(yq[1], "gy", [(i + 1, i) for i in range(n - 1)]),
        ]
    return [in_vmem(a) for a in (swapped(zface, "gz"), *yq)]


def body(fields, parent_wind, diffusivity, wall_type, building_count, slot_of, parent_of):
    _, levels, tiles, columns = fields.shape
    d = Dims(levels, tiles, columns, slot_of.shape[0], lax.axis_size("gx"), lax.axis_size("gy"))
    assert columns == LANES and lax.axis_size("gz") == 2 and d.n_gx & (d.n_gx - 1) == 0
    params = pltpu.CompilerParams(vmem_limit_bytes=24 << 20)
    small = [in_hbm(a) for a in (wall_type, parent_wind, diffusivity, building_count, slot_of, parent_of)]
    rows = FIELDS * levels * tiles
    pad_t = pltpu.VMEM((d.pad_rows, LANES), F32)
    x_t = pltpu.VMEM((FIELDS * levels, LANES), F32)
    z_t = pltpu.VMEM((FIELDS * tiles, LANES), F32)
    y_ts = [pltpu.VMEM((tiles, d.groups * LANES), F32)] * d.y_sends

    n_small = len(small)
    *small, pad, xa, xb, zface = (packed := pl.pallas_call(
        functools.partial(pack_kernel, d),
        out_shape=[pltpu.SMEM(a.shape, a.dtype) if a.shape != wall_type.shape else pltpu.VMEM(a.shape, a.dtype) for a in small]
        + [pad_t, x_t, x_t, z_t, *y_ts],
        in_specs=[pl.BlockSpec(memory_space=pltpu.HBM)] * (1 + n_small),
        out_specs=[VM] + [SM] * (n_small - 1) + [VM] * (4 + d.y_sends),
        scratch_shapes=[pltpu.SemaphoreType.DMA((FIELDS + n_small,))],
        compiler_params=params,
        name="pack",
    )(in_hbm(fields), *small))[: n_small + 4]
    yq = packed[n_small + 4 :]
    faces = x_swapped(xa, xb) + zy_swapped(d, zface, yq)
    hbm = pl.BlockSpec(memory_space=pltpu.HBM)

    def ints(n):
        return pltpu.SMEM((n,), jnp.int32)

    wall_coef, drag, from_left, from_right, masks, send_table, place_table, counts = pl.pallas_call(
        functools.partial(prepare_kernel, d),
        out_shape=[pltpu.VMEM((tiles, LANES), F32), pltpu.VMEM((levels * tiles, LANES), F32), x_t, x_t]
        + [pltpu.VMEM(((d.parents + 1) * tiles, LANES), F32)]
        + [ints(d.n_gx * d.capacity), ints(SLOTS + 1), ints(d.parents)],
        in_specs=[VM] * 2 + [SM] * 5,
        out_specs=[VM] * 5 + [SM] * 3,
        scratch_shapes=[ints(d.n_gx)],
        compiler_params=params,
        name="prepare",
    )(in_vmem(pad), in_vmem(small[0]), *small[1:])

    _, new_pad, factor, zface, head, *rest = pl.pallas_call(
        functools.partial(step_one_kernel, d),
        out_shape=[pad_t, pad_t, pltpu.VMEM(((levels + 1) * tiles, LANES), F32), z_t, x_t, *y_ts]
        + [pltpu.VMEM((d.part + d.riders(k), LANES), F32) for k in range(d.n_gx)],
        in_specs=[VM] * (6 + d.y_sends) + [SM] * 3,
        out_specs=[VM] * (5 + d.y_sends + d.n_gx),
        input_output_aliases={0: 0},
        compiler_params=params,
        name="step_one",
    )(in_vmem(pad), *faces, in_vmem(wall_coef), in_vmem(drag), small[1], small[2], send_table)
    yq, stress = rest[: d.y_sends], rest[d.y_sends :]
    faces = zy_swapped(d, zface, yq)
    stress = [stress[0]] + [in_vmem(crossed(stress[k], "gx", k)) for k in range(1, d.n_gx)]

    per_parent = -(-FIELDS * (levels // RATIO) // 8) * 8
    state_t = pltpu.VMEM((rows + tiles, LANES), F32)
    _, state, own_sums, sent_sums, sent_b = pl.pallas_call(
        functools.partial(step_two_kernel, d),
        out_shape=[
            pad_t,
            state_t,
            pltpu.VMEM((d.parents * per_parent, LANES), F32),
            pltpu.VMEM((per_parent, LANES), F32),
            pltpu.VMEM((d.late * levels + per_parent, LANES), F32),
        ],
        in_specs=[VM] * (4 + d.y_sends) + [SM] * 2,
        out_specs=[VM] * 5,
        scratch_shapes=[pltpu.VMEM(((d.parents + 1) * per_parent, LANES), F32)],
        input_output_aliases={0: 0},
        compiler_params=params,
        name="step_two",
    )(in_vmem(new_pad), in_vmem(factor), *faces, in_vmem(masks), small[1], small[2])
    got = x_swapped(sent_sums, sent_b)

    flushed = pl.pallas_call(
        functools.partial(flush_kernel, d),
        out_shape=jax.ShapeDtypeStruct((rows, LANES), F32),
        in_specs=[VM],
        out_specs=hbm,
        scratch_shapes=[pltpu.SemaphoreType.DMA((1,))],
        compiler_params=params,
        name="flush",
    )(in_vmem(state))

    new_fields, _, wall_stress, parent_mean = pl.pallas_call(
        functools.partial(finish_kernel, d),
        out_shape=[
            jax.ShapeDtypeStruct((rows, LANES), F32),
            state_t,
            jax.ShapeDtypeStruct((levels * SLOTS, LANES), F32),
            jax.ShapeDtypeStruct((d.parents, FIELDS, levels // RATIO, columns // RATIO), F32),
        ],
        in_specs=[VM] * 2 + [hbm] + [VM] * 5 + [SM] * 3 + [VM] * d.n_gx,
        out_specs=[hbm, VM, hbm, hbm],
        scratch_shapes=[
            pltpu.VMEM((3 * per_parent, LANES), F32),
            pltpu.VMEM((d.n_gx * d.capacity * levels, LANES), F32),
            pltpu.VMEM(((levels + 1) * SLOTS, LANES), F32),
            pltpu.VMEM((d.parents, FIELDS, levels // RATIO, columns // RATIO), F32),
            pltpu.SemaphoreType.DMA((2 * FIELDS + 2,)),
        ],
        input_output_aliases={2: 0, 3: 1},
        compiler_params=params,
        name="finish",
    )(
        in_vmem(from_left),
        in_vmem(from_right),
        flushed,
        *[in_vmem(a) for a in (state, head, own_sums)],
        *got,
        small[5],
        place_table,
        counts,
        *[in_vmem(stress[0])],
        *stress[1:],
    )
    return (
        new_fields.reshape(fields.shape),
        wall_stress.reshape(levels, SLOTS, columns),
        parent_mean,
    )


def solution(mesh):
    in_specs = (
        P(None, "gz", ("groups", "gx"), "gy"),
        P(None, ("groups", "gz")),
        P(),
        P(("groups", "gx"), "gy"),
        P(("groups", "gx")),
        P("groups"),
        P("groups"),
    )
    out_specs = (
        P(None, "gz", ("groups", "gx"), "gy"),
        P("gz", ("groups", "gx"), "gy"),
        P(("groups", "gx"), None, "gz", "gy"),
    )
    return jax.shard_map(body, mesh=mesh, in_specs=in_specs, out_specs=out_specs, check_vma=False)
```

```python
import functools

import jax
import jax.numpy as jnp
from jax import lax
from jax.experimental import pallas as pl
from jax.experimental.pallas import tpu as pltpu
from jax.sharding import PartitionSpec as P

FIELDS = 5
RATIO = 8
BMAX = 32
SLOTS = 8

TABLE = (0.4, 0.8, 1.3, 2.0)
STEP = 0.25

FRONT = 8
LANES = 128
F32 = jnp.float32

VM = pl.BlockSpec(memory_space=pltpu.VMEM)
SM = pl.BlockSpec(memory_space=pltpu.SMEM)


def in_hbm(array):
    return pltpu.with_memory_space_constraint(array, pltpu.HBM)


def in_vmem(array):
    return pltpu.with_memory_space_constraint(array, pltpu.VMEM)


class Dims:
    def __init__(self, levels, tiles, columns, all_tiles, n_gx, n_gy):
        self.levels, self.tiles, self.columns = levels, tiles, columns
        self.all_tiles, self.n_gx, self.n_gy = all_tiles, n_gx, n_gy
        self.block = FRONT + tiles
        self.pad_rows = FIELDS * (levels + 2) * self.block + 8
        self.capacity = (tiles + n_gx - 1) // n_gx
        self.per_group = LANES // (2 * levels)
        self.groups = -(-FIELDS // self.per_group)
        self.parents = tiles // RATIO
        self.y_sends = 1 if n_gy == 2 else 2
        self.part = self.capacity * levels
        self.early = 2 if n_gx == 4 else 0
        self.late = FIELDS - self.early

    def riders(self, k):
        return self.levels * (FIELDS if k == 1 else self.early if k == 3 else 0)


def base_row(d, f, z):
    return (f * (d.levels + 2) + z + 1) * d.block


def lane_of(d, f, z):
    return 2 * ((f % d.per_group) * d.levels + z)


def x_choices(d):
    even = lax.rem(lax.axis_index("gx"), 2) == 0
    return [jnp.where(even, d.tiles - 1, 0), jnp.where(even, 0, d.tiles - 1)]


def add_edges(d, packed, pad, f, lane, raw=None):
    pair = lax.rem(lax.shift_right_logical(lane + 1, 1), LANES // 2)
    g = f // d.per_group
    for z in range(d.levels):
        if raw is None:
            cells = pad[pl.ds(base_row(d, f, z) + FRONT, d.tiles), :]
        else:
            cells = raw[f, z]
            pad[pl.ds(base_row(d, f, z) + FRONT, d.tiles), :] = cells
        place = lane_of(d, f, z)
        moved = pltpu.roll(cells, place, 1) if place else cells
        packed[g] = jnp.where(pair == place // 2, moved, packed[g])
    return packed


def write_y(d, outs, packed, lane):
    odd = lax.rem(lane, 2) == 1
    first = lax.axis_index("gy") == 0
    for g in range(d.groups):
        tail = pltpu.roll(jnp.where(odd, packed[g], 0.0), 2, 1)
        head = jnp.where(odd, 0.0, packed[g])
        messages = [jnp.where(first, tail, head)] if d.y_sends == 1 else [tail, head]
        for out, message in zip(outs, messages):
            out[:, g * LANES : (g + 1) * LANES] = message


def pack_kernel(d, fields, *refs):
    n_small = len(refs[: (len(refs) - 5 - d.y_sends) // 2])
    small, refs = refs[:n_small], refs[n_small:]
    small_out, (pad, xa, xb, zface), yq = refs[:n_small], refs[n_small : n_small + 4], refs[n_small + 4 : -2]
    raw, sems = refs[-2:]
    lane = lax.broadcasted_iota(jnp.int32, (d.tiles, LANES), 1)
    copies = []
    for f in range(FIELDS):
        copies.append(pltpu.make_async_copy(fields.at[f], raw.at[f], sems.at[f]))
    moves = [
        pltpu.make_async_copy(source, target, sems.at[FIELDS + i])
        for i, (source, target) in enumerate(zip(small, small_out))
    ]
    for copy in copies + moves:
        copy.start()
    zero_x = jnp.zeros((d.levels, LANES), F32)
    for f in range(FIELDS):
        set_x_halos(d, pad, f, zero_x, zero_x)
        for z in (-1, d.levels):
            pad[pl.ds(base_row(d, f, z) + FRONT, d.tiles), :] = jnp.zeros((d.tiles, LANES), F32)
    z_out = jnp.where(lax.axis_index("gz") == 0, d.levels - 1, 0)
    packed = [jnp.zeros((d.tiles, LANES), F32)] * d.groups
    for f in range(FIELDS):
        copies[f].wait()
        packed = add_edges(d, packed, pad, f, lane, raw)
        for out, tile in zip((xa, xb), x_choices(d)):
            out[f * d.levels : (f + 1) * d.levels, :] = pad[
                pl.ds(base_row(d, f, 0) + FRONT + tile, d.levels, stride=d.block), :
            ]
        zface[f * d.tiles : (f + 1) * d.tiles, :] = pad[
            pl.ds(pl.multiple_of(base_row(d, f, z_out) + FRONT, 8), d.tiles), :
        ]
    write_y(d, yq, packed, lane)
    for copy in moves:
        copy.wait()


def x_halos(d, xa, xb, rows):
    a, b = xa[rows, :], xb[rows, :]
    return left_right(d, a, b)


def left_right(d, a, b):
    me = lax.axis_index("gx")
    even = lax.rem(me, 2) == 0
    left = jnp.where(me == 0, 0.0, jnp.where(even, b, a))
    right = jnp.where(me == d.n_gx - 1, 0.0, jnp.where(even, a, b))
    return left, right


def set_x_halos(d, pad, f, left, right):
    pad[pl.ds(base_row(d, f, 0) + FRONT - 1, d.levels, stride=d.block), :] = left
    pad[pl.ds(base_row(d, f, 0) + d.block, d.levels, stride=d.block), :] = right


def set_z_halos(d, pad, zface):
    low = lax.axis_index("gz") == 0
    for f in range(FIELDS):
        face = zface[f * d.tiles : (f + 1) * d.tiles, :]
        pad[pl.ds(base_row(d, f, -1) + FRONT, d.tiles), :] = jnp.where(low, 0.0, face)
        pad[pl.ds(base_row(d, f, d.levels) + FRONT, d.tiles), :] = jnp.where(low, face, 0.0)


def y_halo(d, yq, f, z):
    g = f // d.per_group
    halo = yq[0][:, g * LANES : (g + 1) * LANES]
    if d.y_sends == 2:
        halo = halo + yq[1][:, g * LANES : (g + 1) * LANES]
    return pltpu.roll(halo, LANES - 1 - lane_of(d, f, z), 1)


def stencil(d, pad, yq, wind, diff, f, z, lane):
    base = base_row(d, f, z)
    v = pad[pl.ds(pl.multiple_of(base + FRONT, 8), d.tiles), :]
    xm = pad[pl.ds(base + FRONT - 1, d.tiles), :]
    xp = pad[pl.ds(base + FRONT + 1, d.tiles), :]
    zm = pad[pl.ds(pl.multiple_of(base + FRONT - d.block, 8), d.tiles), :]
    zp = pad[pl.ds(pl.multiple_of(base + FRONT + d.block, 8), d.tiles), :]
    halo = 0.0 if yq is None else y_halo(d, yq, f, z)
    yp = jnp.where(lane == d.columns - 1, halo, pltpu.roll(v, LANES - 1, 1))
    ym = jnp.where(lane == 0, halo, pltpu.roll(v, 1, 1))
    spread = STEP * diff[f]
    wx = (0.5 * STEP) * wind[0, z]
    wy = (0.5 * STEP) * wind[1, z]
    wz = (0.5 * STEP) * wind[2, z]
    new = (1.0 - 6.0 * spread) * v
    new = new + ((spread - wx) * xp + (spread + wx) * xm)
    new = new + ((spread - wy) * yp + (spread + wy) * ym)
    new = new + ((spread - wz) * zp + (spread + wz) * zm)
    return v, new


def speed(u, v, w):
    return jnp.sqrt(u * u + v * v + w * w + 1.0)


def prepare_kernel(d, pad, wall_type, wind, diff, count, slot_of, parent_of, *outs):
    new_pad, wall_coef, from_left, from_right, masks, send_table, place_table, counts, tally = outs
    me = lax.axis_index("gx")
    first_tile = me * d.tiles
    row = lax.broadcasted_iota(jnp.int32, (d.tiles, LANES), 0)
    strength = jnp.zeros((d.tiles, LANES), F32)
    owner = jnp.full((d.tiles, LANES), -1, jnp.int32)
    for x in range(d.tiles):
        held = jnp.where(slot_of[first_tile + x] >= 0, count[x], 0).astype(F32) * (1.0 / BMAX)
        strength = jnp.where(row == x, held, strength)
        owner = jnp.where(row == x, parent_of[first_tile + x] - me * d.parents, owner)
    kind = wall_type[...]
    value = jnp.zeros((d.tiles, LANES), F32)
    for code, entry in enumerate(TABLE):
        value = jnp.where(kind == code, entry, value)
    coef = value * strength
    wall_coef[...] = coef

    lane = lax.broadcasted_iota(jnp.int32, (d.tiles, LANES), 1)

    def level(z, carry):
        both = [stencil(d, pad, None, wind, diff, f, z, lane) for f in range(FIELDS)]
        drag = STEP * (coef * speed(*(both[f][0] for f in range(3))))
        for f in range(FIELDS):
            new = both[f][1] - drag * both[f][0] if f < 3 else both[f][1]
            new_pad[pl.ds(pl.multiple_of(base_row(d, f, z) + FRONT, 8), d.tiles), :] = new
        return carry

    lax.fori_loop(0, d.levels, level, 0, unroll=8)
    for p in range(d.parents + 1):
        masks[p * d.tiles : (p + 1) * d.tiles, :] = jnp.where(owner == p, 1.0, 0.0)
    for z in range(d.levels):
        wx = (0.5 * STEP) * wind[0, z]
        for f in range(FIELDS):
            spread = STEP * diff[f]
            from_left[f * d.levels + z : f * d.levels + z + 1, :] = jnp.full((1, LANES), spread + wx, F32)
            from_right[f * d.levels + z : f * d.levels + z + 1, :] = jnp.full((1, LANES), spread - wx, F32)
    for k in range(d.n_gx):
        tally[k] = 0
    for i in range(d.n_gx * d.capacity):
        send_table[i] = 0
    for x in range(d.tiles):
        slot = slot_of[first_tile + x]

        @pl.when(slot >= 0)
        def _():
            away = lax.bitwise_xor(lax.shift_right_logical(slot, 3), me)
            rank = tally[away]
            send_table[away * d.capacity + rank] = x
            tally[away] = rank + 1

    def source(s, carry):
        away = lax.bitwise_xor(s, me)

        def tile(x, rank):
            slot = slot_of[s * d.tiles + x]
            mine = (slot >= 0) & (lax.shift_right_logical(slot, 3) == me)
            place = jnp.where(mine, slot - me * SLOTS, SLOTS)
            place_table[place] = away * d.capacity + rank
            return rank + mine.astype(jnp.int32)

        lax.fori_loop(0, d.tiles, tile, 0, unroll=True)
        return carry

    lax.fori_loop(0, d.n_gx, source, 0)
    before = jnp.maximum(first_tile - d.tiles, 0)
    for p in range(d.parents):
        total = jnp.int32(0)
        for x in range(d.tiles):
            total = total + (parent_of[first_tile + x] == me * d.parents + p).astype(jnp.int32)
            if p == 0:
                earlier = parent_of[before + x] == me * d.parents
                total = total + ((me > 0) & earlier).astype(jnp.int32)
        counts[p] = total


def step_one_kernel(d, pad_in, xa, xb, zface, *refs):
    yq = refs[: d.y_sends]
    wall_coef, from_left, from_right, wind, diff, send_table = refs[d.y_sends : d.y_sends + 6]
    outs = refs[d.y_sends + 6 :]
    pad, new_pad, factor, z_out, head = outs[:5]
    yq_out = outs[5 : 5 + d.y_sends]
    stress = outs[5 + d.y_sends :]
    low = lax.axis_index("gz") == 0
    end = jnp.where(low, d.levels - 1, 0)
    changed = []
    for f in range(FIELDS):
        cut = slice(f * d.levels, (f + 1) * d.levels)
        left, right = x_halos(d, xa, xb, cut)
        for tile, added in ((0, from_left[cut, :] * left), (d.tiles - 1, from_right[cut, :] * right)):
            place = pl.ds(base_row(d, f, 0) + FRONT + tile, d.levels, stride=d.block)
            changed.append((place, pad[place, :] + added))
    for place, cells in changed:
        pad[place, :] = cells
    changed = []
    for f in range(FIELDS):
        wz = (0.5 * STEP) * wind[2, end]
        weight = STEP * diff[f] + jnp.where(low, -wz, wz)
        place = pl.ds(pl.multiple_of(base_row(d, f, end) + FRONT, 8), d.tiles)
        changed.append((place, pad[place, :] + weight * zface[f * d.tiles : (f + 1) * d.tiles, :]))
    for place, cells in changed:
        pad[place, :] = cells
    lane = lax.broadcasted_iota(jnp.int32, (d.tiles, LANES), 1)
    coef = wall_coef[...]
    last = jnp.where(lane == d.columns - 1, 1.0, 0.0)
    zeroth = jnp.where(lane == 0, 1.0, 0.0)

    def level(z, carry):
        wy = (0.5 * STEP) * wind[1, z]
        news = []
        for f in range(FIELDS):
            spread = STEP * diff[f]
            place = pl.ds(pl.multiple_of(base_row(d, f, z) + FRONT, 8), d.tiles)
            weight = (spread - wy) * last + (spread + wy) * zeroth
            news.append(pad[place, :] + weight * y_halo(d, yq, f, z))
        for f in range(FIELDS):
            new_pad[pl.ds(pl.multiple_of(base_row(d, f, z) + FRONT, 8), d.tiles), :] = news[f]
        factor[pl.ds(pl.multiple_of(z * d.tiles, 8), d.tiles), :] = coef * speed(*news[:3])
        return carry

    lax.fori_loop(0, d.levels, level, 0, unroll=8)
    packed = [jnp.zeros((d.tiles, LANES), F32)] * d.groups
    for f in range(FIELDS):
        packed = add_edges(d, packed, new_pad, f, lane)
    write_y(d, yq_out, packed, lane)
    first, second = x_choices(d)
    targets = [(head, f * d.levels, f, 0) for f in range(FIELDS)]
    targets += [(stress[1], d.part + f * d.levels, f, first) for f in range(FIELDS)]
    targets += [(stress[3], d.part + i * d.levels, d.late + i, second) for i in range(d.early)]
    for out, start, f, tile in targets:
        out[start : start + d.levels, :] = new_pad[
            pl.ds(base_row(d, f, 0) + FRONT + tile, d.levels, stride=d.block), :
        ]
    z_level = jnp.where(lax.axis_index("gz") == 0, d.levels - 1, 0)
    for f in range(FIELDS):
        z_out[f * d.tiles : (f + 1) * d.tiles, :] = new_pad[
            pl.ds(pl.multiple_of(base_row(d, f, z_level) + FRONT, 8), d.tiles), :
        ]
    for k in range(d.n_gx):
        for c in range(d.capacity):
            tile = send_table[k * d.capacity + c]
            stress[k][c * d.levels : (c + 1) * d.levels, :] = factor[pl.ds(tile, d.levels, stride=d.tiles), :]


def step_two_kernel(d, pad_in, factor, zface, *refs):
    yq = refs[: d.y_sends]
    masks_in, wind, diff = refs[d.y_sends : d.y_sends + 3]
    pad, new_fields, own_sums, sent_sums, sent_b, coarse = refs[-6:]
    zero_x = jnp.zeros((d.levels, LANES), F32)
    for f in range(FIELDS):
        set_x_halos(d, pad, f, zero_x, zero_x)
    set_z_halos(d, pad, zface)
    lane = lax.broadcasted_iota(jnp.int32, (d.tiles, LANES), 1)
    zeros = jnp.zeros((d.tiles, LANES), F32)
    masks = [masks_in[p * d.tiles : (p + 1) * d.tiles, :] for p in range(d.parents + 1)]
    coarse_levels = d.levels // RATIO
    coarse[...] = jnp.zeros_like(coarse)
    rows = d.levels * d.tiles
    per_parent = coarse.shape[0] // (d.parents + 1)

    def coarse_level(k, carry):
        def level(i, sums):
            z = k * RATIO + i
            drag = STEP * factor[pl.ds(pl.multiple_of(z * d.tiles, 8), d.tiles), :]
            added = []
            for f in range(FIELDS):
                v, new = stencil(d, pad, yq, wind, diff, f, z, lane)
                if f < 3:
                    new = new - drag * v
                new_fields[pl.ds(pl.multiple_of(f * rows + z * d.tiles, 8), d.tiles), :] = new
                added.append(sums[f] + new)
            return tuple(added)

        sums = lax.fori_loop(0, RATIO, level, (zeros,) * FIELDS, unroll=8)
        for p in range(d.parents + 1):
            for f in range(FIELDS):
                line = jnp.sum(sums[f] * masks[p], axis=0, keepdims=True)
                coarse[pl.ds(p * per_parent + f * coarse_levels + k, 1), :] = line
        return carry

    lax.fori_loop(0, coarse_levels, coarse_level, 0)
    own_sums[...] = coarse[: d.parents * per_parent, :]
    sent_sums[...] = coarse[d.parents * per_parent :, :]
    second = x_choices(d)[1]
    for f in range(d.late):
        sent_b[f * d.levels : (f + 1) * d.levels, :] = pad[
            pl.ds(base_row(d, f, 0) + FRONT + second, d.levels, stride=d.block), :
        ]
    sent_b[d.late * d.levels :, :] = coarse[d.parents * per_parent :, :]


def flush_kernel(d, state, new_fields, sem):
    copy = pltpu.make_async_copy(state.at[pl.ds(0, new_fields.shape[0]), :], new_fields, sem.at[0])
    copy.start()
    copy.wait()


def finish_kernel(d, from_left, from_right, flushed, state_in, head, coarse, *refs):
    got_a, got_b, parent_of, place_table, counts = refs[:5]
    stress, refs = refs[5 : 5 + d.n_gx], refs[5:]
    new_fields, state, wall_stress, parent_mean, terms, gathered, placed, mean_out, sems = refs[d.n_gx :]
    me = lax.axis_index("gx")
    even = lax.rem(me, 2) == 0
    rows = d.levels * d.tiles
    coarse_levels = d.levels // RATIO
    per_parent = coarse.shape[0] // d.parents
    copies = []
    part = d.part
    for k in range(d.n_gx):
        gathered[k * part : (k + 1) * part, :] = stress[k][:part, :]
    for s in range(SLOTS):
        start = pl.multiple_of(place_table[s] * d.levels, 8)
        placed[pl.ds(s, d.levels, stride=SLOTS), :] = gathered[pl.ds(start, d.levels), :]
    copies.append(pltpu.make_async_copy(placed.at[pl.ds(0, d.levels * SLOTS), :], wall_stress, sems.at[2 * FIELDS]))
    copies[-1].start()
    for f in range(FIELDS):
        cut = slice(f * d.levels, (f + 1) * d.levels)
        a = stress[1][d.part + f * d.levels : d.part + (f + 1) * d.levels, :]
        if f < d.late:
            b = got_b[cut, :]
        else:
            b = stress[3][d.part + (f - d.late) * d.levels : d.part + (f - d.late + 1) * d.levels, :]
        left, right = left_right(d, a, b)
        left, right = from_left[cut, :] * left, from_right[cut, :] * right
        ahead = from_right[cut, :] * head[cut, :]
        for tile, added in ((0, left), (d.tiles - 1, right)):
            place = pl.ds(f * rows + tile, d.levels, stride=d.tiles)
            state[place, :] = state[place, :] + added
        for i, tile in enumerate((0, d.tiles - 1)):
            ends = [
                array.at[pl.ds(f * rows, rows), :].reshape(d.levels, d.tiles, LANES).at[:, pl.ds(tile, 1), :]
                for array in (state, new_fields)
            ]
            copies.append(pltpu.make_async_copy(*ends, sems.at[2 * f + i]))
            copies[-1].start()
        for i, term in enumerate((left, right, ahead)):
            terms[i * per_parent + f * coarse_levels : i * per_parent + (f + 1) * coarse_levels, :] = jnp.sum(
                term.reshape(coarse_levels, RATIO, LANES), axis=1
            )
    filled = FIELDS * coarse_levels
    if filled < per_parent:
        for i in range(3):
            terms[i * per_parent + filled : (i + 1) * per_parent, :] = jnp.zeros((per_parent - filled, LANES), F32)
    got = jnp.where(even, got_b[d.late * d.levels :, :], got_a[...])
    first_tile = me * d.tiles
    first_parent = parent_of[first_tile] - me * d.parents
    last_parent = parent_of[first_tile + d.tiles - 1] - me * d.parents
    before = jnp.maximum(first_tile - 1, 0)
    ahead_counts = (me > 0) & (parent_of[before] == me * d.parents)
    pick_row = lax.broadcasted_iota(jnp.int32, (LANES, LANES), 0)
    pick_lane = lax.broadcasted_iota(jnp.int32, (LANES, LANES), 1)
    pick = jnp.where(pick_row // RATIO == pick_lane, 1.0, 0.0)
    for p in range(d.parents):
        total = coarse[p * per_parent : (p + 1) * per_parent, :]
        total = total + jnp.where(first_parent == p, terms[:per_parent, :], 0.0)
        total = total + jnp.where(last_parent == p, terms[per_parent : 2 * per_parent, :], 0.0)
        if p == 0:
            total = total + jnp.where(me == 0, 0.0, got)
            total = total + jnp.where(ahead_counts, terms[2 * per_parent :, :], 0.0)
        total = jnp.dot(total, pick, precision=lax.Precision.HIGHEST, preferred_element_type=F32)
        mean = total / (jnp.full(total.shape, counts[p], jnp.int32).astype(F32) * (RATIO * RATIO))
        for f in range(FIELDS):
            mean_out[p, f] = mean[f * coarse_levels : (f + 1) * coarse_levels, : d.columns // RATIO]
    copies.append(pltpu.make_async_copy(mean_out, parent_mean, sems.at[2 * FIELDS + 1]))
    copies[-1].start()
    for copy in copies:
        copy.wait()


def swapped(block, axis):
    return lax.ppermute(block, axis, [(i, i ^ 1) for i in range(lax.axis_size(axis))])


def swapped_between(block, axis, inner):
    n = lax.axis_size(axis)
    route = []
    for i in range(n):
        for k in range(2):
            other = (i, 1 - k) if i in (0, n - 1) else (i + 1 if i % 2 else i - 1, k)
            route.append((2 * i + k, 2 * other[0] + other[1]))
    return lax.ppermute(block, (axis, inner), route)


def crossed(block, axis, distance):
    return lax.ppermute(block, axis, [(i, i ^ distance) for i in range(lax.axis_size(axis))])


def x_swapped(xa, xb):
    return [in_vmem(swapped(xa, "gx")), in_vmem(swapped_between(xb, "gx", "gz"))]


def zy_swapped(d, zface, yq):
    if d.y_sends == 1:
        yq = [swapped(yq[0], "gy")]
    else:
        n = d.n_gy
        yq = [
            lax.ppermute(yq[0], "gy", [(i, i + 1) for i in range(n - 1)]),
            lax.ppermute(yq[1], "gy", [(i + 1, i) for i in range(n - 1)]),
        ]
    return [in_vmem(a) for a in (swapped(zface, "gz"), *yq)]


def body(fields, parent_wind, diffusivity, wall_type, building_count, slot_of, parent_of):
    _, levels, tiles, columns = fields.shape
    d = Dims(levels, tiles, columns, slot_of.shape[0], lax.axis_size("gx"), lax.axis_size("gy"))
    assert columns == LANES and lax.axis_size("gz") == 2 and d.n_gx & (d.n_gx - 1) == 0
    params = pltpu.CompilerParams(vmem_limit_bytes=24 << 20)
    small = [in_hbm(a) for a in (wall_type, parent_wind, diffusivity, building_count, slot_of, parent_of)]
    rows = FIELDS * levels * tiles
    pad_t = pltpu.VMEM((d.pad_rows, LANES), F32)
    x_t = pltpu.VMEM((FIELDS * levels, LANES), F32)
    z_t = pltpu.VMEM((FIELDS * tiles, LANES), F32)
    y_ts = [pltpu.VMEM((tiles, d.groups * LANES), F32)] * d.y_sends

    n_small = len(small)
    *small, pad, xa, xb, zface = (packed := pl.pallas_call(
        functools.partial(pack_kernel, d),
        out_shape=[pltpu.SMEM(a.shape, a.dtype) if a.shape != wall_type.shape else pltpu.VMEM(a.shape, a.dtype) for a in small]
        + [pad_t, x_t, x_t, z_t, *y_ts],
        in_specs=[pl.BlockSpec(memory_space=pltpu.HBM)] * (1 + n_small),
        out_specs=[VM] + [SM] * (n_small - 1) + [VM] * (4 + d.y_sends),
        scratch_shapes=[pltpu.VMEM(fields.shape, F32), pltpu.SemaphoreType.DMA((FIELDS + n_small,))],
        compiler_params=params,
        name="pack",
    )(in_hbm(fields), *small))[: n_small + 4]
    yq = packed[n_small + 4 :]
    faces = x_swapped(xa, xb) + zy_swapped(d, zface, yq)
    hbm = pl.BlockSpec(memory_space=pltpu.HBM)

    def ints(n):
        return pltpu.SMEM((n,), jnp.int32)

    new_pad, wall_coef, from_left, from_right, masks, send_table, place_table, counts = pl.pallas_call(
        functools.partial(prepare_kernel, d),
        out_shape=[pad_t, pltpu.VMEM((tiles, LANES), F32), x_t, x_t]
        + [pltpu.VMEM(((d.parents + 1) * tiles, LANES), F32)]
        + [ints(d.n_gx * d.capacity), ints(SLOTS + 1), ints(d.parents)],
        in_specs=[VM] * 2 + [SM] * 5,
        out_specs=[VM] * 5 + [SM] * 3,
        scratch_shapes=[ints(d.n_gx)],
        compiler_params=params,
        name="prepare",
    )(in_vmem(pad), in_vmem(small[0]), *small[1:])

    _, new_pad, factor, zface, head, *rest = pl.pallas_call(
        functools.partial(step_one_kernel, d),
        out_shape=[pad_t, pad_t, pltpu.VMEM(((levels + 1) * tiles, LANES), F32), z_t, x_t, *y_ts]
        + [pltpu.VMEM((d.part + d.riders(k), LANES), F32) for k in range(d.n_gx)],
        in_specs=[VM] * (7 + d.y_sends) + [SM] * 3,
        out_specs=[VM] * (5 + d.y_sends + d.n_gx),
        input_output_aliases={0: 0},
        compiler_params=params,
        name="step_one",
    )(in_vmem(new_pad), *faces, *[in_vmem(a) for a in (wall_coef, from_left, from_right)], small[1], small[2], send_table)
    yq, stress = rest[: d.y_sends], rest[d.y_sends :]
    faces = zy_swapped(d, zface, yq)
    stress = [stress[0]] + [in_vmem(crossed(stress[k], "gx", k)) for k in range(1, d.n_gx)]

    per_parent = -(-FIELDS * (levels // RATIO) // 8) * 8
    state_t = pltpu.VMEM((rows + tiles, LANES), F32)
    _, state, own_sums, sent_sums, sent_b = pl.pallas_call(
        functools.partial(step_two_kernel, d),
        out_shape=[
            pad_t,
            state_t,
            pltpu.VMEM((d.parents * per_parent, LANES), F32),
            pltpu.VMEM((per_parent, LANES), F32),
            pltpu.VMEM((d.late * levels + per_parent, LANES), F32),
        ],
        in_specs=[VM] * (4 + d.y_sends) + [SM] * 2,
        out_specs=[VM] * 5,
        scratch_shapes=[pltpu.VMEM(((d.parents + 1) * per_parent, LANES), F32)],
        input_output_aliases={0: 0},
        compiler_params=params,
        name="step_two",
    )(in_vmem(new_pad), in_vmem(factor), *faces, in_vmem(masks), small[1], small[2])
    got = x_swapped(sent_sums, sent_b)

    flushed = pl.pallas_call(
        functools.partial(flush_kernel, d),
        out_shape=jax.ShapeDtypeStruct((rows, LANES), F32),
        in_specs=[VM],
        out_specs=hbm,
        scratch_shapes=[pltpu.SemaphoreType.DMA((1,))],
        compiler_params=params,
        name="flush",
    )(in_vmem(state))

    new_fields, _, wall_stress, parent_mean = pl.pallas_call(
        functools.partial(finish_kernel, d),
        out_shape=[
            jax.ShapeDtypeStruct((rows, LANES), F32),
            state_t,
            jax.ShapeDtypeStruct((levels * SLOTS, LANES), F32),
            jax.ShapeDtypeStruct((d.parents, FIELDS, levels // RATIO, columns // RATIO), F32),
        ],
        in_specs=[VM] * 2 + [hbm] + [VM] * 5 + [SM] * 3 + [VM] * d.n_gx,
        out_specs=[hbm, VM, hbm, hbm],
        scratch_shapes=[
            pltpu.VMEM((3 * per_parent, LANES), F32),
            pltpu.VMEM((d.n_gx * d.capacity * levels, LANES), F32),
            pltpu.VMEM(((levels + 1) * SLOTS, LANES), F32),
            pltpu.VMEM((d.parents, FIELDS, levels // RATIO, columns // RATIO), F32),
            pltpu.SemaphoreType.DMA((2 * FIELDS + 2,)),
        ],
        input_output_aliases={2: 0, 3: 1},
        compiler_params=params,
        name="finish",
    )(
        in_vmem(from_left),
        in_vmem(from_right),
        flushed,
        *[in_vmem(a) for a in (state, head, own_sums)],
        *got,
        small[5],
        place_table,
        counts,
        *[in_vmem(stress[0])],
        *stress[1:],
    )
    return (
        new_fields.reshape(fields.shape),
        wall_stress.reshape(levels, SLOTS, columns),
        parent_mean,
    )


def solution(mesh):
    in_specs = (
        P(None, "gz", ("groups", "gx"), "gy"),
        P(None, ("groups", "gz")),
        P(),
        P(("groups", "gx"), "gy"),
        P(("groups", "gx")),
        P("groups"),
        P("groups"),
    )
    out_specs = (
        P(None, "gz", ("groups", "gx"), "gy"),
        P("gz", ("groups", "gx"), "gy"),
        P(("groups", "gx"), None, "gz", "gy"),
    )
    return jax.shard_map(body, mesh=mesh, in_specs=in_specs, out_specs=out_specs, check_vma=False)
```

```python
import functools

import jax
import jax.numpy as jnp
from jax import lax
from jax.experimental import pallas as pl
from jax.experimental.pallas import tpu as pltpu
from jax.sharding import PartitionSpec as P

FIELDS = 5
RATIO = 8
BMAX = 32
SLOTS = 8

TABLE = (0.4, 0.8, 1.3, 2.0)
STEP = 0.25

FRONT = 8
LANES = 128
F32 = jnp.float32

VM = pl.BlockSpec(memory_space=pltpu.VMEM)
SM = pl.BlockSpec(memory_space=pltpu.SMEM)


def in_hbm(array):
    return pltpu.with_memory_space_constraint(array, pltpu.HBM)


def in_vmem(array):
    return pltpu.with_memory_space_constraint(array, pltpu.VMEM)


class Dims:
    def __init__(self, levels, tiles, columns, all_tiles, n_gx, n_gy):
        self.levels, self.tiles, self.columns = levels, tiles, columns
        self.all_tiles, self.n_gx, self.n_gy = all_tiles, n_gx, n_gy
        self.block = FRONT + tiles
        self.pad_rows = FIELDS * (levels + 2) * self.block + 8
        self.capacity = (tiles + n_gx - 1) // n_gx
        self.per_group = LANES // (2 * levels)
        self.groups = -(-FIELDS // self.per_group)
        self.parents = tiles // RATIO
        self.y_sends = 1 if n_gy == 2 else 2
        self.part = self.capacity * levels
        self.early = 2 if n_gx == 4 else 0
        self.late = FIELDS - self.early

    def riders(self, k):
        return self.levels * (FIELDS if k == 1 else self.early if k == 3 else 0)


def base_row(d, f, z):
    return (f * (d.levels + 2) + z + 1) * d.block


def lane_of(d, f, z):
    return 2 * ((f % d.per_group) * d.levels + z)


def x_choices(d):
    even = lax.rem(lax.axis_index("gx"), 2) == 0
    return [jnp.where(even, d.tiles - 1, 0), jnp.where(even, 0, d.tiles - 1)]


def add_edges(d, packed, pad, f, lane, raw=None):
    pair = lax.rem(lax.shift_right_logical(lane + 1, 1), LANES // 2)
    g = f // d.per_group
    for z in range(d.levels):
        if raw is None:
            cells = pad[pl.ds(base_row(d, f, z) + FRONT, d.tiles), :]
        else:
            cells = raw[f, z]
            pad[pl.ds(base_row(d, f, z) + FRONT, d.tiles), :] = cells
        place = lane_of(d, f, z)
        moved = pltpu.roll(cells, place, 1) if place else cells
        packed[g] = jnp.where(pair == place // 2, moved, packed[g])
    return packed


def write_y(d, outs, packed, lane):
    odd = lax.rem(lane, 2) == 1
    first = lax.axis_index("gy") == 0
    for g in range(d.groups):
        tail = pltpu.roll(jnp.where(odd, packed[g], 0.0), 2, 1)
        head = jnp.where(odd, 0.0, packed[g])
        messages = [jnp.where(first, tail, head)] if d.y_sends == 1 else [tail, head]
        for out, message in zip(outs, messages):
            out[:, g * LANES : (g + 1) * LANES] = message


def pack_kernel(d, fields, *refs):
    n_small = len(refs[: (len(refs) - 5 - d.y_sends) // 2])
    small, refs = refs[:n_small], refs[n_small:]
    small_out, (pad, xa, xb, zface), yq = refs[:n_small], refs[n_small : n_small + 4], refs[n_small + 4 : -2]
    raw, sems = refs[-2:]
    lane = lax.broadcasted_iota(jnp.int32, (d.tiles, LANES), 1)
    copies = []
    for f in range(FIELDS):
        copies.append(pltpu.make_async_copy(fields.at[f], raw.at[f], sems.at[f]))
    moves = [
        pltpu.make_async_copy(source, target, sems.at[FIELDS + i])
        for i, (source, target) in enumerate(zip(small, small_out))
    ]
    for copy in copies + moves:
        copy.start()
    zero_x = jnp.zeros((d.levels, LANES), F32)
    for f in range(FIELDS):
        set_x_halos(d, pad, f, zero_x, zero_x)
        for z in (-1, d.levels):
            pad[pl.ds(base_row(d, f, z) + FRONT, d.tiles), :] = jnp.zeros((d.tiles, LANES), F32)
    z_out = jnp.where(lax.axis_index("gz") == 0, d.levels - 1, 0)
    packed = [jnp.zeros((d.tiles, LANES), F32)] * d.groups
    for f in range(FIELDS):
        copies[f].wait()
        packed = add_edges(d, packed, pad, f, lane, raw)
        for out, tile in zip((xa, xb), x_choices(d)):
            out[f * d.levels : (f + 1) * d.levels, :] = pad[
                pl.ds(base_row(d, f, 0) + FRONT + tile, d.levels, stride=d.block), :
            ]
        zface[f * d.tiles : (f + 1) * d.tiles, :] = pad[
            pl.ds(pl.multiple_of(base_row(d, f, z_out) + FRONT, 8), d.tiles), :
        ]
    write_y(d, yq, packed, lane)
    for copy in moves:
        copy.wait()


def x_halos(d, xa, xb, rows):
    a, b = xa[rows, :], xb[rows, :]
    return left_right(d, a, b)


def left_right(d, a, b):
    me = lax.axis_index("gx")
    even = lax.rem(me, 2) == 0
    left = jnp.where(me == 0, 0.0, jnp.where(even, b, a))
    right = jnp.where(me == d.n_gx - 1, 0.0, jnp.where(even, a, b))
    return left, right


def set_x_halos(d, pad, f, left, right):
    pad[pl.ds(base_row(d, f, 0) + FRONT - 1, d.levels, stride=d.block), :] = left
    pad[pl.ds(base_row(d, f, 0) + d.block, d.levels, stride=d.block), :] = right


def set_z_halos(d, pad, zface):
    low = lax.axis_index("gz") == 0
    for f in range(FIELDS):
        face = zface[f * d.tiles : (f + 1) * d.tiles, :]
        pad[pl.ds(base_row(d, f, -1) + FRONT, d.tiles), :] = jnp.where(low, 0.0, face)
        pad[pl.ds(base_row(d, f, d.levels) + FRONT, d.tiles), :] = jnp.where(low, face, 0.0)


def y_halo(d, yq, f, z):
    g = f // d.per_group
    halo = yq[0][:, g * LANES : (g + 1) * LANES]
    if d.y_sends == 2:
        halo = halo + yq[1][:, g * LANES : (g + 1) * LANES]
    return pltpu.roll(halo, LANES - 1 - lane_of(d, f, z), 1)


def stencil(d, pad, yq, wind, diff, f, z, lane):
    base = base_row(d, f, z)
    v = pad[pl.ds(pl.multiple_of(base + FRONT, 8), d.tiles), :]
    xm = pad[pl.ds(base + FRONT - 1, d.tiles), :]
    xp = pad[pl.ds(base + FRONT + 1, d.tiles), :]
    zm = pad[pl.ds(pl.multiple_of(base + FRONT - d.block, 8), d.tiles), :]
    zp = pad[pl.ds(pl.multiple_of(base + FRONT + d.block, 8), d.tiles), :]
    halo = 0.0 if yq is None else y_halo(d, yq, f, z)
    yp = jnp.where(lane == d.columns - 1, halo, pltpu.roll(v, LANES - 1, 1))
    ym = jnp.where(lane == 0, halo, pltpu.roll(v, 1, 1))
    spread = STEP * diff[f]
    wx = (0.5 * STEP) * wind[0, z]
    wy = (0.5 * STEP) * wind[1, z]
    wz = (0.5 * STEP) * wind[2, z]
    new = (1.0 - 6.0 * spread) * v
    new = new + ((spread - wx) * xp + (spread + wx) * xm)
    new = new + ((spread - wy) * yp + (spread + wy) * ym)
    new = new + ((spread - wz) * zp + (spread + wz) * zm)
    return v, new


def speed(u, v, w):
    return jnp.sqrt(u * u + v * v + w * w + 1.0)


def prepare_kernel(d, pad, wall_type, wind, diff, count, slot_of, parent_of, *outs):
    new_pad, wall_coef, from_left, from_right, masks, send_table, place_table, counts, tally = outs
    me = lax.axis_index("gx")
    first_tile = me * d.tiles
    row = lax.broadcasted_iota(jnp.int32, (d.tiles, LANES), 0)
    strength = jnp.zeros((d.tiles, LANES), F32)
    owner = jnp.full((d.tiles, LANES), -1, jnp.int32)
    for x in range(d.tiles):
        held = jnp.where(slot_of[first_tile + x] >= 0, count[x], 0).astype(F32) * (1.0 / BMAX)
        strength = jnp.where(row == x, held, strength)
        owner = jnp.where(row == x, parent_of[first_tile + x] - me * d.parents, owner)
    kind = wall_type[...]
    value = jnp.zeros((d.tiles, LANES), F32)
    for code, entry in enumerate(TABLE):
        value = jnp.where(kind == code, entry, value)
    coef = value * strength
    wall_coef[...] = coef

    lane = lax.broadcasted_iota(jnp.int32, (d.tiles, LANES), 1)

    def level(z, carry):
        both = [stencil(d, pad, None, wind, diff, f, z, lane) for f in range(FIELDS)]
        drag = STEP * (coef * speed(*(both[f][0] for f in range(3))))
        for f in range(FIELDS):
            new = both[f][1] - drag * both[f][0] if f < 3 else both[f][1]
            new_pad[pl.ds(pl.multiple_of(base_row(d, f, z) + FRONT, 8), d.tiles), :] = new
        return carry

    lax.fori_loop(0, d.levels, level, 0, unroll=8)
    for p in range(d.parents + 1):
        masks[p * d.tiles : (p + 1) * d.tiles, :] = jnp.where(owner == p, 1.0, 0.0)
    for z in range(d.levels):
        wx = (0.5 * STEP) * wind[0, z]
        for f in range(FIELDS):
            spread = STEP * diff[f]
            from_left[f * d.levels + z : f * d.levels + z + 1, :] = jnp.full((1, LANES), spread + wx, F32)
            from_right[f * d.levels + z : f * d.levels + z + 1, :] = jnp.full((1, LANES), spread - wx, F32)
    for k in range(d.n_gx):
        tally[k] = 0
    for i in range(d.n_gx * d.capacity):
        send_table[i] = 0
    for x in range(d.tiles):
        slot = slot_of[first_tile + x]

        @pl.when(slot >= 0)
        def _():
            away = lax.bitwise_xor(lax.shift_right_logical(slot, 3), me)
            rank = tally[away]
            send_table[away * d.capacity + rank] = x
            tally[away] = rank + 1

    def source(s, carry):
        away = lax.bitwise_xor(s, me)

        def tile(x, rank):
            slot = slot_of[s * d.tiles + x]
            mine = (slot >= 0) & (lax.shift_right_logical(slot, 3) == me)
            place = jnp.where(mine, slot - me * SLOTS, SLOTS)
            place_table[place] = away * d.capacity + rank
            return rank + mine.astype(jnp.int32)

        lax.fori_loop(0, d.tiles, tile, 0, unroll=True)
        return carry

    lax.fori_loop(0, d.n_gx, source, 0)
    before = jnp.maximum(first_tile - d.tiles, 0)
    for p in range(d.parents):
        total = jnp.int32(0)
        for x in range(d.tiles):
            total = total + (parent_of[first_tile + x] == me * d.parents + p).astype(jnp.int32)
            if p == 0:
                earlier = parent_of[before + x] == me * d.parents
                total = total + ((me > 0) & earlier).astype(jnp.int32)
        counts[p] = total


def step_one_kernel(d, pad_in, xa, xb, zface, *refs):
    yq = refs[: d.y_sends]
    wall_coef, from_left, from_right, wind, diff, send_table = refs[d.y_sends : d.y_sends + 6]
    outs = refs[d.y_sends + 6 :]
    pad, new_pad, factor, z_out, head = outs[:5]
    yq_out = outs[5 : 5 + d.y_sends]
    stress = outs[5 + d.y_sends :]
    low = lax.axis_index("gz") == 0
    end = jnp.where(low, d.levels - 1, 0)
    changed = []
    for f in range(FIELDS):
        cut = slice(f * d.levels, (f + 1) * d.levels)
        left, right = x_halos(d, xa, xb, cut)
        for tile, added in ((0, from_left[cut, :] * left), (d.tiles - 1, from_right[cut, :] * right)):
            place = pl.ds(base_row(d, f, 0) + FRONT + tile, d.levels, stride=d.block)
            changed.append((place, pad[place, :] + added))
    for place, cells in changed:
        pad[place, :] = cells
    changed = []
    for f in range(FIELDS):
        wz = (0.5 * STEP) * wind[2, end]
        weight = STEP * diff[f] + jnp.where(low, -wz, wz)
        place = pl.ds(pl.multiple_of(base_row(d, f, end) + FRONT, 8), d.tiles)
        changed.append((place, pad[place, :] + weight * zface[f * d.tiles : (f + 1) * d.tiles, :]))
    for place, cells in changed:
        pad[place, :] = cells
    lane = lax.broadcasted_iota(jnp.int32, (d.tiles, LANES), 1)
    coef = wall_coef[...]
    last = jnp.where(lane == d.columns - 1, 1.0, 0.0)
    zeroth = jnp.where(lane == 0, 1.0, 0.0)

    def level(z, carry):
        wy = (0.5 * STEP) * wind[1, z]
        news = []
        for f in range(FIELDS):
            spread = STEP * diff[f]
            place = pl.ds(pl.multiple_of(base_row(d, f, z) + FRONT, 8), d.tiles)
            weight = (spread - wy) * last + (spread + wy) * zeroth
            news.append(pad[place, :] + weight * y_halo(d, yq, f, z))
        for f in range(FIELDS):
            new_pad[pl.ds(pl.multiple_of(base_row(d, f, z) + FRONT, 8), d.tiles), :] = news[f]
        factor[pl.ds(pl.multiple_of(z * d.tiles, 8), d.tiles), :] = coef * speed(*news[:3])
        return carry

    lax.fori_loop(0, d.levels, level, 0, unroll=8)
    packed = [jnp.zeros((d.tiles, LANES), F32)] * d.groups
    for f in range(FIELDS):
        packed = add_edges(d, packed, new_pad, f, lane)
    write_y(d, yq_out, packed, lane)
    first, second = x_choices(d)
    targets = [(head, f * d.levels, f, 0) for f in range(FIELDS)]
    targets += [(stress[1], d.part + f * d.levels, f, first) for f in range(FIELDS)]
    targets += [(stress[3], d.part + i * d.levels, d.late + i, second) for i in range(d.early)]
    for out, start, f, tile in targets:
        out[start : start + d.levels, :] = new_pad[
            pl.ds(base_row(d, f, 0) + FRONT + tile, d.levels, stride=d.block), :
        ]
    z_level = jnp.where(lax.axis_index("gz") == 0, d.levels - 1, 0)
    for f in range(FIELDS):
        z_out[f * d.tiles : (f + 1) * d.tiles, :] = new_pad[
            pl.ds(pl.multiple_of(base_row(d, f, z_level) + FRONT, 8), d.tiles), :
        ]
    for k in range(d.n_gx):
        for c in range(d.capacity):
            tile = send_table[k * d.capacity + c]
            stress[k][c * d.levels : (c + 1) * d.levels, :] = factor[pl.ds(tile, d.levels, stride=d.tiles), :]


def local_two_kernel(d, pad_in, factor, wind, diff, pad, raw):
    zero_x = jnp.zeros((d.levels, LANES), F32)
    for f in range(FIELDS):
        set_x_halos(d, pad, f, zero_x, zero_x)
        for z in (-1, d.levels):
            pad[pl.ds(base_row(d, f, z) + FRONT, d.tiles), :] = jnp.zeros((d.tiles, LANES), F32)
    lane = lax.broadcasted_iota(jnp.int32, (d.tiles, LANES), 1)
    rows = d.levels * d.tiles

    def level(z, carry):
        drag = STEP * factor[pl.ds(pl.multiple_of(z * d.tiles, 8), d.tiles), :]
        for f in range(FIELDS):
            v, new = stencil(d, pad, None, wind, diff, f, z, lane)
            if f < 3:
                new = new - drag * v
            raw[pl.ds(pl.multiple_of(f * rows + z * d.tiles, 8), d.tiles), :] = new
        return carry

    lax.fori_loop(0, d.levels, level, 0, unroll=8)


def step_two_kernel(d, raw_in, pad, zface, *refs):
    yq = refs[: d.y_sends]
    masks_in, wind, diff = refs[d.y_sends : d.y_sends + 3]
    raw, new_fields, own_sums, sent_sums, sent_b, coarse = refs[-6:]
    rows = d.levels * d.tiles
    low = lax.axis_index("gz") == 0
    end = jnp.where(low, d.levels - 1, 0)
    changed = []
    for f in range(FIELDS):
        wz = (0.5 * STEP) * wind[2, end]
        weight = STEP * diff[f] + jnp.where(low, -wz, wz)
        place = pl.ds(pl.multiple_of(f * rows + end * d.tiles, 8), d.tiles)
        changed.append((place, raw[place, :] + weight * zface[f * d.tiles : (f + 1) * d.tiles, :]))
    for place, cells in changed:
        raw[place, :] = cells
    lane = lax.broadcasted_iota(jnp.int32, (d.tiles, LANES), 1)
    last = jnp.where(lane == d.columns - 1, 1.0, 0.0)
    zeroth = jnp.where(lane == 0, 1.0, 0.0)
    zeros = jnp.zeros((d.tiles, LANES), F32)
    masks = [masks_in[p * d.tiles : (p + 1) * d.tiles, :] for p in range(d.parents + 1)]
    coarse_levels = d.levels // RATIO
    coarse[...] = jnp.zeros_like(coarse)
    per_parent = coarse.shape[0] // (d.parents + 1)

    def coarse_level(k, carry):
        def level(i, sums):
            z = k * RATIO + i
            wy = (0.5 * STEP) * wind[1, z]
            added = []
            for f in range(FIELDS):
                spread = STEP * diff[f]
                place = pl.ds(pl.multiple_of(f * rows + z * d.tiles, 8), d.tiles)
                weight = (spread - wy) * last + (spread + wy) * zeroth
                new = raw[place, :] + weight * y_halo(d, yq, f, z)
                new_fields[place, :] = new
                added.append(sums[f] + new)
            return tuple(added)

        sums = lax.fori_loop(0, RATIO, level, (zeros,) * FIELDS, unroll=8)
        for p in range(d.parents + 1):
            for f in range(FIELDS):
                line = jnp.sum(sums[f] * masks[p], axis=0, keepdims=True)
                coarse[pl.ds(p * per_parent + f * coarse_levels + k, 1), :] = line
        return carry

    lax.fori_loop(0, coarse_levels, coarse_level, 0)
    own_sums[...] = coarse[: d.parents * per_parent, :]
    sent_sums[...] = coarse[d.parents * per_parent :, :]
    second = x_choices(d)[1]
    for f in range(d.late):
        sent_b[f * d.levels : (f + 1) * d.levels, :] = pad[
            pl.ds(base_row(d, f, 0) + FRONT + second, d.levels, stride=d.block), :
        ]
    sent_b[d.late * d.levels :, :] = coarse[d.parents * per_parent :, :]


def flush_kernel(d, state, new_fields, sem):
    copy = pltpu.make_async_copy(state.at[pl.ds(0, new_fields.shape[0]), :], new_fields, sem.at[0])
    copy.start()
    copy.wait()


def finish_kernel(d, from_left, from_right, flushed, state_in, head, coarse, *refs):
    got_a, got_b, parent_of, place_table, counts = refs[:5]
    stress, refs = refs[5 : 5 + d.n_gx], refs[5:]
    new_fields, state, wall_stress, parent_mean, terms, gathered, placed, mean_out, sems = refs[d.n_gx :]
    me = lax.axis_index("gx")
    even = lax.rem(me, 2) == 0
    rows = d.levels * d.tiles
    coarse_levels = d.levels // RATIO
    per_parent = coarse.shape[0] // d.parents
    copies = []
    part = d.part
    for k in range(d.n_gx):
        gathered[k * part : (k + 1) * part, :] = stress[k][:part, :]
    for s in range(SLOTS):
        start = pl.multiple_of(place_table[s] * d.levels, 8)
        placed[pl.ds(s, d.levels, stride=SLOTS), :] = gathered[pl.ds(start, d.levels), :]
    copies.append(pltpu.make_async_copy(placed.at[pl.ds(0, d.levels * SLOTS), :], wall_stress, sems.at[2 * FIELDS]))
    copies[-1].start()
    for f in range(FIELDS):
        cut = slice(f * d.levels, (f + 1) * d.levels)
        a = stress[1][d.part + f * d.levels : d.part + (f + 1) * d.levels, :]
        if f < d.late:
            b = got_b[cut, :]
        else:
            b = stress[3][d.part + (f - d.late) * d.levels : d.part + (f - d.late + 1) * d.levels, :]
        left, right = left_right(d, a, b)
        left, right = from_left[cut, :] * left, from_right[cut, :] * right
        ahead = from_right[cut, :] * head[cut, :]
        for tile, added in ((0, left), (d.tiles - 1, right)):
            place = pl.ds(f * rows + tile, d.levels, stride=d.tiles)
            state[place, :] = state[place, :] + added
        for i, tile in enumerate((0, d.tiles - 1)):
            ends = [
                array.at[pl.ds(f * rows, rows), :].reshape(d.levels, d.tiles, LANES).at[:, pl.ds(tile, 1), :]
                for array in (state, new_fields)
            ]
            copies.append(pltpu.make_async_copy(*ends, sems.at[2 * f + i]))
            copies[-1].start()
        for i, term in enumerate((left, right, ahead)):
            terms[i * per_parent + f * coarse_levels : i * per_parent + (f + 1) * coarse_levels, :] = jnp.sum(
                term.reshape(coarse_levels, RATIO, LANES), axis=1
            )
    filled = FIELDS * coarse_levels
    if filled < per_parent:
        for i in range(3):
            terms[i * per_parent + filled : (i + 1) * per_parent, :] = jnp.zeros((per_parent - filled, LANES), F32)
    got = jnp.where(even, got_b[d.late * d.levels :, :], got_a[...])
    first_tile = me * d.tiles
    first_parent = parent_of[first_tile] - me * d.parents
    last_parent = parent_of[first_tile + d.tiles - 1] - me * d.parents
    before = jnp.maximum(first_tile - 1, 0)
    ahead_counts = (me > 0) & (parent_of[before] == me * d.parents)
    pick_row = lax.broadcasted_iota(jnp.int32, (LANES, LANES), 0)
    pick_lane = lax.broadcasted_iota(jnp.int32, (LANES, LANES), 1)
    pick = jnp.where(pick_row // RATIO == pick_lane, 1.0, 0.0)
    for p in range(d.parents):
        total = coarse[p * per_parent : (p + 1) * per_parent, :]
        total = total + jnp.where(first_parent == p, terms[:per_parent, :], 0.0)
        total = total + jnp.where(last_parent == p, terms[per_parent : 2 * per_parent, :], 0.0)
        if p == 0:
            total = total + jnp.where(me == 0, 0.0, got)
            total = total + jnp.where(ahead_counts, terms[2 * per_parent :, :], 0.0)
        total = jnp.dot(total, pick, precision=lax.Precision.HIGHEST, preferred_element_type=F32)
        mean = total / (jnp.full(total.shape, counts[p], jnp.int32).astype(F32) * (RATIO * RATIO))
        for f in range(FIELDS):
            mean_out[p, f] = mean[f * coarse_levels : (f + 1) * coarse_levels, : d.columns // RATIO]
    copies.append(pltpu.make_async_copy(mean_out, parent_mean, sems.at[2 * FIELDS + 1]))
    copies[-1].start()
    for copy in copies:
        copy.wait()


def swapped(block, axis):
    return lax.ppermute(block, axis, [(i, i ^ 1) for i in range(lax.axis_size(axis))])


def swapped_between(block, axis, inner):
    n = lax.axis_size(axis)
    route = []
    for i in range(n):
        for k in range(2):
            other = (i, 1 - k) if i in (0, n - 1) else (i + 1 if i % 2 else i - 1, k)
            route.append((2 * i + k, 2 * other[0] + other[1]))
    return lax.ppermute(block, (axis, inner), route)


def crossed(block, axis, distance):
    return lax.ppermute(block, axis, [(i, i ^ distance) for i in range(lax.axis_size(axis))])


def x_swapped(xa, xb):
    return [in_vmem(swapped(xa, "gx")), in_vmem(swapped_between(xb, "gx", "gz"))]


def zy_swapped(d, zface, yq):
    if d.y_sends == 1:
        yq = [swapped(yq[0], "gy")]
    else:
        n = d.n_gy
        yq = [
            lax.ppermute(yq[0], "gy", [(i, i + 1) for i in range(n - 1)]),
            lax.ppermute(yq[1], "gy", [(i + 1, i) for i in range(n - 1)]),
        ]
    return [in_vmem(a) for a in (swapped(zface, "gz"), *yq)]


def body(fields, parent_wind, diffusivity, wall_type, building_count, slot_of, parent_of):
    _, levels, tiles, columns = fields.shape
    d = Dims(levels, tiles, columns, slot_of.shape[0], lax.axis_size("gx"), lax.axis_size("gy"))
    assert columns == LANES and lax.axis_size("gz") == 2 and d.n_gx & (d.n_gx - 1) == 0
    params = pltpu.CompilerParams(vmem_limit_bytes=24 << 20)
    small = [in_hbm(a) for a in (wall_type, parent_wind, diffusivity, building_count, slot_of, parent_of)]
    rows = FIELDS * levels * tiles
    pad_t = pltpu.VMEM((d.pad_rows, LANES), F32)
    x_t = pltpu.VMEM((FIELDS * levels, LANES), F32)
    z_t = pltpu.VMEM((FIELDS * tiles, LANES), F32)
    y_ts = [pltpu.VMEM((tiles, d.groups * LANES), F32)] * d.y_sends

    n_small = len(small)
    *small, pad, xa, xb, zface = (packed := pl.pallas_call(
        functools.partial(pack_kernel, d),
        out_shape=[pltpu.SMEM(a.shape, a.dtype) if a.shape != wall_type.shape else pltpu.VMEM(a.shape, a.dtype) for a in small]
        + [pad_t, x_t, x_t, z_t, *y_ts],
        in_specs=[pl.BlockSpec(memory_space=pltpu.HBM)] * (1 + n_small),
        out_specs=[VM] + [SM] * (n_small - 1) + [VM] * (4 + d.y_sends),
        scratch_shapes=[pltpu.VMEM(fields.shape, F32), pltpu.SemaphoreType.DMA((FIELDS + n_small,))],
        compiler_params=params,
        name="pack",
    )(in_hbm(fields), *small))[: n_small + 4]
    yq = packed[n_small + 4 :]
    faces = x_swapped(xa, xb) + zy_swapped(d, zface, yq)
    hbm = pl.BlockSpec(memory_space=pltpu.HBM)

    def ints(n):
        return pltpu.SMEM((n,), jnp.int32)

    new_pad, wall_coef, from_left, from_right, masks, send_table, place_table, counts = pl.pallas_call(
        functools.partial(prepare_kernel, d),
        out_shape=[pad_t, pltpu.VMEM((tiles, LANES), F32), x_t, x_t]
        + [pltpu.VMEM(((d.parents + 1) * tiles, LANES), F32)]
        + [ints(d.n_gx * d.capacity), ints(SLOTS + 1), ints(d.parents)],
        in_specs=[VM] * 2 + [SM] * 5,
        out_specs=[VM] * 5 + [SM] * 3,
        scratch_shapes=[ints(d.n_gx)],
        compiler_params=params,
        name="prepare",
    )(in_vmem(pad), in_vmem(small[0]), *small[1:])

    _, new_pad, factor, zface, head, *rest = pl.pallas_call(
        functools.partial(step_one_kernel, d),
        out_shape=[pad_t, pad_t, pltpu.VMEM(((levels + 1) * tiles, LANES), F32), z_t, x_t, *y_ts]
        + [pltpu.VMEM((d.part + d.riders(k), LANES), F32) for k in range(d.n_gx)],
        in_specs=[VM] * (7 + d.y_sends) + [SM] * 3,
        out_specs=[VM] * (5 + d.y_sends + d.n_gx),
        input_output_aliases={0: 0},
        compiler_params=params,
        name="step_one",
    )(in_vmem(new_pad), *faces, *[in_vmem(a) for a in (wall_coef, from_left, from_right)], small[1], small[2], send_table)
    yq, stress = rest[: d.y_sends], rest[d.y_sends :]
    faces = zy_swapped(d, zface, yq)
    stress = [stress[0]] + [in_vmem(crossed(stress[k], "gx", k)) for k in range(1, d.n_gx)]

    per_parent = -(-FIELDS * (levels // RATIO) // 8) * 8
    state_t = pltpu.VMEM((rows + tiles, LANES), F32)
    new_pad, raw = pl.pallas_call(
        functools.partial(local_two_kernel, d),
        out_shape=[pad_t, state_t],
        in_specs=[VM] * 2 + [SM] * 2,
        out_specs=[VM] * 2,
        input_output_aliases={0: 0},
        compiler_params=params,
        name="local_two",
    )(in_vmem(new_pad), in_vmem(factor), small[1], small[2])
    _, state, own_sums, sent_sums, sent_b = pl.pallas_call(
        functools.partial(step_two_kernel, d),
        out_shape=[
            state_t,
            state_t,
            pltpu.VMEM((d.parents * per_parent, LANES), F32),
            pltpu.VMEM((per_parent, LANES), F32),
            pltpu.VMEM((d.late * levels + per_parent, LANES), F32),
        ],
        in_specs=[VM] * (4 + d.y_sends) + [SM] * 2,
        out_specs=[VM] * 5,
        scratch_shapes=[pltpu.VMEM(((d.parents + 1) * per_parent, LANES), F32)],
        input_output_aliases={0: 0},
        compiler_params=params,
        name="step_two",
    )(in_vmem(raw), in_vmem(new_pad), *faces, in_vmem(masks), small[1], small[2])
    got = x_swapped(sent_sums, sent_b)

    flushed = pl.pallas_call(
        functools.partial(flush_kernel, d),
        out_shape=jax.ShapeDtypeStruct((rows, LANES), F32),
        in_specs=[VM],
        out_specs=hbm,
        scratch_shapes=[pltpu.SemaphoreType.DMA((1,))],
        compiler_params=params,
        name="flush",
    )(in_vmem(state))

    new_fields, _, wall_stress, parent_mean = pl.pallas_call(
        functools.partial(finish_kernel, d),
        out_shape=[
            jax.ShapeDtypeStruct((rows, LANES), F32),
            state_t,
            jax.ShapeDtypeStruct((levels * SLOTS, LANES), F32),
            jax.ShapeDtypeStruct((d.parents, FIELDS, levels // RATIO, columns // RATIO), F32),
        ],
        in_specs=[VM] * 2 + [hbm] + [VM] * 5 + [SM] * 3 + [VM] * d.n_gx,
        out_specs=[hbm, VM, hbm, hbm],
        scratch_shapes=[
            pltpu.VMEM((3 * per_parent, LANES), F32),
            pltpu.VMEM((d.n_gx * d.capacity * levels, LANES), F32),
            pltpu.VMEM(((levels + 1) * SLOTS, LANES), F32),
            pltpu.VMEM((d.parents, FIELDS, levels // RATIO, columns // RATIO), F32),
            pltpu.SemaphoreType.DMA((2 * FIELDS + 2,)),
        ],
        input_output_aliases={2: 0, 3: 1},
        compiler_params=params,
        name="finish",
    )(
        in_vmem(from_left),
        in_vmem(from_right),
        flushed,
        *[in_vmem(a) for a in (state, head, own_sums)],
        *got,
        small[5],
        place_table,
        counts,
        *[in_vmem(stress[0])],
        *stress[1:],
    )
    return (
        new_fields.reshape(fields.shape),
        wall_stress.reshape(levels, SLOTS, columns),
        parent_mean,
    )


def solution(mesh):
    in_specs = (
        P(None, "gz", ("groups", "gx"), "gy"),
        P(None, ("groups", "gz")),
        P(),
        P(("groups", "gx"), "gy"),
        P(("groups", "gx")),
        P("groups"),
        P("groups"),
    )
    out_specs = (
        P(None, "gz", ("groups", "gx"), "gy"),
        P("gz", ("groups", "gx"), "gy"),
        P(("groups", "gx"), None, "gz", "gy"),
    )
    return jax.shard_map(body, mesh=mesh, in_specs=in_specs, out_specs=out_specs, check_vma=False)
```

```python
import functools

import jax
import jax.numpy as jnp
from jax import lax
from jax.experimental import pallas as pl
from jax.experimental.pallas import tpu as pltpu
from jax.sharding import PartitionSpec as P

FIELDS = 5
RATIO = 8
BMAX = 32
SLOTS = 8

TABLE = (0.4, 0.8, 1.3, 2.0)
STEP = 0.25

FRONT = 8
LANES = 128
F32 = jnp.float32

VM = pl.BlockSpec(memory_space=pltpu.VMEM)
SM = pl.BlockSpec(memory_space=pltpu.SMEM)


def in_hbm(array):
    return pltpu.with_memory_space_constraint(array, pltpu.HBM)


def in_vmem(array):
    return pltpu.with_memory_space_constraint(array, pltpu.VMEM)


class Dims:
    def __init__(self, levels, tiles, columns, all_tiles, n_gx, n_gy):
        self.levels, self.tiles, self.columns = levels, tiles, columns
        self.all_tiles, self.n_gx, self.n_gy = all_tiles, n_gx, n_gy
        self.block = FRONT + tiles
        self.pad_rows = FIELDS * (levels + 2) * self.block + 8
        self.capacity = (tiles + n_gx - 1) // n_gx
        self.per_group = LANES // (2 * levels)
        self.groups = -(-FIELDS // self.per_group)
        self.parents = tiles // RATIO
        self.y_sends = 1 if n_gy == 2 else 2
        self.part = self.capacity * levels
        self.early = 2 if n_gx == 4 else 0
        self.late = FIELDS - self.early

    def riders(self, k):
        return self.levels * (FIELDS if k == 1 else self.early if k == 3 else 0)


def base_row(d, f, z):
    return (f * (d.levels + 2) + z + 1) * d.block


def lane_of(d, f, z):
    return 2 * ((f % d.per_group) * d.levels + z)


def x_choices(d):
    even = lax.rem(lax.axis_index("gx"), 2) == 0
    return [jnp.where(even, d.tiles - 1, 0), jnp.where(even, 0, d.tiles - 1)]


def add_edges(d, packed, pad, f, lane, raw=None):
    pair = lax.rem(lax.shift_right_logical(lane + 1, 1), LANES // 2)
    g = f // d.per_group
    for z in range(d.levels):
        if raw is None:
            cells = pad[pl.ds(base_row(d, f, z) + FRONT, d.tiles), :]
        else:
            cells = raw[f, z]
            pad[pl.ds(base_row(d, f, z) + FRONT, d.tiles), :] = cells
        place = lane_of(d, f, z)
        moved = pltpu.roll(cells, place, 1) if place else cells
        packed[g] = jnp.where(pair == place // 2, moved, packed[g])
    return packed


def write_y(d, outs, packed, lane):
    odd = lax.rem(lane, 2) == 1
    first = lax.axis_index("gy") == 0
    for g in range(d.groups):
        tail = pltpu.roll(jnp.where(odd, packed[g], 0.0), 2, 1)
        head = jnp.where(odd, 0.0, packed[g])
        messages = [jnp.where(first, tail, head)] if d.y_sends == 1 else [tail, head]
        for out, message in zip(outs, messages):
            out[:, g * LANES : (g + 1) * LANES] = message


def pack_kernel(d, fields, *refs):
    n_small = len(refs[: (len(refs) - 5 - d.y_sends) // 2])
    small, refs = refs[:n_small], refs[n_small:]
    small_out, (pad, xa, xb, zface), yq = refs[:n_small], refs[n_small : n_small + 4], refs[n_small + 4 : -2]
    raw, sems = refs[-2:]
    lane = lax.broadcasted_iota(jnp.int32, (d.tiles, LANES), 1)
    copies = []
    for f in range(FIELDS):
        copies.append(pltpu.make_async_copy(fields.at[f], raw.at[f], sems.at[f]))
    moves = [
        pltpu.make_async_copy(source, target, sems.at[FIELDS + i])
        for i, (source, target) in enumerate(zip(small, small_out))
    ]
    for copy in copies + moves:
        copy.start()
    zero_x = jnp.zeros((d.levels, LANES), F32)
    for f in range(FIELDS):
        set_x_halos(d, pad, f, zero_x, zero_x)
        for z in (-1, d.levels):
            pad[pl.ds(base_row(d, f, z) + FRONT, d.tiles), :] = jnp.zeros((d.tiles, LANES), F32)
    z_out = jnp.where(lax.axis_index("gz") == 0, d.levels - 1, 0)
    packed = [jnp.zeros((d.tiles, LANES), F32)] * d.groups
    for f in range(FIELDS):
        copies[f].wait()
        packed = add_edges(d, packed, pad, f, lane, raw)
        for out, tile in zip((xa, xb), x_choices(d)):
            out[f * d.levels : (f + 1) * d.levels, :] = pad[
                pl.ds(base_row(d, f, 0) + FRONT + tile, d.levels, stride=d.block), :
            ]
        zface[f * d.tiles : (f + 1) * d.tiles, :] = pad[
            pl.ds(pl.multiple_of(base_row(d, f, z_out) + FRONT, 8), d.tiles), :
        ]
    write_y(d, yq, packed, lane)
    for copy in moves:
        copy.wait()


def x_halos(d, xa, xb, rows):
    a, b = xa[rows, :], xb[rows, :]
    return left_right(d, a, b)


def left_right(d, a, b):
    me = lax.axis_index("gx")
    even = lax.rem(me, 2) == 0
    left = jnp.where(me == 0, 0.0, jnp.where(even, b, a))
    right = jnp.where(me == d.n_gx - 1, 0.0, jnp.where(even, a, b))
    return left, right


def set_x_halos(d, pad, f, left, right):
    pad[pl.ds(base_row(d, f, 0) + FRONT - 1, d.levels, stride=d.block), :] = left
    pad[pl.ds(base_row(d, f, 0) + d.block, d.levels, stride=d.block), :] = right


def set_z_halos(d, pad, zface):
    low = lax.axis_index("gz") == 0
    for f in range(FIELDS):
        face = zface[f * d.tiles : (f + 1) * d.tiles, :]
        pad[pl.ds(base_row(d, f, -1) + FRONT, d.tiles), :] = jnp.where(low, 0.0, face)
        pad[pl.ds(base_row(d, f, d.levels) + FRONT, d.tiles), :] = jnp.where(low, face, 0.0)


def y_halo(d, yq, f, z):
    g = f // d.per_group
    halo = yq[0][:, g * LANES : (g + 1) * LANES]
    if d.y_sends == 2:
        halo = halo + yq[1][:, g * LANES : (g + 1) * LANES]
    return pltpu.roll(halo, LANES - 1 - lane_of(d, f, z), 1)


def stencil(d, pad, yq, wind, diff, f, z, lane):
    base = base_row(d, f, z)
    v = pad[pl.ds(pl.multiple_of(base + FRONT, 8), d.tiles), :]
    xm = pad[pl.ds(base + FRONT - 1, d.tiles), :]
    xp = pad[pl.ds(base + FRONT + 1, d.tiles), :]
    zm = pad[pl.ds(pl.multiple_of(base + FRONT - d.block, 8), d.tiles), :]
    zp = pad[pl.ds(pl.multiple_of(base + FRONT + d.block, 8), d.tiles), :]
    halo = 0.0 if yq is None else y_halo(d, yq, f, z)
    yp = jnp.where(lane == d.columns - 1, halo, pltpu.roll(v, LANES - 1, 1))
    ym = jnp.where(lane == 0, halo, pltpu.roll(v, 1, 1))
    spread = STEP * diff[f]
    wx = (0.5 * STEP) * wind[0, z]
    wy = (0.5 * STEP) * wind[1, z]
    wz = (0.5 * STEP) * wind[2, z]
    new = (1.0 - 6.0 * spread) * v
    new = new + ((spread - wx) * xp + (spread + wx) * xm)
    new = new + ((spread - wy) * yp + (spread + wy) * ym)
    new = new + ((spread - wz) * zp + (spread + wz) * zm)
    return v, new


def speed(u, v, w):
    return jnp.sqrt(u * u + v * v + w * w + 1.0)


def prepare_kernel(d, pad, wall_type, wind, diff, count, slot_of, parent_of, *outs):
    new_pad, wall_coef, from_left, from_right, masks, send_table, place_table, counts, tally = outs
    me = lax.axis_index("gx")
    first_tile = me * d.tiles
    row = lax.broadcasted_iota(jnp.int32, (d.tiles, LANES), 0)
    strength = jnp.zeros((d.tiles, LANES), F32)
    owner = jnp.full((d.tiles, LANES), -1, jnp.int32)
    for x in range(d.tiles):
        held = jnp.where(slot_of[first_tile + x] >= 0, count[x], 0).astype(F32) * (1.0 / BMAX)
        strength = jnp.where(row == x, held, strength)
        owner = jnp.where(row == x, parent_of[first_tile + x] - me * d.parents, owner)
    kind = wall_type[...]
    value = jnp.zeros((d.tiles, LANES), F32)
    for code, entry in enumerate(TABLE):
        value = jnp.where(kind == code, entry, value)
    coef = value * strength
    wall_coef[...] = coef

    lane = lax.broadcasted_iota(jnp.int32, (d.tiles, LANES), 1)

    def level(z, carry):
        both = [stencil(d, pad, None, wind, diff, f, z, lane) for f in range(FIELDS)]
        drag = STEP * (coef * speed(*(both[f][0] for f in range(3))))
        for f in range(FIELDS):
            new = both[f][1] - drag * both[f][0] if f < 3 else both[f][1]
            new_pad[pl.ds(pl.multiple_of(base_row(d, f, z) + FRONT, 8), d.tiles), :] = new
        return carry

    lax.fori_loop(0, d.levels, level, 0, unroll=8)
    for p in range(d.parents + 1):
        masks[p * d.tiles : (p + 1) * d.tiles, :] = jnp.where(owner == p, 1.0, 0.0)
    for z in range(d.levels):
        wx = (0.5 * STEP) * wind[0, z]
        for f in range(FIELDS):
            spread = STEP * diff[f]
            from_left[f * d.levels + z : f * d.levels + z + 1, :] = jnp.full((1, LANES), spread + wx, F32)
            from_right[f * d.levels + z : f * d.levels + z + 1, :] = jnp.full((1, LANES), spread - wx, F32)
    for k in range(d.n_gx):
        tally[k] = 0
    for i in range(d.n_gx * d.capacity):
        send_table[i] = 0
    for x in range(d.tiles):
        slot = slot_of[first_tile + x]

        @pl.when(slot >= 0)
        def _():
            away = lax.bitwise_xor(lax.shift_right_logical(slot, 3), me)
            rank = tally[away]
            send_table[away * d.capacity + rank] = x
            tally[away] = rank + 1

    def source(s, carry):
        away = lax.bitwise_xor(s, me)

        def tile(x, rank):
            slot = slot_of[s * d.tiles + x]
            mine = (slot >= 0) & (lax.shift_right_logical(slot, 3) == me)
            place = jnp.where(mine, slot - me * SLOTS, SLOTS)
            place_table[place] = away * d.capacity + rank
            return rank + mine.astype(jnp.int32)

        lax.fori_loop(0, d.tiles, tile, 0, unroll=True)
        return carry

    lax.fori_loop(0, d.n_gx, source, 0)
    before = jnp.maximum(first_tile - d.tiles, 0)
    for p in range(d.parents):
        total = jnp.int32(0)
        for x in range(d.tiles):
            total = total + (parent_of[first_tile + x] == me * d.parents + p).astype(jnp.int32)
            if p == 0:
                earlier = parent_of[before + x] == me * d.parents
                total = total + ((me > 0) & earlier).astype(jnp.int32)
        counts[p] = total


def step_one_kernel(d, pad_in, xa, xb, zface, *refs):
    yq = refs[: d.y_sends]
    wall_coef, from_left, from_right, wind, diff, send_table = refs[d.y_sends : d.y_sends + 6]
    outs = refs[d.y_sends + 6 :]
    pad, new_pad, factor, z_out, head = outs[:5]
    yq_out = outs[5 : 5 + d.y_sends]
    stress = outs[5 + d.y_sends :]
    low = lax.axis_index("gz") == 0
    end = jnp.where(low, d.levels - 1, 0)
    changed = []
    for f in range(FIELDS):
        cut = slice(f * d.levels, (f + 1) * d.levels)
        left, right = x_halos(d, xa, xb, cut)
        for tile, added in ((0, from_left[cut, :] * left), (d.tiles - 1, from_right[cut, :] * right)):
            place = pl.ds(base_row(d, f, 0) + FRONT + tile, d.levels, stride=d.block)
            changed.append((place, pad[place, :] + added))
    for place, cells in changed:
        pad[place, :] = cells
    changed = []
    for f in range(FIELDS):
        wz = (0.5 * STEP) * wind[2, end]
        weight = STEP * diff[f] + jnp.where(low, -wz, wz)
        place = pl.ds(pl.multiple_of(base_row(d, f, end) + FRONT, 8), d.tiles)
        changed.append((place, pad[place, :] + weight * zface[f * d.tiles : (f + 1) * d.tiles, :]))
    for place, cells in changed:
        pad[place, :] = cells
    lane = lax.broadcasted_iota(jnp.int32, (d.tiles, LANES), 1)
    coef = wall_coef[...]
    last = jnp.where(lane == d.columns - 1, 1.0, 0.0)
    zeroth = jnp.where(lane == 0, 1.0, 0.0)

    def level(z, carry):
        wy = (0.5 * STEP) * wind[1, z]
        news = []
        for f in range(FIELDS):
            spread = STEP * diff[f]
            place = pl.ds(pl.multiple_of(base_row(d, f, z) + FRONT, 8), d.tiles)
            weight = (spread - wy) * last + (spread + wy) * zeroth
            news.append(pad[place, :] + weight * y_halo(d, yq, f, z))
        for f in range(FIELDS):
            new_pad[pl.ds(pl.multiple_of(base_row(d, f, z) + FRONT, 8), d.tiles), :] = news[f]
        factor[pl.ds(pl.multiple_of(z * d.tiles, 8), d.tiles), :] = coef * speed(*news[:3])
        return carry

    lax.fori_loop(0, d.levels, level, 0, unroll=8)
    packed = [jnp.zeros((d.tiles, LANES), F32)] * d.groups
    for f in range(FIELDS):
        packed = add_edges(d, packed, new_pad, f, lane)
    write_y(d, yq_out, packed, lane)
    first, second = x_choices(d)
    targets = [(head, f * d.levels, f, 0) for f in range(FIELDS)]
    targets += [(stress[1], d.part + f * d.levels, f, first) for f in range(FIELDS)]
    targets += [(stress[3], d.part + i * d.levels, d.late + i, second) for i in range(d.early)]
    for out, start, f, tile in targets:
        out[start : start + d.levels, :] = new_pad[
            pl.ds(base_row(d, f, 0) + FRONT + tile, d.levels, stride=d.block), :
        ]
    z_level = jnp.where(lax.axis_index("gz") == 0, d.levels - 1, 0)
    for f in range(FIELDS):
        z_out[f * d.tiles : (f + 1) * d.tiles, :] = new_pad[
            pl.ds(pl.multiple_of(base_row(d, f, z_level) + FRONT, 8), d.tiles), :
        ]
    for k in range(d.n_gx):
        for c in range(d.capacity):
            tile = send_table[k * d.capacity + c]
            stress[k][c * d.levels : (c + 1) * d.levels, :] = factor[pl.ds(tile, d.levels, stride=d.tiles), :]


def local_two_kernel(d, pad_in, factor, masks_in, wind, diff, pad, raw, tail):
    zero_x = jnp.zeros((d.levels, LANES), F32)
    for f in range(FIELDS):
        set_x_halos(d, pad, f, zero_x, zero_x)
        for z in (-1, d.levels):
            pad[pl.ds(base_row(d, f, z) + FRONT, d.tiles), :] = jnp.zeros((d.tiles, LANES), F32)
    lane = lax.broadcasted_iota(jnp.int32, (d.tiles, LANES), 1)
    rows = d.levels * d.tiles

    zeros = jnp.zeros((d.tiles, LANES), F32)
    mask = masks_in[d.parents * d.tiles :, :]
    tail[...] = jnp.zeros_like(tail)
    coarse_levels = d.levels // RATIO

    def coarse_level(k, carry):
        def level(i, sums):
            z = k * RATIO + i
            drag = STEP * factor[pl.ds(pl.multiple_of(z * d.tiles, 8), d.tiles), :]
            added = []
            for f in range(FIELDS):
                v, new = stencil(d, pad, None, wind, diff, f, z, lane)
                if f < 3:
                    new = new - drag * v
                raw[pl.ds(pl.multiple_of(f * rows + z * d.tiles, 8), d.tiles), :] = new
                added.append(sums[f] + new)
            return tuple(added)

        sums = lax.fori_loop(0, RATIO, level, (zeros,) * FIELDS, unroll=8)
        for f in range(FIELDS):
            tail[pl.ds(f * coarse_levels + k, 1), :] = jnp.sum(sums[f] * mask, axis=0, keepdims=True)
        return carry

    lax.fori_loop(0, coarse_levels, coarse_level, 0)


def tail_kernel(d, tail, pad, zface, *refs):
    yq = refs[: d.y_sends]
    masks_in, wind, diff, sent_sums, sent_b, sums = refs[d.y_sends :]
    mask = masks_in[d.parents * d.tiles :, :]
    coarse_levels = d.levels // RATIO
    low = lax.axis_index("gz") == 0
    end = jnp.where(low, d.levels - 1, 0)
    end_block = jnp.where(low, coarse_levels - 1, 0)
    wz = (0.5 * STEP) * wind[2, end]
    lane = lax.broadcasted_iota(jnp.int32, (8, LANES), 1)
    last = jnp.where(lane == d.columns - 1, 1.0, 0.0)
    zeroth = jnp.where(lane == 0, 1.0, 0.0)
    halos = []
    for g in range(d.groups):
        halo = yq[0][:, g * LANES : (g + 1) * LANES]
        if d.y_sends == 2:
            halo = halo + yq[1][:, g * LANES : (g + 1) * LANES]
        halos.append(jnp.broadcast_to(jnp.sum(halo * mask, axis=0, keepdims=True), (8, LANES)))
    sums[...] = tail[...]
    lines = [[jnp.zeros((8, LANES), F32)] * coarse_levels for _ in range(FIELDS)]
    for z in range(d.levels):
        wy = (0.5 * STEP) * wind[1, z]
        for f in range(FIELDS):
            spread = STEP * diff[f]
            weight = (spread - wy) * last + (spread + wy) * zeroth
            moved = pltpu.roll(halos[f // d.per_group], LANES - 1 - lane_of(d, f, z), 1)
            lines[f][z // RATIO] = lines[f][z // RATIO] + weight * moved
    for f in range(FIELDS):
        face = jnp.sum(zface[f * d.tiles : (f + 1) * d.tiles, :] * mask, axis=0, keepdims=True)
        face = (STEP * diff[f] + jnp.where(low, -wz, wz)) * face
        for k in range(coarse_levels):
            line = lines[f][k][:1, :] + jnp.where(end_block == k, face, 0.0)
            at = f * coarse_levels + k
            sums[at : at + 1, :] = sums[at : at + 1, :] + line
    sent_sums[...] = sums[...]
    second = x_choices(d)[1]
    for f in range(d.late):
        sent_b[f * d.levels : (f + 1) * d.levels, :] = pad[
            pl.ds(base_row(d, f, 0) + FRONT + second, d.levels, stride=d.block), :
        ]
    sent_b[d.late * d.levels :, :] = sums[...]


def step_two_kernel(d, raw_in, zface, *refs):
    yq = refs[: d.y_sends]
    masks_in, wind, diff = refs[d.y_sends : d.y_sends + 3]
    raw, new_fields, coarse = refs[-3:]
    rows = d.levels * d.tiles
    low = lax.axis_index("gz") == 0
    end = jnp.where(low, d.levels - 1, 0)
    changed = []
    for f in range(FIELDS):
        wz = (0.5 * STEP) * wind[2, end]
        weight = STEP * diff[f] + jnp.where(low, -wz, wz)
        place = pl.ds(pl.multiple_of(f * rows + end * d.tiles, 8), d.tiles)
        changed.append((place, raw[place, :] + weight * zface[f * d.tiles : (f + 1) * d.tiles, :]))
    for place, cells in changed:
        raw[place, :] = cells
    lane = lax.broadcasted_iota(jnp.int32, (d.tiles, LANES), 1)
    last = jnp.where(lane == d.columns - 1, 1.0, 0.0)
    zeroth = jnp.where(lane == 0, 1.0, 0.0)
    zeros = jnp.zeros((d.tiles, LANES), F32)
    masks = [masks_in[p * d.tiles : (p + 1) * d.tiles, :] for p in range(d.parents)]
    coarse_levels = d.levels // RATIO
    coarse[...] = jnp.zeros_like(coarse)
    per_parent = coarse.shape[0] // d.parents

    def coarse_level(k, carry):
        def level(i, sums):
            z = k * RATIO + i
            wy = (0.5 * STEP) * wind[1, z]
            added = []
            for f in range(FIELDS):
                spread = STEP * diff[f]
                place = pl.ds(pl.multiple_of(f * rows + z * d.tiles, 8), d.tiles)
                weight = (spread - wy) * last + (spread + wy) * zeroth
                new = raw[place, :] + weight * y_halo(d, yq, f, z)
                new_fields[place, :] = new
                added.append(sums[f] + new)
            return tuple(added)

        sums = lax.fori_loop(0, RATIO, level, (zeros,) * FIELDS, unroll=8)
        for p in range(d.parents):
            for f in range(FIELDS):
                line = jnp.sum(sums[f] * masks[p], axis=0, keepdims=True)
                coarse[pl.ds(p * per_parent + f * coarse_levels + k, 1), :] = line
        return carry

    lax.fori_loop(0, coarse_levels, coarse_level, 0)


def flush_kernel(d, state, from_right, head, own_sums, parent_of, new_fields, sums, terms, sem):
    copy = pltpu.make_async_copy(state.at[pl.ds(0, new_fields.shape[0]), :], new_fields, sem.at[0])
    copy.start()
    coarse_levels = d.levels // RATIO
    terms[...] = jnp.zeros_like(terms)
    for f in range(FIELDS):
        cut = slice(f * d.levels, (f + 1) * d.levels)
        term = from_right[cut, :] * head[cut, :]
        terms[f * coarse_levels : (f + 1) * coarse_levels, :] = jnp.sum(
            term.reshape(coarse_levels, RATIO, LANES), axis=1
        )
    me = lax.axis_index("gx")
    before = jnp.maximum(me * d.tiles - 1, 0)
    counts = (me > 0) & (parent_of[before] == me * d.parents)
    per_parent = terms.shape[0]
    sums[:per_parent, :] = own_sums[:per_parent, :] + jnp.where(counts, terms[...], 0.0)
    sums[per_parent:, :] = own_sums[per_parent:, :]
    copy.wait()


def finish_kernel(d, from_left, from_right, flushed, state_in, coarse, *refs):
    got_a, got_b, parent_of, place_table, counts = refs[:5]
    stress, refs = refs[5 : 5 + d.n_gx], refs[5:]
    new_fields, state, wall_stress, parent_mean, terms, gathered, placed, mean_out, sems = refs[d.n_gx :]
    me = lax.axis_index("gx")
    even = lax.rem(me, 2) == 0
    rows = d.levels * d.tiles
    coarse_levels = d.levels // RATIO
    per_parent = coarse.shape[0] // d.parents
    copies = []
    part = d.part
    for k in range(d.n_gx):
        gathered[k * part : (k + 1) * part, :] = stress[k][:part, :]
    for s in range(SLOTS):
        start = pl.multiple_of(place_table[s] * d.levels, 8)
        placed[pl.ds(s, d.levels, stride=SLOTS), :] = gathered[pl.ds(start, d.levels), :]
    copies.append(pltpu.make_async_copy(placed.at[pl.ds(0, d.levels * SLOTS), :], wall_stress, sems.at[2 * FIELDS]))
    copies[-1].start()
    for f in range(FIELDS):
        cut = slice(f * d.levels, (f + 1) * d.levels)
        a = stress[1][d.part + f * d.levels : d.part + (f + 1) * d.levels, :]
        if f < d.late:
            b = got_b[cut, :]
        else:
            b = stress[3][d.part + (f - d.late) * d.levels : d.part + (f - d.late + 1) * d.levels, :]
        left, right = left_right(d, a, b)
        left, right = from_left[cut, :] * left, from_right[cut, :] * right
        for tile, added in ((0, left), (d.tiles - 1, right)):
            place = pl.ds(f * rows + tile, d.levels, stride=d.tiles)
            state[place, :] = state[place, :] + added
        for i, tile in enumerate((0, d.tiles - 1)):
            ends = [
                array.at[pl.ds(f * rows, rows), :].reshape(d.levels, d.tiles, LANES).at[:, pl.ds(tile, 1), :]
                for array in (state, new_fields)
            ]
            copies.append(pltpu.make_async_copy(*ends, sems.at[2 * f + i]))
            copies[-1].start()
        for i, term in enumerate((left, right)):
            terms[i * per_parent + f * coarse_levels : i * per_parent + (f + 1) * coarse_levels, :] = jnp.sum(
                term.reshape(coarse_levels, RATIO, LANES), axis=1
            )
    filled = FIELDS * coarse_levels
    if filled < per_parent:
        for i in range(2):
            terms[i * per_parent + filled : (i + 1) * per_parent, :] = jnp.zeros((per_parent - filled, LANES), F32)
    got = jnp.where(even, got_b[d.late * d.levels :, :], got_a[...])
    first_tile = me * d.tiles
    first_parent = parent_of[first_tile] - me * d.parents
    last_parent = parent_of[first_tile + d.tiles - 1] - me * d.parents
    pick_row = lax.broadcasted_iota(jnp.int32, (LANES, LANES), 0)
    pick_lane = lax.broadcasted_iota(jnp.int32, (LANES, LANES), 1)
    pick = jnp.where(pick_row // RATIO == pick_lane, 1.0, 0.0)
    totals = []
    for p in range(d.parents):
        total = coarse[p * per_parent : (p + 1) * per_parent, :]
        total = total + jnp.where(first_parent == p, terms[:per_parent, :], 0.0)
        total = total + jnp.where(last_parent == p, terms[per_parent : 2 * per_parent, :], 0.0)
        if p == 0:
            total = total + jnp.where(me == 0, 0.0, got)
        totals.append(total)
    summed = jnp.dot(
        jnp.concatenate(totals, axis=0), pick, precision=lax.Precision.HIGHEST, preferred_element_type=F32
    )
    for p in range(d.parents):
        total = summed[p * per_parent : (p + 1) * per_parent, :]
        mean = total / (jnp.full(total.shape, counts[p], jnp.int32).astype(F32) * (RATIO * RATIO))
        for f in range(FIELDS):
            mean_out[p, f] = mean[f * coarse_levels : (f + 1) * coarse_levels, : d.columns // RATIO]
    copies.append(pltpu.make_async_copy(mean_out, parent_mean, sems.at[2 * FIELDS + 1]))
    copies[-1].start()
    for copy in copies:
        copy.wait()


def swapped(block, axis):
    return lax.ppermute(block, axis, [(i, i ^ 1) for i in range(lax.axis_size(axis))])


def swapped_between(block, axis, inner):
    n = lax.axis_size(axis)
    route = []
    for i in range(n):
        for k in range(2):
            other = (i, 1 - k) if i in (0, n - 1) else (i + 1 if i % 2 else i - 1, k)
            route.append((2 * i + k, 2 * other[0] + other[1]))
    return lax.ppermute(block, (axis, inner), route)


def crossed(block, axis, distance):
    return lax.ppermute(block, axis, [(i, i ^ distance) for i in range(lax.axis_size(axis))])


def x_swapped(xa, xb):
    return [in_vmem(swapped(xa, "gx")), in_vmem(swapped_between(xb, "gx", "gz"))]


def zy_swapped(d, zface, yq):
    if d.y_sends == 1:
        yq = [swapped(yq[0], "gy")]
    else:
        n = d.n_gy
        yq = [
            lax.ppermute(yq[0], "gy", [(i, i + 1) for i in range(n - 1)]),
            lax.ppermute(yq[1], "gy", [(i + 1, i) for i in range(n - 1)]),
        ]
    return [in_vmem(a) for a in (swapped(zface, "gz"), *yq)]


def body(fields, parent_wind, diffusivity, wall_type, building_count, slot_of, parent_of):
    _, levels, tiles, columns = fields.shape
    d = Dims(levels, tiles, columns, slot_of.shape[0], lax.axis_size("gx"), lax.axis_size("gy"))
    assert columns == LANES and lax.axis_size("gz") == 2 and d.n_gx & (d.n_gx - 1) == 0
    params = pltpu.CompilerParams(vmem_limit_bytes=24 << 20)
    small = [in_hbm(a) for a in (wall_type, parent_wind, diffusivity, building_count, slot_of, parent_of)]
    rows = FIELDS * levels * tiles
    pad_t = pltpu.VMEM((d.pad_rows, LANES), F32)
    x_t = pltpu.VMEM((FIELDS * levels, LANES), F32)
    z_t = pltpu.VMEM((FIELDS * tiles, LANES), F32)
    y_ts = [pltpu.VMEM((tiles, d.groups * LANES), F32)] * d.y_sends

    n_small = len(small)
    *small, pad, xa, xb, zface = (packed := pl.pallas_call(
        functools.partial(pack_kernel, d),
        out_shape=[pltpu.SMEM(a.shape, a.dtype) if a.shape != wall_type.shape else pltpu.VMEM(a.shape, a.dtype) for a in small]
        + [pad_t, x_t, x_t, z_t, *y_ts],
        in_specs=[pl.BlockSpec(memory_space=pltpu.HBM)] * (1 + n_small),
        out_specs=[VM] + [SM] * (n_small - 1) + [VM] * (4 + d.y_sends),
        scratch_shapes=[pltpu.VMEM(fields.shape, F32), pltpu.SemaphoreType.DMA((FIELDS + n_small,))],
        compiler_params=params,
        name="pack",
    )(in_hbm(fields), *small))[: n_small + 4]
    yq = packed[n_small + 4 :]
    faces = x_swapped(xa, xb) + zy_swapped(d, zface, yq)
    hbm = pl.BlockSpec(memory_space=pltpu.HBM)

    def ints(n):
        return pltpu.SMEM((n,), jnp.int32)

    new_pad, wall_coef, from_left, from_right, masks, send_table, place_table, counts = pl.pallas_call(
        functools.partial(prepare_kernel, d),
        out_shape=[pad_t, pltpu.VMEM((tiles, LANES), F32), x_t, x_t]
        + [pltpu.VMEM(((d.parents + 1) * tiles, LANES), F32)]
        + [ints(d.n_gx * d.capacity), ints(SLOTS + 1), ints(d.parents)],
        in_specs=[VM] * 2 + [SM] * 5,
        out_specs=[VM] * 5 + [SM] * 3,
        scratch_shapes=[ints(d.n_gx)],
        compiler_params=params,
        name="prepare",
    )(in_vmem(pad), in_vmem(small[0]), *small[1:])

    _, new_pad, factor, zface, head, *rest = pl.pallas_call(
        functools.partial(step_one_kernel, d),
        out_shape=[pad_t, pad_t, pltpu.VMEM(((levels + 1) * tiles, LANES), F32), z_t, x_t, *y_ts]
        + [pltpu.VMEM((d.part + d.riders(k), LANES), F32) for k in range(d.n_gx)],
        in_specs=[VM] * (7 + d.y_sends) + [SM] * 3,
        out_specs=[VM] * (5 + d.y_sends + d.n_gx),
        input_output_aliases={0: 0},
        compiler_params=params,
        name="step_one",
    )(in_vmem(new_pad), *faces, *[in_vmem(a) for a in (wall_coef, from_left, from_right)], small[1], small[2], send_table)
    yq, stress = rest[: d.y_sends], rest[d.y_sends :]
    faces = zy_swapped(d, zface, yq)
    stress = [stress[0]] + [in_vmem(crossed(stress[k], "gx", k)) for k in range(1, d.n_gx)]

    per_parent = -(-FIELDS * (levels // RATIO) // 8) * 8
    state_t = pltpu.VMEM((rows + tiles, LANES), F32)
    new_pad, raw, tail = pl.pallas_call(
        functools.partial(local_two_kernel, d),
        out_shape=[pad_t, state_t, pltpu.VMEM((per_parent, LANES), F32)],
        in_specs=[VM] * 3 + [SM] * 2,
        out_specs=[VM] * 3,
        input_output_aliases={0: 0},
        compiler_params=params,
        name="local_two",
    )(in_vmem(new_pad), in_vmem(factor), in_vmem(masks), small[1], small[2])
    sent_sums, sent_b = pl.pallas_call(
        functools.partial(tail_kernel, d),
        out_shape=[
            pltpu.VMEM((per_parent, LANES), F32),
            pltpu.VMEM((d.late * levels + per_parent, LANES), F32),
        ],
        in_specs=[VM] * (4 + d.y_sends) + [SM] * 2,
        out_specs=[VM] * 2,
        scratch_shapes=[pltpu.VMEM((per_parent, LANES), F32)],
        compiler_params=params,
        name="tail",
    )(in_vmem(tail), in_vmem(new_pad), *faces, in_vmem(masks), small[1], small[2])
    _, state, own_sums = pl.pallas_call(
        functools.partial(step_two_kernel, d),
        out_shape=[state_t, state_t, pltpu.VMEM((d.parents * per_parent, LANES), F32)],
        in_specs=[VM] * (3 + d.y_sends) + [SM] * 2,
        out_specs=[VM] * 3,
        input_output_aliases={0: 0},
        compiler_params=params,
        name="step_two",
    )(in_vmem(raw), *faces, in_vmem(masks), small[1], small[2])
    got = x_swapped(sent_sums, sent_b)

    flushed, own_sums = pl.pallas_call(
        functools.partial(flush_kernel, d),
        out_shape=[jax.ShapeDtypeStruct((rows, LANES), F32), pltpu.VMEM((d.parents * per_parent, LANES), F32)],
        in_specs=[VM] * 4 + [SM],
        out_specs=[hbm, VM],
        scratch_shapes=[pltpu.VMEM((per_parent, LANES), F32), pltpu.SemaphoreType.DMA((1,))],
        compiler_params=params,
        name="flush",
    )(*[in_vmem(a) for a in (state, from_right, head, own_sums)], small[5])

    new_fields, _, wall_stress, parent_mean = pl.pallas_call(
        functools.partial(finish_kernel, d),
        out_shape=[
            jax.ShapeDtypeStruct((rows, LANES), F32),
            state_t,
            jax.ShapeDtypeStruct((levels * SLOTS, LANES), F32),
            jax.ShapeDtypeStruct((d.parents, FIELDS, levels // RATIO, columns // RATIO), F32),
        ],
        in_specs=[VM] * 2 + [hbm] + [VM] * 4 + [SM] * 3 + [VM] * d.n_gx,
        out_specs=[hbm, VM, hbm, hbm],
        scratch_shapes=[
            pltpu.VMEM((2 * per_parent, LANES), F32),
            pltpu.VMEM((d.n_gx * d.capacity * levels, LANES), F32),
            pltpu.VMEM(((levels + 1) * SLOTS, LANES), F32),
            pltpu.VMEM((d.parents, FIELDS, levels // RATIO, columns // RATIO), F32),
            pltpu.SemaphoreType.DMA((2 * FIELDS + 2,)),
        ],
        input_output_aliases={2: 0, 3: 1},
        compiler_params=params,
        name="finish",
    )(
        in_vmem(from_left),
        in_vmem(from_right),
        flushed,
        in_vmem(state),
        in_vmem(own_sums),
        *got,
        small[5],
        place_table,
        counts,
        *[in_vmem(stress[0])],
        *stress[1:],
    )
    return (
        new_fields.reshape(fields.shape),
        wall_stress.reshape(levels, SLOTS, columns),
        parent_mean,
    )


def solution(mesh):
    in_specs = (
        P(None, "gz", ("groups", "gx"), "gy"),
        P(None, ("groups", "gz")),
        P(),
        P(("groups", "gx"), "gy"),
        P(("groups", "gx")),
        P("groups"),
        P("groups"),
    )
    out_specs = (
        P(None, "gz", ("groups", "gx"), "gy"),
        P("gz", ("groups", "gx"), "gy"),
        P(("groups", "gx"), None, "gz", "gy"),
    )
    return jax.shard_map(body, mesh=mesh, in_specs=in_specs, out_specs=out_specs, check_vma=False)
```

```python
import functools

import jax
import jax.numpy as jnp
from jax import lax
from jax.experimental import pallas as pl
from jax.experimental.pallas import tpu as pltpu
from jax.sharding import PartitionSpec as P

FIELDS = 5
RATIO = 8
BMAX = 32
SLOTS = 8

TABLE = (0.4, 0.8, 1.3, 2.0)
STEP = 0.25

FRONT = 8
LANES = 128
F32 = jnp.float32

VM = pl.BlockSpec(memory_space=pltpu.VMEM)
SM = pl.BlockSpec(memory_space=pltpu.SMEM)


def in_hbm(array):
    return pltpu.with_memory_space_constraint(array, pltpu.HBM)


def in_vmem(array):
    return pltpu.with_memory_space_constraint(array, pltpu.VMEM)


class Dims:
    def __init__(self, levels, tiles, columns, all_tiles, n_gx, n_gy):
        self.levels, self.tiles, self.columns = levels, tiles, columns
        self.all_tiles, self.n_gx, self.n_gy = all_tiles, n_gx, n_gy
        self.block = FRONT + tiles
        self.pad_rows = FIELDS * (levels + 2) * self.block + 8
        self.capacity = (tiles + n_gx - 1) // n_gx
        self.per_group = LANES // (2 * levels)
        self.groups = -(-FIELDS // self.per_group)
        self.parents = tiles // RATIO
        self.y_sends = 1 if n_gy == 2 else 2
        self.part = self.capacity * levels
        self.early = 2 if n_gx == 4 else 0
        self.late = FIELDS - self.early

    def riders(self, k):
        return self.levels * (FIELDS if k == 1 else self.early if k == 3 else 0)


def base_row(d, f, z):
    return (f * (d.levels + 2) + z + 1) * d.block


def lane_of(d, f, z):
    return 2 * ((f % d.per_group) * d.levels + z)


def x_choices(d):
    even = lax.rem(lax.axis_index("gx"), 2) == 0
    return [jnp.where(even, d.tiles - 1, 0), jnp.where(even, 0, d.tiles - 1)]


def add_edges(d, packed, pad, f, lane, raw=None):
    pair = lax.rem(lax.shift_right_logical(lane + 1, 1), LANES // 2)
    g = f // d.per_group
    for z in range(d.levels):
        if raw is None:
            cells = pad[pl.ds(base_row(d, f, z) + FRONT, d.tiles), :]
        else:
            cells = raw[f, z]
            pad[pl.ds(base_row(d, f, z) + FRONT, d.tiles), :] = cells
        place = lane_of(d, f, z)
        moved = pltpu.roll(cells, place, 1) if place else cells
        packed[g] = jnp.where(pair == place // 2, moved, packed[g])
    return packed


def write_y(d, outs, packed, lane):
    odd = lax.rem(lane, 2) == 1
    first = lax.axis_index("gy") == 0
    for g in range(d.groups):
        tail = pltpu.roll(jnp.where(odd, packed[g], 0.0), 2, 1)
        head = jnp.where(odd, 0.0, packed[g])
        messages = [jnp.where(first, tail, head)] if d.y_sends == 1 else [tail, head]
        for out, message in zip(outs, messages):
            out[:, g * LANES : (g + 1) * LANES] = message


def pack_kernel(d, fields, *refs):
    n_small = len(refs[: (len(refs) - 5 - d.y_sends) // 2])
    small, refs = refs[:n_small], refs[n_small:]
    small_out, (pad, xa, xb, zface), yq = refs[:n_small], refs[n_small : n_small + 4], refs[n_small + 4 : -2]
    raw, sems = refs[-2:]
    lane = lax.broadcasted_iota(jnp.int32, (d.tiles, LANES), 1)
    copies = []
    for f in range(FIELDS):
        copies.append(pltpu.make_async_copy(fields.at[f], raw.at[f], sems.at[f]))
    moves = [
        pltpu.make_async_copy(source, target, sems.at[FIELDS + i])
        for i, (source, target) in enumerate(zip(small, small_out))
    ]
    for copy in copies + moves:
        copy.start()
    zero_x = jnp.zeros((d.levels, LANES), F32)
    for f in range(FIELDS):
        set_x_halos(d, pad, f, zero_x, zero_x)
        for z in (-1, d.levels):
            pad[pl.ds(base_row(d, f, z) + FRONT, d.tiles), :] = jnp.zeros((d.tiles, LANES), F32)
    z_out = jnp.where(lax.axis_index("gz") == 0, d.levels - 1, 0)
    packed = [jnp.zeros((d.tiles, LANES), F32)] * d.groups
    for f in range(FIELDS):
        copies[f].wait()
        packed = add_edges(d, packed, pad, f, lane, raw)
        for out, tile in zip((xa, xb), x_choices(d)):
            out[f * d.levels : (f + 1) * d.levels, :] = pad[
                pl.ds(base_row(d, f, 0) + FRONT + tile, d.levels, stride=d.block), :
            ]
        zface[f * d.tiles : (f + 1) * d.tiles, :] = pad[
            pl.ds(pl.multiple_of(base_row(d, f, z_out) + FRONT, 8), d.tiles), :
        ]
    write_y(d, yq, packed, lane)
    for copy in moves:
        copy.wait()


def x_halos(d, xa, xb, rows):
    a, b = xa[rows, :], xb[rows, :]
    return left_right(d, a, b)


def left_right(d, a, b):
    me = lax.axis_index("gx")
    even = lax.rem(me, 2) == 0
    left = jnp.where(me == 0, 0.0, jnp.where(even, b, a))
    right = jnp.where(me == d.n_gx - 1, 0.0, jnp.where(even, a, b))
    return left, right


def set_x_halos(d, pad, f, left, right):
    pad[pl.ds(base_row(d, f, 0) + FRONT - 1, d.levels, stride=d.block), :] = left
    pad[pl.ds(base_row(d, f, 0) + d.block, d.levels, stride=d.block), :] = right


def set_z_halos(d, pad, zface):
    low = lax.axis_index("gz") == 0
    for f in range(FIELDS):
        face = zface[f * d.tiles : (f + 1) * d.tiles, :]
        pad[pl.ds(base_row(d, f, -1) + FRONT, d.tiles), :] = jnp.where(low, 0.0, face)
        pad[pl.ds(base_row(d, f, d.levels) + FRONT, d.tiles), :] = jnp.where(low, face, 0.0)


def y_halo(d, yq, f, z):
    g = f // d.per_group
    halo = yq[0][:, g * LANES : (g + 1) * LANES]
    if d.y_sends == 2:
        halo = halo + yq[1][:, g * LANES : (g + 1) * LANES]
    return pltpu.roll(halo, LANES - 1 - lane_of(d, f, z), 1)


def stencil(d, pad, yq, wind, diff, f, z, lane):
    base = base_row(d, f, z)
    v = pad[pl.ds(pl.multiple_of(base + FRONT, 8), d.tiles), :]
    xm = pad[pl.ds(base + FRONT - 1, d.tiles), :]
    xp = pad[pl.ds(base + FRONT + 1, d.tiles), :]
    zm = pad[pl.ds(pl.multiple_of(base + FRONT - d.block, 8), d.tiles), :]
    zp = pad[pl.ds(pl.multiple_of(base + FRONT + d.block, 8), d.tiles), :]
    halo = 0.0 if yq is None else y_halo(d, yq, f, z)
    yp = jnp.where(lane == d.columns - 1, halo, pltpu.roll(v, LANES - 1, 1))
    ym = jnp.where(lane == 0, halo, pltpu.roll(v, 1, 1))
    spread = STEP * diff[f]
    wx = (0.5 * STEP) * wind[0, z]
    wy = (0.5 * STEP) * wind[1, z]
    wz = (0.5 * STEP) * wind[2, z]
    new = (1.0 - 6.0 * spread) * v
    new = new + ((spread - wx) * xp + (spread + wx) * xm)
    new = new + ((spread - wy) * yp + (spread + wy) * ym)
    new = new + ((spread - wz) * zp + (spread + wz) * zm)
    return v, new


def speed(u, v, w):
    return jnp.sqrt(u * u + v * v + w * w + 1.0)


def prepare_kernel(d, pad, wall_type, wind, diff, count, slot_of, parent_of, *outs):
    new_pad, wall_coef, from_left, from_right, masks, send_table, place_table, counts, tally = outs
    me = lax.axis_index("gx")
    first_tile = me * d.tiles
    row = lax.broadcasted_iota(jnp.int32, (d.tiles, LANES), 0)
    strength = jnp.zeros((d.tiles, LANES), F32)
    owner = jnp.full((d.tiles, LANES), -1, jnp.int32)
    for x in range(d.tiles):
        held = jnp.where(slot_of[first_tile + x] >= 0, count[x], 0).astype(F32) * (1.0 / BMAX)
        strength = jnp.where(row == x, held, strength)
        owner = jnp.where(row == x, parent_of[first_tile + x] - me * d.parents, owner)
    kind = wall_type[...]
    value = jnp.zeros((d.tiles, LANES), F32)
    for code, entry in enumerate(TABLE):
        value = jnp.where(kind == code, entry, value)
    coef = value * strength
    wall_coef[...] = coef

    lane = lax.broadcasted_iota(jnp.int32, (d.tiles, LANES), 1)

    def level(z, carry):
        both = [stencil(d, pad, None, wind, diff, f, z, lane) for f in range(FIELDS)]
        drag = STEP * (coef * speed(*(both[f][0] for f in range(3))))
        for f in range(FIELDS):
            new = both[f][1] - drag * both[f][0] if f < 3 else both[f][1]
            new_pad[pl.ds(pl.multiple_of(base_row(d, f, z) + FRONT, 8), d.tiles), :] = new
        return carry

    lax.fori_loop(0, d.levels, level, 0, unroll=8)
    for p in range(d.parents + 1):
        masks[p * d.tiles : (p + 1) * d.tiles, :] = jnp.where(owner == p, 1.0, 0.0)
    for z in range(d.levels):
        wx = (0.5 * STEP) * wind[0, z]
        for f in range(FIELDS):
            spread = STEP * diff[f]
            from_left[f * d.levels + z : f * d.levels + z + 1, :] = jnp.full((1, LANES), spread + wx, F32)
            from_right[f * d.levels + z : f * d.levels + z + 1, :] = jnp.full((1, LANES), spread - wx, F32)
    for k in range(d.n_gx):
        tally[k] = 0
    for i in range(d.n_gx * d.capacity):
        send_table[i] = 0
    for x in range(d.tiles):
        slot = slot_of[first_tile + x]

        @pl.when(slot >= 0)
        def _():
            away = lax.bitwise_xor(lax.shift_right_logical(slot, 3), me)
            rank = tally[away]
            send_table[away * d.capacity + rank] = x
            tally[away] = rank + 1

    def source(s, carry):
        away = lax.bitwise_xor(s, me)

        def tile(x, rank):
            slot = slot_of[s * d.tiles + x]
            mine = (slot >= 0) & (lax.shift_right_logical(slot, 3) == me)
            place = jnp.where(mine, slot - me * SLOTS, SLOTS)
            place_table[place] = away * d.capacity + rank
            return rank + mine.astype(jnp.int32)

        lax.fori_loop(0, d.tiles, tile, 0, unroll=True)
        return carry

    lax.fori_loop(0, d.n_gx, source, 0)
    before = jnp.maximum(first_tile - d.tiles, 0)
    for p in range(d.parents):
        total = jnp.int32(0)
        for x in range(d.tiles):
            total = total + (parent_of[first_tile + x] == me * d.parents + p).astype(jnp.int32)
            if p == 0:
                earlier = parent_of[before + x] == me * d.parents
                total = total + ((me > 0) & earlier).astype(jnp.int32)
        counts[p] = total


def step_one_kernel(d, pad_in, xa, xb, zface, *refs):
    yq = refs[: d.y_sends]
    wall_coef, from_left, from_right, wind, diff, send_table = refs[d.y_sends : d.y_sends + 6]
    outs = refs[d.y_sends + 6 :]
    pad, new_pad, factor, z_out, head = outs[:5]
    yq_out = outs[5 : 5 + d.y_sends]
    stress = outs[5 + d.y_sends :]
    low = lax.axis_index("gz") == 0
    end = jnp.where(low, d.levels - 1, 0)
    changed = []
    for f in range(FIELDS):
        cut = slice(f * d.levels, (f + 1) * d.levels)
        left, right = x_halos(d, xa, xb, cut)
        for tile, added in ((0, from_left[cut, :] * left), (d.tiles - 1, from_right[cut, :] * right)):
            place = pl.ds(base_row(d, f, 0) + FRONT + tile, d.levels, stride=d.block)
            changed.append((place, pad[place, :] + added))
    for place, cells in changed:
        pad[place, :] = cells
    changed = []
    for f in range(FIELDS):
        wz = (0.5 * STEP) * wind[2, end]
        weight = STEP * diff[f] + jnp.where(low, -wz, wz)
        place = pl.ds(pl.multiple_of(base_row(d, f, end) + FRONT, 8), d.tiles)
        changed.append((place, pad[place, :] + weight * zface[f * d.tiles : (f + 1) * d.tiles, :]))
    for place, cells in changed:
        pad[place, :] = cells
    lane = lax.broadcasted_iota(jnp.int32, (d.tiles, LANES), 1)
    coef = wall_coef[...]
    last = jnp.where(lane == d.columns - 1, 1.0, 0.0)
    zeroth = jnp.where(lane == 0, 1.0, 0.0)

    def level(z, carry):
        wy = (0.5 * STEP) * wind[1, z]
        news = []
        for f in range(FIELDS):
            spread = STEP * diff[f]
            place = pl.ds(pl.multiple_of(base_row(d, f, z) + FRONT, 8), d.tiles)
            weight = (spread - wy) * last + (spread + wy) * zeroth
            news.append(pad[place, :] + weight * y_halo(d, yq, f, z))
        for f in range(FIELDS):
            new_pad[pl.ds(pl.multiple_of(base_row(d, f, z) + FRONT, 8), d.tiles), :] = news[f]
        factor[pl.ds(pl.multiple_of(z * d.tiles, 8), d.tiles), :] = coef * speed(*news[:3])
        return carry

    lax.fori_loop(0, d.levels, level, 0, unroll=16)
    packed = [jnp.zeros((d.tiles, LANES), F32)] * d.groups
    for f in range(FIELDS):
        packed = add_edges(d, packed, new_pad, f, lane)
    write_y(d, yq_out, packed, lane)
    first, second = x_choices(d)
    targets = [(head, f * d.levels, f, 0) for f in range(FIELDS)]
    targets += [(stress[1], d.part + f * d.levels, f, first) for f in range(FIELDS)]
    targets += [(stress[3], d.part + i * d.levels, d.late + i, second) for i in range(d.early)]
    for out, start, f, tile in targets:
        out[start : start + d.levels, :] = new_pad[
            pl.ds(base_row(d, f, 0) + FRONT + tile, d.levels, stride=d.block), :
        ]
    z_level = jnp.where(lax.axis_index("gz") == 0, d.levels - 1, 0)
    for f in range(FIELDS):
        z_out[f * d.tiles : (f + 1) * d.tiles, :] = new_pad[
            pl.ds(pl.multiple_of(base_row(d, f, z_level) + FRONT, 8), d.tiles), :
        ]
    for k in range(d.n_gx):
        for c in range(d.capacity):
            tile = send_table[k * d.capacity + c]
            stress[k][c * d.levels : (c + 1) * d.levels, :] = factor[pl.ds(tile, d.levels, stride=d.tiles), :]


def local_two_kernel(d, pad_in, factor, masks_in, wind, diff, pad, raw, tail):
    zero_x = jnp.zeros((d.levels, LANES), F32)
    for f in range(FIELDS):
        set_x_halos(d, pad, f, zero_x, zero_x)
        for z in (-1, d.levels):
            pad[pl.ds(base_row(d, f, z) + FRONT, d.tiles), :] = jnp.zeros((d.tiles, LANES), F32)
    lane = lax.broadcasted_iota(jnp.int32, (d.tiles, LANES), 1)
    rows = d.levels * d.tiles

    zeros = jnp.zeros((d.tiles, LANES), F32)
    mask = masks_in[d.parents * d.tiles :, :]
    tail[...] = jnp.zeros_like(tail)
    coarse_levels = d.levels // RATIO

    def coarse_level(k, carry):
        def level(i, sums):
            z = k * RATIO + i
            drag = STEP * factor[pl.ds(pl.multiple_of(z * d.tiles, 8), d.tiles), :]
            added = []
            for f in range(FIELDS):
                v, new = stencil(d, pad, None, wind, diff, f, z, lane)
                if f < 3:
                    new = new - drag * v
                raw[pl.ds(pl.multiple_of(f * rows + z * d.tiles, 8), d.tiles), :] = new
                added.append(sums[f] + new)
            return tuple(added)

        sums = lax.fori_loop(0, RATIO, level, (zeros,) * FIELDS, unroll=8)
        for f in range(FIELDS):
            tail[pl.ds(f * coarse_levels + k, 1), :] = jnp.sum(sums[f] * mask, axis=0, keepdims=True)
        return carry

    lax.fori_loop(0, coarse_levels, coarse_level, 0)


def tail_kernel(d, tail, pad, zface, *refs):
    yq = refs[: d.y_sends]
    masks_in, wind, diff, sent_sums, sent_b, sums = refs[d.y_sends :]
    mask = masks_in[d.parents * d.tiles :, :]
    coarse_levels = d.levels // RATIO
    low = lax.axis_index("gz") == 0
    end = jnp.where(low, d.levels - 1, 0)
    end_block = jnp.where(low, coarse_levels - 1, 0)
    wz = (0.5 * STEP) * wind[2, end]
    lane = lax.broadcasted_iota(jnp.int32, (8, LANES), 1)
    last = jnp.where(lane == d.columns - 1, 1.0, 0.0)
    zeroth = jnp.where(lane == 0, 1.0, 0.0)
    halos = []
    for g in range(d.groups):
        halo = yq[0][:, g * LANES : (g + 1) * LANES]
        if d.y_sends == 2:
            halo = halo + yq[1][:, g * LANES : (g + 1) * LANES]
        halos.append(jnp.broadcast_to(jnp.sum(halo * mask, axis=0, keepdims=True), (8, LANES)))
    sums[...] = tail[...]
    lines = [[jnp.zeros((8, LANES), F32)] * coarse_levels for _ in range(FIELDS)]
    for z in range(d.levels):
        wy = (0.5 * STEP) * wind[1, z]
        for f in range(FIELDS):
            spread = STEP * diff[f]
            weight = (spread - wy) * last + (spread + wy) * zeroth
            moved = pltpu.roll(halos[f // d.per_group], LANES - 1 - lane_of(d, f, z), 1)
            lines[f][z // RATIO] = lines[f][z // RATIO] + weight * moved
    for f in range(FIELDS):
        face = jnp.sum(zface[f * d.tiles : (f + 1) * d.tiles, :] * mask, axis=0, keepdims=True)
        face = (STEP * diff[f] + jnp.where(low, -wz, wz)) * face
        for k in range(coarse_levels):
            line = lines[f][k][:1, :] + jnp.where(end_block == k, face, 0.0)
            at = f * coarse_levels + k
            sums[at : at + 1, :] = sums[at : at + 1, :] + line
    sent_sums[...] = sums[...]
    second = x_choices(d)[1]
    for f in range(d.late):
        sent_b[f * d.levels : (f + 1) * d.levels, :] = pad[
            pl.ds(base_row(d, f, 0) + FRONT + second, d.levels, stride=d.block), :
        ]
    sent_b[d.late * d.levels :, :] = sums[...]


def step_two_kernel(d, raw_in, zface, *refs):
    yq = refs[: d.y_sends]
    masks_in, wind, diff = refs[d.y_sends : d.y_sends + 3]
    raw, new_fields, coarse = refs[-3:]
    rows = d.levels * d.tiles
    low = lax.axis_index("gz") == 0
    end = jnp.where(low, d.levels - 1, 0)
    changed = []
    for f in range(FIELDS):
        wz = (0.5 * STEP) * wind[2, end]
        weight = STEP * diff[f] + jnp.where(low, -wz, wz)
        place = pl.ds(pl.multiple_of(f * rows + end * d.tiles, 8), d.tiles)
        changed.append((place, raw[place, :] + weight * zface[f * d.tiles : (f + 1) * d.tiles, :]))
    for place, cells in changed:
        raw[place, :] = cells
    lane = lax.broadcasted_iota(jnp.int32, (d.tiles, LANES), 1)
    last = jnp.where(lane == d.columns - 1, 1.0, 0.0)
    zeroth = jnp.where(lane == 0, 1.0, 0.0)
    zeros = jnp.zeros((d.tiles, LANES), F32)
    masks = [masks_in[p * d.tiles : (p + 1) * d.tiles, :] for p in range(d.parents)]
    coarse_levels = d.levels // RATIO
    coarse[...] = jnp.zeros_like(coarse)
    per_parent = coarse.shape[0] // d.parents

    def coarse_level(k, carry):
        def level(i, sums):
            z = k * RATIO + i
            wy = (0.5 * STEP) * wind[1, z]
            added = []
            for f in range(FIELDS):
                spread = STEP * diff[f]
                place = pl.ds(pl.multiple_of(f * rows + z * d.tiles, 8), d.tiles)
                weight = (spread - wy) * last + (spread + wy) * zeroth
                new = raw[place, :] + weight * y_halo(d, yq, f, z)
                new_fields[place, :] = new
                added.append(sums[f] + new)
            return tuple(added)

        sums = lax.fori_loop(0, RATIO, level, (zeros,) * FIELDS, unroll=8)
        for p in range(d.parents):
            for f in range(FIELDS):
                line = jnp.sum(sums[f] * masks[p], axis=0, keepdims=True)
                coarse[pl.ds(p * per_parent + f * coarse_levels + k, 1), :] = line
        return carry

    lax.fori_loop(0, coarse_levels, coarse_level, 0)


def flush_kernel(d, state, from_right, head, own_sums, parent_of, new_fields, sums, terms, sem):
    copy = pltpu.make_async_copy(state.at[pl.ds(0, new_fields.shape[0]), :], new_fields, sem.at[0])
    copy.start()
    coarse_levels = d.levels // RATIO
    terms[...] = jnp.zeros_like(terms)
    for f in range(FIELDS):
        cut = slice(f * d.levels, (f + 1) * d.levels)
        term = from_right[cut, :] * head[cut, :]
        terms[f * coarse_levels : (f + 1) * coarse_levels, :] = jnp.sum(
            term.reshape(coarse_levels, RATIO, LANES), axis=1
        )
    me = lax.axis_index("gx")
    before = jnp.maximum(me * d.tiles - 1, 0)
    counts = (me > 0) & (parent_of[before] == me * d.parents)
    per_parent = terms.shape[0]
    sums[:per_parent, :] = own_sums[:per_parent, :] + jnp.where(counts, terms[...], 0.0)
    sums[per_parent:, :] = own_sums[per_parent:, :]
    copy.wait()


def finish_kernel(d, from_left, from_right, flushed, state_in, coarse, *refs):
    got_a, got_b, parent_of, place_table, counts = refs[:5]
    stress, refs = refs[5 : 5 + d.n_gx], refs[5:]
    new_fields, state, wall_stress, parent_mean, terms, gathered, placed, mean_out, sems = refs[d.n_gx :]
    me = lax.axis_index("gx")
    even = lax.rem(me, 2) == 0
    rows = d.levels * d.tiles
    coarse_levels = d.levels // RATIO
    per_parent = coarse.shape[0] // d.parents
    copies = []
    part = d.part
    for k in range(d.n_gx):
        gathered[k * part : (k + 1) * part, :] = stress[k][:part, :]
    for s in range(SLOTS):
        start = pl.multiple_of(place_table[s] * d.levels, 8)
        placed[pl.ds(s, d.levels, stride=SLOTS), :] = gathered[pl.ds(start, d.levels), :]
    copies.append(pltpu.make_async_copy(placed.at[pl.ds(0, d.levels * SLOTS), :], wall_stress, sems.at[2 * FIELDS]))
    copies[-1].start()
    for f in range(FIELDS):
        cut = slice(f * d.levels, (f + 1) * d.levels)
        a = stress[1][d.part + f * d.levels : d.part + (f + 1) * d.levels, :]
        if f < d.late:
            b = got_b[cut, :]
        else:
            b = stress[3][d.part + (f - d.late) * d.levels : d.part + (f - d.late + 1) * d.levels, :]
        left, right = left_right(d, a, b)
        left, right = from_left[cut, :] * left, from_right[cut, :] * right
        for tile, added in ((0, left), (d.tiles - 1, right)):
            place = pl.ds(f * rows + tile, d.levels, stride=d.tiles)
            state[place, :] = state[place, :] + added
        for i, tile in enumerate((0, d.tiles - 1)):
            ends = [
                array.at[pl.ds(f * rows, rows), :].reshape(d.levels, d.tiles, LANES).at[:, pl.ds(tile, 1), :]
                for array in (state, new_fields)
            ]
            copies.append(pltpu.make_async_copy(*ends, sems.at[2 * f + i]))
            copies[-1].start()
        for i, term in enumerate((left, right)):
            terms[i * per_parent + f * coarse_levels : i * per_parent + (f + 1) * coarse_levels, :] = jnp.sum(
                term.reshape(coarse_levels, RATIO, LANES), axis=1
            )
    filled = FIELDS * coarse_levels
    if filled < per_parent:
        for i in range(2):
            terms[i * per_parent + filled : (i + 1) * per_parent, :] = jnp.zeros((per_parent - filled, LANES), F32)
    got = jnp.where(even, got_b[d.late * d.levels :, :], got_a[...])
    first_tile = me * d.tiles
    first_parent = parent_of[first_tile] - me * d.parents
    last_parent = parent_of[first_tile + d.tiles - 1] - me * d.parents
    pick_row = lax.broadcasted_iota(jnp.int32, (LANES, LANES), 0)
    pick_lane = lax.broadcasted_iota(jnp.int32, (LANES, LANES), 1)
    pick = jnp.where(pick_row // RATIO == pick_lane, 1.0, 0.0)
    totals = []
    for p in range(d.parents):
        total = coarse[p * per_parent : (p + 1) * per_parent, :]
        total = total + jnp.where(first_parent == p, terms[:per_parent, :], 0.0)
        total = total + jnp.where(last_parent == p, terms[per_parent : 2 * per_parent, :], 0.0)
        if p == 0:
            total = total + jnp.where(me == 0, 0.0, got)
        totals.append(total)
    summed = jnp.dot(
        jnp.concatenate(totals, axis=0), pick, precision=lax.Precision.HIGHEST, preferred_element_type=F32
    )
    for p in range(d.parents):
        total = summed[p * per_parent : (p + 1) * per_parent, :]
        mean = total / (jnp.full(total.shape, counts[p], jnp.int32).astype(F32) * (RATIO * RATIO))
        for f in range(FIELDS):
            mean_out[p, f] = mean[f * coarse_levels : (f + 1) * coarse_levels, : d.columns // RATIO]
    copies.append(pltpu.make_async_copy(mean_out, parent_mean, sems.at[2 * FIELDS + 1]))
    copies[-1].start()
    for copy in copies:
        copy.wait()


def swapped(block, axis):
    return lax.ppermute(block, axis, [(i, i ^ 1) for i in range(lax.axis_size(axis))])


def swapped_between(block, axis, inner):
    n = lax.axis_size(axis)
    route = []
    for i in range(n):
        for k in range(2):
            other = (i, 1 - k) if i in (0, n - 1) else (i + 1 if i % 2 else i - 1, k)
            route.append((2 * i + k, 2 * other[0] + other[1]))
    return lax.ppermute(block, (axis, inner), route)


def crossed(block, axis, distance):
    return lax.ppermute(block, axis, [(i, i ^ distance) for i in range(lax.axis_size(axis))])


def x_swapped(xa, xb):
    return [in_vmem(swapped(xa, "gx")), in_vmem(swapped_between(xb, "gx", "gz"))]


def zy_swapped(d, zface, yq):
    if d.y_sends == 1:
        yq = [swapped(yq[0], "gy")]
    else:
        n = d.n_gy
        yq = [
            lax.ppermute(yq[0], "gy", [(i, i + 1) for i in range(n - 1)]),
            lax.ppermute(yq[1], "gy", [(i + 1, i) for i in range(n - 1)]),
        ]
    return [in_vmem(a) for a in (swapped(zface, "gz"), *yq)]


def body(fields, parent_wind, diffusivity, wall_type, building_count, slot_of, parent_of):
    _, levels, tiles, columns = fields.shape
    d = Dims(levels, tiles, columns, slot_of.shape[0], lax.axis_size("gx"), lax.axis_size("gy"))
    assert columns == LANES and lax.axis_size("gz") == 2 and d.n_gx & (d.n_gx - 1) == 0
    params = pltpu.CompilerParams(vmem_limit_bytes=24 << 20)
    small = [in_hbm(a) for a in (wall_type, parent_wind, diffusivity, building_count, slot_of, parent_of)]
    rows = FIELDS * levels * tiles
    pad_t = pltpu.VMEM((d.pad_rows, LANES), F32)
    x_t = pltpu.VMEM((FIELDS * levels, LANES), F32)
    z_t = pltpu.VMEM((FIELDS * tiles, LANES), F32)
    y_ts = [pltpu.VMEM((tiles, d.groups * LANES), F32)] * d.y_sends

    n_small = len(small)
    *small, pad, xa, xb, zface = (packed := pl.pallas_call(
        functools.partial(pack_kernel, d),
        out_shape=[pltpu.SMEM(a.shape, a.dtype) if a.shape != wall_type.shape else pltpu.VMEM(a.shape, a.dtype) for a in small]
        + [pad_t, x_t, x_t, z_t, *y_ts],
        in_specs=[pl.BlockSpec(memory_space=pltpu.HBM)] * (1 + n_small),
        out_specs=[VM] + [SM] * (n_small - 1) + [VM] * (4 + d.y_sends),
        scratch_shapes=[pltpu.VMEM(fields.shape, F32), pltpu.SemaphoreType.DMA((FIELDS + n_small,))],
        compiler_params=params,
        name="pack",
    )(in_hbm(fields), *small))[: n_small + 4]
    yq = packed[n_small + 4 :]
    faces = x_swapped(xa, xb) + zy_swapped(d, zface, yq)
    hbm = pl.BlockSpec(memory_space=pltpu.HBM)

    def ints(n):
        return pltpu.SMEM((n,), jnp.int32)

    new_pad, wall_coef, from_left, from_right, masks, send_table, place_table, counts = pl.pallas_call(
        functools.partial(prepare_kernel, d),
        out_shape=[pad_t, pltpu.VMEM((tiles, LANES), F32), x_t, x_t]
        + [pltpu.VMEM(((d.parents + 1) * tiles, LANES), F32)]
        + [ints(d.n_gx * d.capacity), ints(SLOTS + 1), ints(d.parents)],
        in_specs=[VM] * 2 + [SM] * 5,
        out_specs=[VM] * 5 + [SM] * 3,
        scratch_shapes=[ints(d.n_gx)],
        compiler_params=params,
        name="prepare",
    )(in_vmem(pad), in_vmem(small[0]), *small[1:])

    _, new_pad, factor, zface, head, *rest = pl.pallas_call(
        functools.partial(step_one_kernel, d),
        out_shape=[pad_t, pad_t, pltpu.VMEM(((levels + 1) * tiles, LANES), F32), z_t, x_t, *y_ts]
        + [pltpu.VMEM((d.part + d.riders(k), LANES), F32) for k in range(d.n_gx)],
        in_specs=[VM] * (7 + d.y_sends) + [SM] * 3,
        out_specs=[VM] * (5 + d.y_sends + d.n_gx),
        input_output_aliases={0: 0},
        compiler_params=params,
        name="step_one",
    )(in_vmem(new_pad), *faces, *[in_vmem(a) for a in (wall_coef, from_left, from_right)], small[1], small[2], send_table)
    yq, stress = rest[: d.y_sends], rest[d.y_sends :]
    faces = zy_swapped(d, zface, yq)
    stress = [stress[0]] + [in_vmem(crossed(stress[k], "gx", k)) for k in range(1, d.n_gx)]

    per_parent = -(-FIELDS * (levels // RATIO) // 8) * 8
    state_t = pltpu.VMEM((rows + tiles, LANES), F32)
    new_pad, raw, tail = pl.pallas_call(
        functools.partial(local_two_kernel, d),
        out_shape=[pad_t, state_t, pltpu.VMEM((per_parent, LANES), F32)],
        in_specs=[VM] * 3 + [SM] * 2,
        out_specs=[VM] * 3,
        input_output_aliases={0: 0},
        compiler_params=params,
        name="local_two",
    )(in_vmem(new_pad), in_vmem(factor), in_vmem(masks), small[1], small[2])
    sent_sums, sent_b = pl.pallas_call(
        functools.partial(tail_kernel, d),
        out_shape=[
            pltpu.VMEM((per_parent, LANES), F32),
            pltpu.VMEM((d.late * levels + per_parent, LANES), F32),
        ],
        in_specs=[VM] * (4 + d.y_sends) + [SM] * 2,
        out_specs=[VM] * 2,
        scratch_shapes=[pltpu.VMEM((per_parent, LANES), F32)],
        compiler_params=params,
        name="tail",
    )(in_vmem(tail), in_vmem(new_pad), *faces, in_vmem(masks), small[1], small[2])
    _, state, own_sums = pl.pallas_call(
        functools.partial(step_two_kernel, d),
        out_shape=[state_t, state_t, pltpu.VMEM((d.parents * per_parent, LANES), F32)],
        in_specs=[VM] * (3 + d.y_sends) + [SM] * 2,
        out_specs=[VM] * 3,
        input_output_aliases={0: 0},
        compiler_params=params,
        name="step_two",
    )(in_vmem(raw), *faces, in_vmem(masks), small[1], small[2])
    got = x_swapped(sent_sums, sent_b)

    flushed, own_sums = pl.pallas_call(
        functools.partial(flush_kernel, d),
        out_shape=[jax.ShapeDtypeStruct((rows, LANES), F32), pltpu.VMEM((d.parents * per_parent, LANES), F32)],
        in_specs=[VM] * 4 + [SM],
        out_specs=[hbm, VM],
        scratch_shapes=[pltpu.VMEM((per_parent, LANES), F32), pltpu.SemaphoreType.DMA((1,))],
        compiler_params=params,
        name="flush",
    )(*[in_vmem(a) for a in (state, from_right, head, own_sums)], small[5])

    new_fields, _, wall_stress, parent_mean = pl.pallas_call(
        functools.partial(finish_kernel, d),
        out_shape=[
            jax.ShapeDtypeStruct((rows, LANES), F32),
            state_t,
            jax.ShapeDtypeStruct((levels * SLOTS, LANES), F32),
            jax.ShapeDtypeStruct((d.parents, FIELDS, levels // RATIO, columns // RATIO), F32),
        ],
        in_specs=[VM] * 2 + [hbm] + [VM] * 4 + [SM] * 3 + [VM] * d.n_gx,
        out_specs=[hbm, VM, hbm, hbm],
        scratch_shapes=[
            pltpu.VMEM((2 * per_parent, LANES), F32),
            pltpu.VMEM((d.n_gx * d.capacity * levels, LANES), F32),
            pltpu.VMEM(((levels + 1) * SLOTS, LANES), F32),
            pltpu.VMEM((d.parents, FIELDS, levels // RATIO, columns // RATIO), F32),
            pltpu.SemaphoreType.DMA((2 * FIELDS + 2,)),
        ],
        input_output_aliases={2: 0, 3: 1},
        compiler_params=params,
        name="finish",
    )(
        in_vmem(from_left),
        in_vmem(from_right),
        flushed,
        in_vmem(state),
        in_vmem(own_sums),
        *got,
        small[5],
        place_table,
        counts,
        *[in_vmem(stress[0])],
        *stress[1:],
    )
    return (
        new_fields.reshape(fields.shape),
        wall_stress.reshape(levels, SLOTS, columns),
        parent_mean,
    )


def solution(mesh):
    in_specs = (
        P(None, "gz", ("groups", "gx"), "gy"),
        P(None, ("groups", "gz")),
        P(),
        P(("groups", "gx"), "gy"),
        P(("groups", "gx")),
        P("groups"),
        P("groups"),
    )
    out_specs = (
        P(None, "gz", ("groups", "gx"), "gy"),
        P("gz", ("groups", "gx"), "gy"),
        P(("groups", "gx"), None, "gz", "gy"),
    )
    return jax.shard_map(body, mesh=mesh, in_specs=in_specs, out_specs=out_specs, check_vma=False)
```
